256 devices in a mesh: row: 32 (over z, y_hi, core), col: 8 (over x, y_lo).
Axes of the slice: x: 4, y: 4 (y_hi: 2, y_lo: 2; y = y_hi * 2 + y_lo), z: 8, core: 2. Of those that a mesh axis runs over, the one named last changes fastest.
Arguments:
- homolog_embedding: float32 [128, 256, 256], P(None, 'row'), may hold values from -6 to 6
- pair_features: float32 [256, 256, 128], P('row', 'col'), may hold values from -6 to 6
- first_operand_matrix: float32 [256, 32], replicated, may hold values from -0.375 to 0.375
- second_operand_matrix: float32 [256, 32], replicated, may hold values from -0.375 to 0.375
- outer_output_weight: float32 [1024, 128], replicated, may hold values from -2 to 2
- triangle_input_weight: float32 [128, 512], replicated, may hold values from -0.5 to 0.5
- output_gate_weight: float32 [128, 128], replicated, may hold values from -0.5 to 0.5
- triangle_output_weight: float32 [128, 128], replicated, may hold values from -0.5 to 0.5
Outputs:
- pair_out: float32 [256, 256, 128], P('row', 'col')
The draws below stay inside these ranges and needn't reach their ends.
All inputs are finite; a program needn't handle non-finite values.
Results may differ from the reference program's by a relative error of at most 0.000057.
Values sent between devices are 32-bit elements; how exact they have to be, the bound alone decides.
No kernel may reach another device: no remote copies, remote signals or barrier semaphores. Data moves between devices by JAX's collectives and lax.ppermute only.
A program may use at most 64 MiB of HBM per device.

```python
import jax
import jax.numpy as jnp
from jax import lax

HOMOLOG_COUNT = 128
ROSTER_DEPTH = 256
HALF_WIDTH = 32
CZ = 128
CH = 128
RES_ROW = 8
CHAIN_LENGTH = 256


def block_scale(own_key, dims, split, least, largest):
    gain = 1.0
    for axis_at, parts in split:
        draws = jax.random.uniform(jax.random.fold_in(jax.random.fold_in(own_key, 6), axis_at), (parts,), jnp.float32, least / len(split), largest / len(split))
        gain = gain * jnp.repeat(jnp.exp(draws), dims[axis_at] // parts).reshape((-1,) + (1,) * (len(dims) - 1 - axis_at))
    return gain


def bell_draw(own_key, shape, width, limit, pieces=(), kind=jnp.bfloat16):
    gain = block_scale(own_key, shape, pieces, -0.22, 0.18) if pieces else 1.0
    array = jax.random.normal(own_key, shape, jnp.float32) * width * gain
    return jnp.minimum(jnp.maximum(array, -limit), limit).astype(kind)


def setup_inputs(seed: int = 0) -> dict:
    seeds = jax.random.split(jax.random.key(seed), 9)
    homolog_embedding = bell_draw(seeds[0], (HOMOLOG_COUNT, CHAIN_LENGTH, ROSTER_DEPTH), 1.0, 6.0, ((1, 32),), jnp.float32)
    pair_features = bell_draw(seeds[1], (CHAIN_LENGTH, CHAIN_LENGTH, CZ), 1.0, 6.0, ((0, 32), (1, 8)), jnp.float32)
    first_operand_matrix = bell_draw(seeds[2], (ROSTER_DEPTH, HALF_WIDTH), ROSTER_DEPTH ** -0.5, 0.375, (), jnp.float32)
    second_operand_matrix = bell_draw(seeds[3], (ROSTER_DEPTH, HALF_WIDTH), ROSTER_DEPTH ** -0.5, 0.375, (), jnp.float32)
    outer_output_weight = bell_draw(seeds[4], (HALF_WIDTH * HALF_WIDTH, CZ), (HALF_WIDTH * HALF_WIDTH // HOMOLOG_COUNT) ** -0.5, 2.0, (), jnp.float32)
    triangle_input_weight = bell_draw(seeds[5], (CZ, 4 * CH), CZ ** -0.5, 0.5, (), jnp.float32)
    output_gate_weight = bell_draw(seeds[6], (CZ, CZ), CZ ** -0.5, 0.5, (), jnp.float32)
    triangle_output_weight = bell_draw(seeds[7], (CH, CZ), CH ** -0.5, 0.5, (), jnp.float32)
    return {"homolog_embedding": homolog_embedding, "pair_features": pair_features, "first_operand_matrix": first_operand_matrix, "second_operand_matrix": second_operand_matrix, "outer_output_weight": outer_output_weight, "triangle_input_weight": triangle_input_weight, "output_gate_weight": output_gate_weight, "triangle_output_weight": triangle_output_weight}


epsilon = 1e-05
top_precision = lax.Precision.HIGHEST

def apply_layer_norm(values):
    average = lax.optimization_barrier(jnp.mean(values, -1, keepdims=True))
    centred = values - average
    variance = lax.optimization_barrier(jnp.mean(centred * centred, -1, keepdims=True))
    return centred * lax.rsqrt(variance + epsilon)

def reference(homolog_embedding, pair_features, first_operand_matrix, second_operand_matrix, outer_output_weight, triangle_input_weight, output_gate_weight, triangle_output_weight):
    sequence_number = homolog_embedding.shape[0]
    residue_number = homolog_embedding.shape[1]
    row_block_list = RES_ROW
    normalized_input = apply_layer_norm(homolog_embedding)
    left_alignment_proj = jnp.einsum('bxp,pg->bxg', normalized_input, first_operand_matrix, precision=top_precision)
    right_alignment_proj = jnp.einsum('bxp,pg->bxg', normalized_input, second_operand_matrix, precision=top_precision)
    left_factor_blocks = left_alignment_proj.reshape(sequence_number, residue_number // row_block_list, row_block_list, left_alignment_proj.shape[2]).transpose(1, 0, 2, 3)

    def outer_block(left_factor_block):
        outer_product_total = jnp.einsum('emp,eqk->mqpk', left_factor_block, right_alignment_proj, precision=top_precision) / sequence_number
        flattened = outer_product_total.reshape(row_block_list, residue_number, -1)
        return jnp.einsum('ijf,fz->ijz', flattened, outer_output_weight, precision=top_precision)
    update = lax.map(outer_block, left_factor_blocks).reshape(residue_number, residue_number, -1)
    pair_mid = pair_features + update
    normed_pair = apply_layer_norm(pair_mid)
    hidden_width = triangle_output_weight.shape[0]
    projected = jnp.einsum('ijz,zh->ijh', normed_pair, triangle_input_weight, precision=top_precision)
    left_edge = jax.nn.sigmoid(projected[..., hidden_width:2 * hidden_width]) * projected[..., :hidden_width]
    right_edge = jax.nn.sigmoid(projected[..., 3 * hidden_width:]) * projected[..., 2 * hidden_width:3 * hidden_width]
    gate_act = jax.nn.sigmoid(jnp.einsum('ijz,zy->ijy', normed_pair, output_gate_weight, precision=top_precision))
    edge_blocks = left_edge.reshape(residue_number // row_block_list, row_block_list, residue_number, hidden_width)

    def triangle_block(edge_block):
        return jnp.einsum('ikc,jkc->ijc', edge_block, right_edge, precision=top_precision)
    mixed_edges = lax.map(triangle_block, edge_blocks).reshape(residue_number, residue_number, hidden_width)
    return pair_mid + gate_act * jnp.einsum('ijc,cz->ijz', apply_layer_norm(mixed_edges), triangle_output_weight, precision=top_precision)
```

```python
import jax
import jax.numpy as jnp
from jax import lax
from jax.sharding import Mesh, PartitionSpec as P

epsilon = 1e-05
top_precision = lax.Precision.HIGHEST

ALL = ("z", "yh", "core", "x", "yl")
ROW = ("z", "yh", "core")
COL = ("x", "yl")
LAYER = ("z", "x", "yl")
QUAD = ("yh", "core")


def apply_layer_norm(values):
    average = jnp.mean(values, -1, keepdims=True)
    centred = values - average
    variance = jnp.mean(centred * centred, -1, keepdims=True)
    return centred * lax.rsqrt(variance + epsilon)


def ring_distance(a, b, n):
    d = (a - b) % n
    return min(d, n - d)


def panel_permutation():
    pairs = []
    for c in range(8):
        targets = sorted(range(8), key=lambda z: -ring_distance(z, c, 8))
        sources = sorted(
            range(8), key=lambda k: ring_distance(k // 2, c // 2, 4) + abs(k % 2 - c % 2)
        )
        for z, k in zip(targets, sources):
            for o in range(4):
                pairs.append(((c * 4 + o) * 8 + k, (z * 4 + o) * 8 + c))
    return pairs


def per_device(homolog, pair, w_first, w_second, w_outer, w_tri, w_gate, w_out):
    normed = apply_layer_norm(homolog)
    right = jnp.einsum("sip,pg->sig", normed, w_second, precision=top_precision)
    moved = lax.ppermute(right, ALL, panel_permutation())
    left = jnp.einsum("sip,pg->sig", normed, w_first, precision=top_precision)
    panel = lax.all_gather(moved, QUAD, axis=1, tiled=True)
    outer = jnp.einsum("sia,sjb->ijab", left, panel, precision=top_precision) / 128.0
    pair_mid = pair.reshape(256, 128) + jnp.dot(
        outer.reshape(256, 1024), w_outer, precision=top_precision
    )
    normed_pair = apply_layer_norm(pair_mid)
    w4 = w_tri.reshape(128, 2, 2, 64, 2)
    w_p = w4[:, :, 0].transpose(2, 1, 3, 0).reshape(256, 128)
    w_g = w4[:, :, 1].transpose(2, 1, 3, 0).reshape(256, 128)
    p_t = jnp.einsum("hz,pz->hp", w_p, normed_pair, precision=top_precision)
    g_t = jnp.einsum("hz,pz->hp", w_g, normed_pair, precision=top_precision)
    edges = jax.nn.sigmoid(g_t) * p_t
    gate = jax.nn.sigmoid(jnp.dot(normed_pair, w_gate, precision=top_precision))
    swapped = lax.all_to_all(edges.reshape(64, 4, 256), LAYER, 0, 0, tiled=True)
    rights = lax.all_gather(swapped[:, 2:], QUAD, axis=0)
    left_e = swapped[:, :2].reshape(8, 8, 2, 8, 32).transpose(2, 0, 3, 1, 4).reshape(2, 64, 256)
    right_e = (
        rights.reshape(4, 8, 8, 2, 8, 32).transpose(3, 1, 0, 4, 2, 5).reshape(2, 256, 256)
    )
    mixed = jnp.einsum("cik,cjk->cij", left_e, right_e, precision=top_precision)
    back = mixed.reshape(2, 8, 8, 8, 32).transpose(1, 3, 0, 2, 4).reshape(64, 2, 256)
    mixed_t = lax.all_to_all(back, LAYER, 0, 0, tiled=True).reshape(128, 256)
    update = jnp.dot(apply_layer_norm(mixed_t.T), w_out, precision=top_precision)
    return (pair_mid + gate * update).reshape(8, 32, 128)


def solution(mesh):
    fine = Mesh(mesh.devices.reshape(8, 2, 2, 4, 2), ALL)
    placed = (P(None, ROW, None), P(ROW, COL, None), P(), P(), P(), P(), P(), P())
    return jax.shard_map(
        per_device, mesh=fine, in_specs=placed, out_specs=P(ROW, COL, None), check_vma=False
    )
```

```python
import jax
import jax.numpy as jnp
from jax import lax
from jax.experimental import pallas as pl
from jax.experimental.pallas import tpu as pltpu
from jax.sharding import Mesh, PartitionSpec as P

epsilon = 1e-05
top_precision = lax.Precision.HIGHEST

ALL = ("z", "yh", "core", "x", "yl")
ROW = ("z", "yh", "core")
COL = ("x", "yl")
LAYER = ("z", "x", "yl")
QUAD = ("yh", "core")
VMEM_LIMIT = 32 * 1024 * 1024


def ring_distance(a, b, n):
    d = (a - b) % n
    return min(d, n - d)


def panel_permutation():
    pairs = []
    for c in range(8):
        targets = sorted(range(8), key=lambda z: -ring_distance(z, c, 8))
        sources = sorted(
            range(8), key=lambda k: ring_distance(k // 2, c // 2, 4) + abs(k % 2 - c % 2)
        )
        for z, k in zip(targets, sources):
            for o in range(4):
                pairs.append(((c * 4 + o) * 8 + k, (z * 4 + o) * 8 + c))
    return pairs


def dot(a, b):
    return jnp.dot(a, b, precision=top_precision, preferred_element_type=jnp.float32)


def dot_t(a, b):
    return lax.dot_general(
        a, b, (((1,), (1,)), ((), ())), precision=top_precision, preferred_element_type=jnp.float32
    )


def layer_norm(values, axis):
    average = jnp.mean(values, axis, keepdims=True)
    centred = values - average
    variance = jnp.mean(centred * centred, axis, keepdims=True)
    return centred * lax.rsqrt(variance + epsilon)


def sigmoid(x):
    return 1.0 / (1.0 + jnp.exp(-x))


def factor_kernel(msa_ref, w_ref, left_ref, right_ref):
    w = w_ref[...]
    for i in range(8):
        normed = layer_norm(msa_ref[:, i, :], -1)
        both = dot_t(w, normed)
        left_ref[pl.ds(i * 32, 32), :] = both[:32] * (1.0 / 128.0)
        right_ref[pl.ds(i, 32, stride=8), :] = both[32:]


def pair_kernel(
    left_ref, panel_ref, pair_ref, w_outer_ref, w_tri_ref, w_gate_ref,
    edges_ref, mid_ref, gate_ref, outer_ref, flat_ref,
):
    outer_ref[...] = dot_t(panel_ref[...], left_ref[...])
    lane = lax.broadcasted_iota(jnp.int32, (8, 128), 1)
    low_half = lane < 64
    even = (lane // 32) % 2 == 0
    for o in range(4):
        for bh in range(8):
            for ih in range(2):
                v = [
                    outer_ref[pl.ds((o * 32 + bh * 4 + b) * 8, 8), pl.ds(ih * 128, 128)]
                    for b in range(4)
                ]
                for p in range(2):
                    a, c = v[p], v[p + 2]
                    v[p] = jnp.where(low_half, a, pltpu.roll(c, 64, 1))
                    v[p + 2] = jnp.where(low_half, pltpu.roll(a, 64, 1), c)
                for p in (0, 2):
                    a, c = v[p], v[p + 1]
                    v[p] = jnp.where(even, a, pltpu.roll(c, 32, 1))
                    v[p + 1] = jnp.where(even, pltpu.roll(a, 96, 1), c)
                for il in range(4):
                    i = ih * 4 + il
                    flat_ref[pl.ds((i * 4 + o) * 8, 8), pl.ds(bh * 128, 128)] = v[il]
    mid = pair_ref[...] + dot(flat_ref[...], w_outer_ref[...])
    mid_ref[...] = mid
    normed = layer_norm(mid, -1)
    projected = dot_t(w_tri_ref[...], normed)
    for side in range(2):
        plain, gating = projected[side * 256 :][:128], projected[side * 256 + 128 :][:128]
        edge = sigmoid(gating) * plain
        for h in range(2):
            edges_ref[:, pl.ds((side * 2 + h) * 256, 256)] = edge[h * 64 : h * 64 + 64]
    gate_ref[...] = sigmoid(dot(normed, w_gate_ref[...]))


def swap_blocks(x, sub, lane):
    a, b = x[:, :128], x[:, 128:]
    upper = sub >= 4
    a, b = jnp.where(upper, pltpu.roll(b, 4, 0), a), jnp.where(upper, b, pltpu.roll(a, 4, 0))
    out = []
    for v in (a, b):
        for bit, width in ((2, 64), (1, 32)):
            s = (sub // bit) % 2
            l = (lane // width) % 2
            from_below = pltpu.roll(pltpu.roll(v, 8 - bit, 0), width, 1)
            from_above = pltpu.roll(pltpu.roll(v, bit, 0), 128 - width, 1)
            v = jnp.where(s == l, v, jnp.where(s < l, from_below, from_above))
        out.append(v)
    return jnp.concatenate(out, 1)


def triangle_kernel(left_ref, right_ref, out_ref, l_ref, r_ref):
    sub = lax.broadcasted_iota(jnp.int32, (8, 128), 0)
    lane = lax.broadcasted_iota(jnp.int32, (8, 128), 1)
    for h in range(2):
        for z in range(8):
            x = left_ref[pl.ds(z * 8, 8), pl.ds(h * 256, 256)]
            l_ref[pl.ds(z * 8, 8), :] = swap_blocks(x, sub, lane)
            for o in range(4):
                y = right_ref[pl.ds(o * 64 + z * 8, 8), pl.ds(h * 256, 256)]
                r_ref[pl.ds(z * 32 + o * 8, 8), :] = swap_blocks(y, sub, lane)
        mixed = dot_t(l_ref[...], r_ref[...])
        for z in range(8):
            out_ref[pl.ds(z * 8, 8), pl.ds(h * 256, 256)] = swap_blocks(
                mixed[z * 8 : z * 8 + 8], sub, lane
            )


def output_kernel(mixed_ref, mid_ref, gate_ref, w_ref, out_ref):
    mixed = jnp.concatenate([mixed_ref[:, :256], mixed_ref[:, 256:]], 0)
    normed = layer_norm(mixed, 0)
    out_ref[...] = mid_ref[...] + gate_ref[...] * dot(normed.T, w_ref[...])


def call(kernel, out_shapes, scratch, *args):
    shapes = [jax.ShapeDtypeStruct(s, jnp.float32) for s in out_shapes]
    return pl.pallas_call(
        kernel,
        out_shape=shapes if len(shapes) > 1 else shapes[0],
        scratch_shapes=[pltpu.VMEM(s, jnp.float32) for s in scratch],
        compiler_params=pltpu.CompilerParams(vmem_limit_bytes=VMEM_LIMIT),
    )(*args)


def factors(homolog, w_both):
    return call(factor_kernel, [(256, 128), (256, 128)], [], homolog, w_both)


def pair_stage(left, panel, pair, w_outer, w_tri, w_gate):
    return call(
        pair_kernel,
        [(64, 1024), (256, 128), (256, 128)],
        [(1024, 256), (256, 1024)],
        left, panel, pair, w_outer, w_tri, w_gate,
    )


def triangle(left, right):
    return call(triangle_kernel, [(64, 512)], [(64, 256), (256, 256)], left, right)


def output_stage(mixed, mid, gate, w_out):
    return call(output_kernel, [(256, 128)], [], mixed, mid, gate, w_out)


def per_device(homolog, pair, w_first, w_second, w_outer, w_tri, w_gate, w_out):
    w_both = jnp.concatenate([w_first, w_second], 1).T
    left, right = factors(homolog, w_both)
    moved = lax.ppermute(right, ALL, panel_permutation())
    w_outer_ba = w_outer.reshape(32, 32, 128).transpose(1, 0, 2).reshape(1024, 128)
    panel = lax.all_gather(moved, QUAD, axis=0, tiled=True)
    edges, mid, gate = pair_stage(
        left, panel, pair.reshape(256, 128), w_outer_ba, w_tri.T, w_gate
    )
    swapped = lax.all_to_all(edges, LAYER, 0, 0, tiled=True)
    rights = lax.all_gather(swapped[:, 512:], QUAD, axis=0, tiled=True)
    back = triangle(swapped, rights)
    mixed = lax.all_to_all(back, LAYER, 0, 0, tiled=True)
    return output_stage(mixed, mid, gate, w_out).reshape(8, 32, 128)


def solution(mesh):
    fine = Mesh(mesh.devices.reshape(8, 2, 2, 4, 2), ALL)
    placed = (P(None, ROW, None), P(ROW, COL, None), P(), P(), P(), P(), P(), P())
    return jax.shard_map(
        per_device, mesh=fine, in_specs=placed, out_specs=P(ROW, COL, None), check_vma=False
    )
```

```python
import jax
import jax.numpy as jnp
from jax import lax
from jax.experimental import pallas as pl
from jax.experimental.pallas import tpu as pltpu
from jax.sharding import Mesh, PartitionSpec as P

epsilon = 1e-05

ALL = ("z", "yh", "core", "x", "yl")
ROW = ("z", "yh", "core")
COL = ("x", "yl")
LAYER = ("z", "x", "yl")
QUAD = ("yh", "core")
VMEM_LIMIT = 32 * 1024 * 1024


def panel_permutation(cross):
    pairs = []
    for z in range(8):
        for yh in range(2):
            for core in range(2):
                for c in range(8):
                    source = ((c * 2 + (yh ^ cross)) * 2 + core) * 8 + (z + c) % 8
                    pairs.append((source, ((z * 2 + yh) * 2 + core) * 8 + c))
    return pairs


def mm(a, b):
    return jnp.dot(a, b, preferred_element_type=jnp.float32)


def mm_t(a, b):
    return lax.dot_general(a, b, (((1,), (1,)), ((), ())), preferred_element_type=jnp.float32)


def split(x):
    high = x.astype(jnp.bfloat16)
    return high, (x - high.astype(jnp.float32)).astype(jnp.bfloat16)


def dot_deep(a, b):
    a_high, a_low = split(a)
    b_high, b_low = split(b)
    both = mm(a_high, jnp.concatenate([b_high, b_low], 1))
    return both[:, :128] + both[:, 128:] + mm(a_low, b_high)


def dot_t(a, b):
    a_high, a_low = split(a)
    b_high, b_low = split(b)
    shared = mm_t(jnp.concatenate([a_high, a_low], 1), jnp.concatenate([b_high, b_high], 1))
    return shared + mm_t(a_high, b_low)


def dot_t_wide(a, b):
    a_high, a_low = split(a)
    b_high, b_low = split(b)
    return mm_t(a_high, b_high) + mm_t(a_low, b_high) + mm_t(a_high, b_low)


def layer_norm(values, axis):
    average = jnp.mean(values, axis, keepdims=True)
    centred = values - average
    variance = jnp.mean(centred * centred, axis, keepdims=True)
    return centred * lax.rsqrt(variance + epsilon)


def sigmoid(x):
    return 1.0 / (1.0 + jnp.exp(-x))


def factor_kernel(msa_ref, first_ref, second_ref, left_ref, right_ref, held, sems, result):
    copies = [
        pltpu.make_async_copy(
            msa_ref.at[pl.ds(k * 32, 32)], held.at[pl.ds(k * 32, 32)], sems.at[k]
        )
        for k in range(4)
    ]
    for copy in copies:
        copy.start()
    w_high, w_low = split(jnp.concatenate([first_ref[...], second_ref[...]], 1))
    w_both = jnp.concatenate([w_high, w_low], 1)
    w_rest = jnp.concatenate([w_high, jnp.zeros_like(w_high)], 1)
    for k in range(4):
        copies[k].wait()
        n_high, n_low = split(layer_norm(held[pl.ds(k * 32, 32)].reshape(256, 256), -1))
        result[pl.ds(k * 256, 256), :] = mm(n_high, w_both) + mm(n_low, w_rest)
    for i in range(8):
        turned = result[pl.ds(i, 128, stride=8), :].T
        both = turned[:64] + turned[64:]
        left_ref[pl.ds(i * 32, 32), :] = both[:32] * (1.0 / 128.0)
        right_ref[pl.ds(i, 32, stride=8), :] = both[32:]


def pair_half(left, panel, pair, w_outer, w_tri, w_gate, outer_ref, flat_ref):
    outer_ref[...] = dot_t(panel, left)
    lane = lax.broadcasted_iota(jnp.int32, (8, 128), 1)
    low_half = lane < 64
    even = (lane // 32) % 2 == 0
    for o in range(2):
        for bh in range(8):
            for ih in range(2):
                v = [
                    outer_ref[pl.ds((o * 32 + bh * 4 + b) * 8, 8), pl.ds(ih * 128, 128)]
                    for b in range(4)
                ]
                for p in range(2):
                    a, c = v[p], v[p + 2]
                    v[p] = jnp.where(low_half, a, pltpu.roll(c, 64, 1))
                    v[p + 2] = jnp.where(low_half, pltpu.roll(a, 64, 1), c)
                for p in (0, 2):
                    a, c = v[p], v[p + 1]
                    v[p] = jnp.where(even, a, pltpu.roll(c, 32, 1))
                    v[p + 1] = jnp.where(even, pltpu.roll(a, 96, 1), c)
                for il in range(4):
                    i = ih * 4 + il
                    flat_ref[pl.ds(((8 - i) % 8 * 2 + o) * 8, 8), pl.ds(bh * 128, 128)] = v[il]
    mid = pair + dot_deep(flat_ref[...], w_outer)
    normed = layer_norm(mid, -1)
    projected = dot_t(w_tri, normed)
    edges = []
    for side in range(2):
        plain, gating = projected[side * 256 :][:128], projected[side * 256 + 128 :][:128]
        edge = sigmoid(gating) * plain
        edges += [edge[:64], edge[64:]]
    return mid, sigmoid(dot_deep(normed, w_gate)), edges


def half_pairs(pair_ref, half):
    return jnp.concatenate([pair_ref[(8 - p) % 8, half] for p in range(8)], 0)


def near_kernel(
    left_ref, panel_ref, pair_ref, w_outer_ref, w_tri_ref, w_gate_ref,
    edges_ref, mid_ref, gate_ref, outer_ref, flat_ref,
):
    yh = lax.axis_index("yh")
    pair = half_pairs(pair_ref, yh)
    mid, gate, edges = pair_half(
        left_ref[...], panel_ref[...], pair, w_outer_ref[...], w_tri_ref[...], w_gate_ref[...],
        outer_ref, flat_ref,
    )
    mid_ref[...] = mid
    gate_ref[...] = gate
    for q in range(4):
        edges_ref[pl.ds(q * 64, 64), :] = edges[q]


def far_kernel(
    left_ref, panel_ref, pair_ref, w_outer_ref, w_tri_ref, w_gate_ref,
    near_edges_ref, near_mid_ref, near_gate_ref,
    edges_ref, mid_ref, gate_ref, outer_ref, flat_ref,
):
    yh = lax.axis_index("yh")
    pair = half_pairs(pair_ref, 1 - yh)
    mid, gate, edges = pair_half(
        left_ref[...], panel_ref[...], pair, w_outer_ref[...], w_tri_ref[...], w_gate_ref[...],
        outer_ref, flat_ref,
    )
    mid_ref[yh] = near_mid_ref[...]
    mid_ref[1 - yh] = mid
    gate_ref[yh] = near_gate_ref[...]
    gate_ref[1 - yh] = gate
    for q in range(4):
        near = near_edges_ref[pl.ds(q * 64, 64), :]
        edges_ref[pl.ds(q * 2, 64, stride=8), :] = jnp.where(yh == 0, near, edges[q])
        edges_ref[pl.ds(q * 2 + 1, 64, stride=8), :] = jnp.where(yh == 0, edges[q], near)


def turn_blocks(x, masks):
    x = pltpu.roll(x, 0, 1, stride=16, stride_axis=0)
    for bit, mask in zip((1, 2, 4), masks):
        x = jnp.where(mask, pltpu.roll(x, 8 - bit, 0), x)
    return pltpu.roll(x, 0, 1, stride=16, stride_axis=0)


def triangle_kernel(left_ref, right_ref, out_ref, l_ref, r_ref):
    lane = lax.broadcasted_iota(jnp.int32, (8, 128), 1)
    masks = [(lane // 16) & bit != 0 for bit in (1, 2, 4)]
    for h in range(2):
        for z in range(8):
            for half in range(2):
                lanes = pl.ds(half * 128, 128)
                x = left_ref[pl.ds(z * 64 + h * 2 + half, 8, stride=8), :]
                l_ref[pl.ds(z * 8, 8), lanes] = turn_blocks(x, masks)
                for o in range(4):
                    y = right_ref[pl.ds(o * 256 + z * 32 + h * 2 + half, 8, stride=4), :]
                    row = (o // 2) * 128 + (8 - z) % 8 * 16 + (o % 2) * 8
                    r_ref[pl.ds(row, 8), lanes] = turn_blocks(y, masks)
        mixed = dot_t_wide(l_ref[...], r_ref[...])
        for z in range(8):
            for half in range(2):
                block = mixed[z * 8 : z * 8 + 8, half * 128 : half * 128 + 128]
                out_ref[pl.ds(z * 32 + h * 2 + half, 8, stride=4), :] = turn_blocks(block, masks)


def output_kernel(mixed_ref, mid_ref, gate_ref, w_ref, out_ref):
    w = w_ref[...]
    for half in range(2):
        mixed = jnp.concatenate(
            [mixed_ref[pl.ds(h * 2 + half, 64, stride=4), :] for h in range(2)], 0
        )
        update = dot_deep(layer_norm(mixed, 0).T, w)
        for i in range(8):
            rows = pl.ds((8 - i) % 8 * 16, 16)
            out_ref[i, half] = (
                mid_ref[half, rows, :] + gate_ref[half, rows, :] * update[i * 16 : i * 16 + 16]
            )


def call(kernel, out_shapes, scratch, *args, specs=None, flops=0):
    shapes = [jax.ShapeDtypeStruct(s, jnp.float32) for s in out_shapes]
    extra = {} if specs is None else {"in_specs": specs}
    return pl.pallas_call(
        kernel,
        out_shape=shapes if len(shapes) > 1 else shapes[0],
        scratch_shapes=scratch,
        compiler_params=pltpu.CompilerParams(vmem_limit_bytes=VMEM_LIMIT),
        cost_estimate=pl.CostEstimate(flops=flops, bytes_accessed=2**20, transcendentals=0),
        **extra,
    )(*args)


def vmem(*shape):
    return pltpu.VMEM(shape, jnp.float32)


def factors(homolog, first, second):
    inside = pl.BlockSpec(memory_space=pltpu.VMEM)
    return call(
        factor_kernel,
        [(256, 128), (256, 128)],
        [vmem(128, 8, 256), pltpu.SemaphoreType.DMA((4,)), vmem(1024, 128)],
        homolog, first, second,
        specs=[pl.BlockSpec(memory_space=pl.ANY), inside, inside],
    )


def pair_stage_near(left, panel, pair, w_outer, w_tri, w_gate):
    return call(
        near_kernel,
        [(256, 128), (128, 128), (128, 128)],
        [vmem(512, 256), vmem(128, 1024)],
        left, panel, pair, w_outer, w_tri, w_gate,
        flops=10**9,
    )


def pair_stage_far(left, panel, pair, w_outer, w_tri, w_gate, edges, mid, gate):
    return call(
        far_kernel,
        [(512, 128), (2, 128, 128), (2, 128, 128)],
        [vmem(512, 256), vmem(128, 1024)],
        left, panel, pair, w_outer, w_tri, w_gate, edges, mid, gate,
        flops=10**9,
    )


def triangle(left, right):
    return call(triangle_kernel, [(256, 128)], [vmem(64, 256), vmem(256, 256)], left, right)


def output_stage(mixed, mid, gate, w_out):
    return call(output_kernel, [(8, 2, 16, 128)], [], mixed, mid, gate, w_out)


def per_device(homolog, pair, w_first, w_second, w_outer, w_tri, w_gate, w_out):
    left, right = factors(homolog, w_first, w_second)
    near = lax.ppermute(right, ALL, panel_permutation(0))
    far = lax.ppermute(right, ALL, panel_permutation(1))
    w_outer_ba = w_outer.reshape(32, 32, 128).transpose(1, 0, 2).reshape(1024, 128)
    pair = pair.reshape(8, 2, 16, 128)
    shared = (pair, w_outer_ba, w_tri.T, w_gate)
    near = lax.all_gather(near, "core", axis=0, tiled=True)
    done = pair_stage_near(left, near, *shared)
    far = lax.all_gather(far, "core", axis=0, tiled=True)
    edges, mid, gate = pair_stage_far(left, far, *shared, *done)
    swapped = lax.all_to_all(edges.reshape(64, 8, 128), LAYER, 0, 0, tiled=True)
    rights = lax.all_gather(swapped[:, 4:], QUAD, axis=0, tiled=True)
    back = triangle(swapped.reshape(512, 128), rights.reshape(1024, 128))
    mixed = lax.all_to_all(back.reshape(64, 4, 128), LAYER, 0, 0, tiled=True)
    return output_stage(mixed.reshape(256, 128), mid, gate, w_out).reshape(8, 32, 128)


def solution(mesh):
    fine = Mesh(mesh.devices.reshape(8, 2, 2, 4, 2), ALL)
    placed = (P(None, ROW, None), P(ROW, COL, None), P(), P(), P(), P(), P(), P())
    return jax.shard_map(
        per_device, mesh=fine, in_specs=placed, out_specs=P(ROW, COL, None), check_vma=False
    )
```

```python
import jax
import jax.numpy as jnp
from jax import lax
from jax.experimental import pallas as pl
from jax.experimental.pallas import tpu as pltpu
from jax.sharding import Mesh, PartitionSpec as P

epsilon = 1e-05

ALL = ("z", "yh", "core", "x", "yl")
ROW = ("z", "yh", "core")
COL = ("x", "yl")
LAYER = ("z", "x", "yl")
CHIPS = ("z", "yh", "x", "yl")
VMEM_LIMIT = 32 * 1024 * 1024


def panel_permutation():
    pairs = []
    for z in range(8):
        for o in range(4):
            for c in range(8):
                pairs.append(((c * 4 + o) * 8 + (z + c + 4) % 8, (z * 4 + o) * 8 + c))
    return pairs


def mm(a, b):
    return jnp.dot(a, b, preferred_element_type=jnp.float32)


def mm_t(a, b):
    return lax.dot_general(a, b, (((1,), (1,)), ((), ())), preferred_element_type=jnp.float32)


def split(x):
    high = x.astype(jnp.bfloat16)
    return high, (x - high.astype(jnp.float32)).astype(jnp.bfloat16)


def dot_deep(a, b):
    a_high, a_low = split(a)
    b_high, b_low = split(b)
    both = mm(a_high, jnp.concatenate([b_high, b_low], 1))
    return both[:, :128] + both[:, 128:] + mm(a_low, b_high)


def dot_t(a, b):
    a_high, a_low = split(a)
    b_high, b_low = split(b)
    shared = mm_t(jnp.concatenate([a_high, a_low], 1), jnp.concatenate([b_high, b_high], 1))
    return shared + mm_t(a_high, b_low)


def layer_norm(values, axis):
    average = jnp.mean(values, axis, keepdims=True)
    centred = values - average
    variance = jnp.mean(centred * centred, axis, keepdims=True)
    return centred * lax.rsqrt(variance + epsilon)


def sigmoid(x):
    return 1.0 / (1.0 + jnp.exp(-x))


def turned_rows(p):
    return (8 - p) % 8


def factor_kernel(msa_ref, first_ref, second_ref, pair_ref, shared_ref, right_ref, held, sems, result):
    copies = [
        pltpu.make_async_copy(
            msa_ref.at[pl.ds(k * 32, 32)], held.at[pl.ds(k * 32, 32)], sems.at[k]
        )
        for k in range(4)
    ]
    for copy in copies:
        copy.start()
    w_high, w_low = split(jnp.concatenate([first_ref[...], second_ref[...]], 0))
    w_both = jnp.concatenate([w_high, w_low], 0)
    w_rest = jnp.concatenate([w_high, jnp.zeros_like(w_high)], 0)
    other = 1 - lax.axis_index("yh")
    for p in range(8):
        shared_ref[pl.ds(256 + p * 16, 16), :] = pair_ref[turned_rows(p), other]
    for k in range(4):
        copies[k].wait()
        n_high, n_low = split(layer_norm(held[pl.ds(k * 32, 32)].reshape(256, 256), -1))
        result[pl.ds(k * 256, 256), :] = mm_t(n_high, w_both) + mm_t(n_low, w_rest)
    for i in range(8):
        turned = result[pl.ds(i, 128, stride=8), :].T
        both = turned[:64] + turned[64:]
        shared_ref[pl.ds(i * 32, 32), :] = both[:32] * (1.0 / 128.0)
        right_ref[pl.ds(i, 32, stride=8), :] = both[32:]


def pair_kernel(
    own_ref, met_ref, panel_ref, pair_ref, w_outer_ref, w_tri_ref, w_gate_ref,
    edges_ref, kept_ref, sent_ref, outer_ref, flat_ref,
):
    yh = lax.axis_index("yh")
    left = jnp.concatenate([own_ref[pl.ds(0, 256), :], met_ref[pl.ds(0, 256), :]], 0)
    outer_ref[...] = dot_t(panel_ref[...], left)
    lane = lax.broadcasted_iota(jnp.int32, (8, 128), 1)
    low_half = lane < 64
    even = (lane // 32) % 2 == 0
    for o in range(2):
        for bh in range(8):
            for ih in range(4):
                v = [
                    outer_ref[pl.ds((o * 32 + bh * 4 + b) * 8, 8), pl.ds(ih * 128, 128)]
                    for b in range(4)
                ]
                for p in range(2):
                    a, c = v[p], v[p + 2]
                    v[p] = jnp.where(low_half, a, pltpu.roll(c, 64, 1))
                    v[p + 2] = jnp.where(low_half, pltpu.roll(a, 64, 1), c)
                for p in (0, 2):
                    a, c = v[p], v[p + 1]
                    v[p] = jnp.where(even, a, pltpu.roll(c, 32, 1))
                    v[p + 1] = jnp.where(even, pltpu.roll(a, 96, 1), c)
                for il in range(4):
                    i = ih % 2 * 4 + il
                    row = ih // 2 * 128 + turned_rows(i) * 16 + o * 8
                    flat_ref[pl.ds(row, 8), pl.ds(bh * 128, 128)] = v[il]
    pair = jnp.concatenate(
        [pair_ref[turned_rows(p), yh] for p in range(8)] + [met_ref[pl.ds(256, 128), :]], 0
    )
    mid = pair + dot_deep(flat_ref[...], w_outer_ref[...])
    normed = layer_norm(mid, -1)
    projected = dot_t(w_tri_ref[...], normed)
    for side in range(2):
        plain, gating = projected[side * 256 :][:128], projected[side * 256 + 128 :][:128]
        edge = sigmoid(gating) * plain
        for h in range(2):
            q = side * 2 + h
            own, met = edge[h * 64 : h * 64 + 64, :128], edge[h * 64 : h * 64 + 64, 128:]
            edges_ref[pl.ds(q * 2, 64, stride=8), :] = jnp.where(yh == 0, own, met)
            edges_ref[pl.ds(q * 2 + 1, 64, stride=8), :] = jnp.where(yh == 0, met, own)
    gate = sigmoid(dot_deep(normed, w_gate_ref[...]))
    kept_ref[0], kept_ref[1] = mid[:128], gate[:128]
    sent_ref[0], sent_ref[1] = mid[128:], gate[128:]


def turn_blocks(x, masks):
    x = pltpu.roll(x, 0, 1, stride=16, stride_axis=0)
    for bit, mask in zip((1, 2, 4), masks):
        x = jnp.where(mask, pltpu.roll(x, 8 - bit, 0), x)
    return pltpu.roll(x, 0, 1, stride=16, stride_axis=0)


def triangle_kernel(left_ref, right_ref, out_ref, l_ref, r_ref):
    lane = lax.broadcasted_iota(jnp.int32, (8, 128), 1)
    masks = [(lane // 16) & bit != 0 for bit in (1, 2, 4)]
    for h in range(2):
        for z in range(8):
            for y in range(2):
                x = left_ref[pl.ds(z * 64 + h * 2 + y, 8, stride=8), :]
                l_ref[pl.ds(y * 64 + z * 8, 8), :] = turn_blocks(x, masks)
                for o in range(2):
                    x = right_ref[pl.ds(o * 256 + z * 32 + h * 2 + y, 8, stride=4), :]
                    row = y * 128 + turned_rows(z) * 16 + o * 8
                    r_ref[pl.ds(row, 8), :] = turn_blocks(x, masks)
        mixed = dot_t(l_ref[...], r_ref[...])
        for z in range(8):
            for y in range(2):
                for half in range(2):
                    block = mixed[y * 64 + z * 8 :, half * 128 :][:8, :128]
                    out_ref[pl.ds((z * 2 + y) * 32 + h * 2 + half, 8, stride=4), :] = turn_blocks(
                        block, masks
                    )


def output_kernel(mixed_ref, kept_ref, met_ref, w_ref, out_ref):
    yh = lax.axis_index("yh")
    w = w_ref[...]
    for half in range(2):
        tiles = []
        for h in range(2):
            for z in range(8):
                parts = [
                    mixed_ref[pl.ds((z * 2 + y) * 32 + h * 2 + half, 8, stride=4), :]
                    for y in range(2)
                ]
                tiles.append(parts[0] + parts[1])
        update = dot_deep(layer_norm(jnp.concatenate(tiles, 0), 0).T, w)
        mid = jnp.where(yh == half, kept_ref[0], met_ref[0])
        gate = jnp.where(yh == half, kept_ref[1], met_ref[1])
        for i in range(8):
            p = turned_rows(i) * 16
            out_ref[i, half] = mid[p : p + 16] + gate[p : p + 16] * update[i * 16 : i * 16 + 16]


def call(kernel, out_shapes, scratch, *args, specs=None, limit=VMEM_LIMIT):
    shapes = [jax.ShapeDtypeStruct(s, jnp.float32) for s in out_shapes]
    extra = {} if specs is None else {"in_specs": specs}
    return pl.pallas_call(
        kernel,
        out_shape=shapes if len(shapes) > 1 else shapes[0],
        scratch_shapes=scratch,
        compiler_params=pltpu.CompilerParams(vmem_limit_bytes=limit),
        **extra,
    )(*args)


def vmem(*shape):
    return pltpu.VMEM(shape, jnp.float32)


def factors(homolog, first, second, pair):
    inside = pl.BlockSpec(memory_space=pltpu.VMEM)
    return call(
        factor_kernel,
        [(384, 128), (256, 128)],
        [vmem(128, 8, 256), pltpu.SemaphoreType.DMA((4,)), vmem(1024, 128)],
        homolog, first, second, pair,
        specs=[pl.BlockSpec(memory_space=pltpu.HBM), inside, inside, inside],
        limit=60 * 1024 * 1024,
    )


def pair_stage(own, met, panel, pair, w_outer, w_tri, w_gate):
    return call(
        pair_kernel,
        [(512, 128), (2, 128, 128), (2, 128, 128)],
        [vmem(512, 512), vmem(256, 1024)],
        own, met, panel, pair, w_outer, w_tri, w_gate,
    )


def triangle(left, right):
    return call(triangle_kernel, [(512, 128)], [vmem(128, 128), vmem(256, 128)], left, right)


def output_stage(mixed, kept, met, w_out):
    return call(output_kernel, [(8, 2, 16, 128)], [], mixed, kept, met, w_out)


def per_device(homolog, pair, w_first, w_second, w_outer, w_tri, w_gate, w_out):
    pair = pair.reshape(8, 2, 16, 128)
    shared, right = factors(homolog, w_first.T, w_second.T, pair)
    swap = [(0, 1), (1, 0)]
    panel = lax.ppermute(right, ALL, panel_permutation())
    met = lax.ppermute(shared, "yh", swap)
    w_outer_ba = w_outer.reshape(32, 32, 128).transpose(1, 0, 2).reshape(1024, 128)
    panel = lax.all_gather(panel, "core", axis=0, tiled=True)
    edges, kept, sent = pair_stage(shared, met, panel, pair, w_outer_ba, w_tri.T, w_gate)
    returned = lax.ppermute(sent, "yh", swap)
    swapped = lax.all_to_all(edges.reshape(64, 8, 128), LAYER, 0, 0, tiled=True)
    rights = lax.all_gather(swapped[:, 4:], "core", axis=0, tiled=True)
    back = triangle(swapped.reshape(512, 128), rights.reshape(512, 128))
    mixed = lax.all_to_all(back.reshape(128, 4, 128), CHIPS, 0, 0, tiled=True)
    return output_stage(mixed.reshape(512, 128), kept, returned, w_out).reshape(8, 32, 128)


def solution(mesh):
    fine = Mesh(mesh.devices.reshape(8, 2, 2, 4, 2), ALL)
    placed = (P(None, ROW, None), P(ROW, COL, None), P(), P(), P(), P(), P(), P())
    return jax.shard_map(
        per_device, mesh=fine, in_specs=placed, out_specs=P(ROW, COL, None), check_vma=False
    )
```

```python
import jax
import jax.numpy as jnp
from jax import lax
from jax.experimental import pallas as pl
from jax.experimental.pallas import tpu as pltpu
from jax.sharding import Mesh, PartitionSpec as P

epsilon = 1e-05

ALL = ("z", "yh", "core", "x", "yl")
ROW = ("z", "yh", "core")
COL = ("x", "yl")
LAYER = ("z", "x", "yl")
CHIPS = ("z", "yh", "x", "yl")
VMEM_LIMIT = 32 * 1024 * 1024


PANEL_COLUMNS = (
    (34570126, 24563107, 1675324, 1674523, 1236754, 1234675, 12467530, 1376452),
    (34560127, 45673102, 1675423, 1674253, 1237654, 2643175, 12467530, 1376542),
)


def panel_permutation():
    pairs = []
    for z in range(8):
        for yh in range(2):
            for core in range(2):
                for c in range(8):
                    column = PANEL_COLUMNS[yh][c] // 10 ** (7 - z) % 10
                    source = ((c * 2 + yh) * 2 + core) * 8 + column
                    pairs.append((source, ((z * 2 + yh) * 2 + core) * 8 + c))
    return pairs


def mm(a, b):
    return jnp.dot(a, b, preferred_element_type=jnp.float32)


def mm_t(a, b):
    return lax.dot_general(a, b, (((1,), (1,)), ((), ())), preferred_element_type=jnp.float32)


def split(x):
    high = x.astype(jnp.bfloat16)
    return high, (x - high.astype(jnp.float32)).astype(jnp.bfloat16)


def dot_deep(a, b):
    a_high, a_low = split(a)
    b_high, b_low = split(b)
    both = mm(a_high, jnp.concatenate([b_high, b_low], 1))
    return both[:, :128] + both[:, 128:] + mm(a_low, b_high)


def dot_t(a, b):
    a_high, a_low = split(a)
    b_high, b_low = split(b)
    shared = mm_t(jnp.concatenate([a_high, a_low], 1), jnp.concatenate([b_high, b_high], 1))
    return shared + mm_t(a_high, b_low)


def layer_norm(values, axis):
    average = jnp.mean(values, axis, keepdims=True)
    centred = values - average
    variance = jnp.mean(centred * centred, axis, keepdims=True)
    return centred * lax.rsqrt(variance + epsilon)


def sigmoid(x):
    return 1.0 / (1.0 + jnp.exp(-x))


def turned_rows(p):
    return (8 - p) % 8


def factor_kernel(msa_ref, first_ref, second_ref, pair_ref, shared_ref, right_ref, result):
    w_high, w_low = split(jnp.concatenate([first_ref[...], second_ref[...]], 0))
    w_both = jnp.concatenate([w_high, w_low], 0)
    w_rest = jnp.concatenate([w_high, jnp.zeros_like(w_high)], 0)
    other = 1 - lax.axis_index("yh")
    for p in range(8):
        shared_ref[pl.ds(256 + p * 16, 16), :] = pair_ref[turned_rows(p), other]
    for k in range(4):
        n_high, n_low = split(layer_norm(msa_ref[pl.ds(k * 32, 32)].reshape(256, 256), -1))
        result[pl.ds(k * 256, 256), :] = mm_t(n_high, w_both) + mm_t(n_low, w_rest)
    for i in range(8):
        turned = result[pl.ds(i, 128, stride=8), :].T
        both = turned[:64] + turned[64:]
        shared_ref[pl.ds(i * 32, 32), :] = both[:32] * (1.0 / 128.0)
        right_ref[pl.ds(i, 32, stride=8), :] = both[32:]


def pair_kernel(
    own_ref, met_ref, panel_ref, pair_ref, w_outer_ref, w_tri_ref, w_gate_ref,
    edges_ref, kept_ref, sent_ref, outer_ref, flat_ref,
):
    yh = lax.axis_index("yh")
    left = jnp.concatenate([own_ref[pl.ds(0, 256), :], met_ref[pl.ds(0, 256), :]], 0)
    outer_ref[...] = dot_t(panel_ref[...], left)
    lane = lax.broadcasted_iota(jnp.int32, (8, 128), 1)
    low_half = lane < 64
    even = (lane // 32) % 2 == 0
    for o in range(2):
        for bh in range(8):
            for ih in range(4):
                v = [
                    outer_ref[pl.ds((o * 32 + bh * 4 + b) * 8, 8), pl.ds(ih * 128, 128)]
                    for b in range(4)
                ]
                for p in range(2):
                    a, c = v[p], v[p + 2]
                    v[p] = jnp.where(low_half, a, pltpu.roll(c, 64, 1))
                    v[p + 2] = jnp.where(low_half, pltpu.roll(a, 64, 1), c)
                for p in (0, 2):
                    a, c = v[p], v[p + 1]
                    v[p] = jnp.where(even, a, pltpu.roll(c, 32, 1))
                    v[p + 1] = jnp.where(even, pltpu.roll(a, 96, 1), c)
                for il in range(4):
                    i = ih % 2 * 4 + il
                    row = ih // 2 * 128 + turned_rows(i) * 16 + o * 8
                    flat_ref[pl.ds(row, 8), pl.ds(bh * 128, 128)] = v[il]
    pair = jnp.concatenate(
        [pair_ref[turned_rows(p), yh] for p in range(8)] + [met_ref[pl.ds(256, 128), :]], 0
    )
    mid = pair + dot_deep(flat_ref[...], w_outer_ref[...])
    normed = layer_norm(mid, -1)
    projected = dot_t(w_tri_ref[...], normed)
    for side in range(2):
        plain, gating = projected[side * 256 :][:128], projected[side * 256 + 128 :][:128]
        edge = sigmoid(gating) * plain
        for h in range(2):
            q = side * 2 + h
            own, met = edge[h * 64 : h * 64 + 64, :128], edge[h * 64 : h * 64 + 64, 128:]
            edges_ref[pl.ds(q * 2, 64, stride=8), :] = jnp.where(yh == 0, own, met)
            edges_ref[pl.ds(q * 2 + 1, 64, stride=8), :] = jnp.where(yh == 0, met, own)
    gate = sigmoid(dot_deep(normed, w_gate_ref[...]))
    kept_ref[0], kept_ref[1] = mid[:128], gate[:128]
    sent_ref[0], sent_ref[1] = mid[128:], gate[128:]


def turn_blocks(x, masks):
    x = pltpu.roll(x, 0, 1, stride=16, stride_axis=0)
    for bit, mask in zip((1, 2, 4), masks):
        x = jnp.where(mask, pltpu.roll(x, 8 - bit, 0), x)
    return pltpu.roll(x, 0, 1, stride=16, stride_axis=0)


def triangle_kernel(left_ref, right_ref, out_ref, l_ref, r_ref):
    lane = lax.broadcasted_iota(jnp.int32, (8, 128), 1)
    masks = [(lane // 16) & bit != 0 for bit in (1, 2, 4)]
    for h in range(2):
        for z in range(8):
            for y in range(2):
                x = left_ref[pl.ds(z * 64 + h * 2 + y, 8, stride=8), :]
                l_ref[pl.ds(y * 64 + z * 8, 8), :] = turn_blocks(x, masks)
                for o in range(2):
                    x = right_ref[pl.ds(o * 256 + z * 32 + h * 2 + y, 8, stride=4), :]
                    row = y * 128 + turned_rows(z) * 16 + o * 8
                    r_ref[pl.ds(row, 8), :] = turn_blocks(x, masks)
        mixed = dot_t(l_ref[...], r_ref[...])
        for z in range(8):
            for y in range(2):
                for half in range(2):
                    block = mixed[y * 64 + z * 8 :, half * 128 :][:8, :128]
                    out_ref[pl.ds((z * 2 + y) * 32 + h * 2 + half, 8, stride=4), :] = turn_blocks(
                        block, masks
                    )


def output_kernel(mixed_ref, kept_ref, met_ref, w_ref, out_ref):
    yh = lax.axis_index("yh")
    w = w_ref[...]
    for half in range(2):
        tiles = []
        for h in range(2):
            for z in range(8):
                parts = [
                    mixed_ref[pl.ds((z * 2 + y) * 32 + h * 2 + half, 8, stride=4), :]
                    for y in range(2)
                ]
                tiles.append(parts[0] + parts[1])
        update = dot_deep(layer_norm(jnp.concatenate(tiles, 0), 0).T, w)
        mid = jnp.where(yh == half, kept_ref[0], met_ref[0])
        gate = jnp.where(yh == half, kept_ref[1], met_ref[1])
        for i in range(8):
            p = turned_rows(i) * 16
            out_ref[i, half] = mid[p : p + 16] + gate[p : p + 16] * update[i * 16 : i * 16 + 16]


def call(kernel, out_shapes, scratch, *args):
    shapes = [jax.ShapeDtypeStruct(s, jnp.float32) for s in out_shapes]
    return pl.pallas_call(
        kernel,
        out_shape=shapes if len(shapes) > 1 else shapes[0],
        scratch_shapes=scratch,
        compiler_params=pltpu.CompilerParams(vmem_limit_bytes=VMEM_LIMIT),
    )(*args)


def vmem(*shape):
    return pltpu.VMEM(shape, jnp.float32)


def factors(homolog, first, second, pair):
    return call(
        factor_kernel, [(384, 128), (256, 128)], [vmem(1024, 128)], homolog, first, second, pair
    )


def pair_stage(own, met, panel, pair, w_outer, w_tri, w_gate):
    return call(
        pair_kernel,
        [(512, 128), (2, 128, 128), (2, 128, 128)],
        [vmem(512, 512), vmem(256, 1024)],
        own, met, panel, pair, w_outer, w_tri, w_gate,
    )


def triangle(left, right):
    return call(triangle_kernel, [(512, 128)], [vmem(128, 128), vmem(256, 128)], left, right)


def output_stage(mixed, kept, met, w_out):
    return call(output_kernel, [(8, 2, 16, 128)], [], mixed, kept, met, w_out)


def per_device(homolog, pair, w_first, w_second, w_outer, w_tri, w_gate, w_out):
    pair = pair.reshape(8, 2, 16, 128)
    shared, right = factors(homolog, w_first.T, w_second.T, pair)
    swap = [(0, 1), (1, 0)]
    panel = lax.ppermute(right, ALL, panel_permutation())
    met = lax.ppermute(shared, "yh", swap)
    w_outer_ba = w_outer.reshape(32, 32, 128).transpose(1, 0, 2).reshape(1024, 128)
    panel = lax.all_gather(panel, "core", axis=0, tiled=True)
    edges, kept, sent = pair_stage(shared, met, panel, pair, w_outer_ba, w_tri.T, w_gate)
    returned = lax.ppermute(sent, "yh", swap)
    swapped = lax.all_to_all(edges.reshape(64, 8, 128), LAYER, 0, 0, tiled=True)
    rights = lax.all_gather(swapped[:, 4:], "core", axis=0, tiled=True)
    rights, returned = lax.optimization_barrier((rights, returned))
    back = triangle(swapped.reshape(512, 128), rights.reshape(512, 128))
    mixed = lax.all_to_all(back.reshape(128, 4, 128), CHIPS, 0, 0, tiled=True)
    return output_stage(mixed.reshape(512, 128), kept, returned, w_out).reshape(8, 32, 128)


def solution(mesh):
    fine = Mesh(mesh.devices.reshape(8, 2, 2, 4, 2), ALL)
    placed = (P(None, ROW, None), P(ROW, COL, None), P(), P(), P(), P(), P(), P())
    return jax.shard_map(
        per_device, mesh=fine, in_specs=placed, out_specs=P(ROW, COL, None), check_vma=False
    )
```

```python
import jax
import jax.numpy as jnp
from jax import lax
from jax.experimental import pallas as pl
from jax.experimental.pallas import tpu as pltpu
from jax.sharding import Mesh, PartitionSpec as P

epsilon = 1e-05

ALL = ("z", "yh", "core", "x", "yl")
ROW = ("z", "yh", "core")
COL = ("x", "yl")
LAYER = ("z", "x", "yl")
CHIPS = ("z", "yh", "x", "yl")
VMEM_LIMIT = 32 * 1024 * 1024


PANEL_COLUMNS = (
    (34570126, 24563107, 1675324, 1674523, 1236754, 1234675, 12467530, 1376452),
    (34560127, 45673102, 1675423, 1674253, 1237654, 2643175, 12467530, 1376542),
)


def panel_permutation():
    pairs = []
    for z in range(8):
        for yh in range(2):
            for core in range(2):
                for c in range(8):
                    column = PANEL_COLUMNS[yh][c] // 10 ** (7 - z) % 10
                    source = ((c * 2 + yh) * 2 + core) * 8 + column
                    pairs.append((source, ((z * 2 + yh) * 2 + core) * 8 + c))
    return pairs


def mm(a, b):
    return jnp.dot(a, b, preferred_element_type=jnp.float32)


def mm_t(a, b):
    return lax.dot_general(a, b, (((1,), (1,)), ((), ())), preferred_element_type=jnp.float32)


def split(x):
    high = x.astype(jnp.bfloat16)
    return high, (x - high.astype(jnp.float32)).astype(jnp.bfloat16)


def dot_deep(a, b):
    a_high, a_low = split(a)
    b_high, b_low = split(b)
    both = mm(a_high, jnp.concatenate([b_high, b_low], 1))
    return both[:, :128] + both[:, 128:] + mm(a_low, b_high)


def dot_t(a, b):
    a_high, a_low = split(a)
    b_high, b_low = split(b)
    shared = mm_t(jnp.concatenate([a_high, a_low], 1), jnp.concatenate([b_high, b_high], 1))
    return shared + mm_t(a_high, b_low)


def layer_norm(values, axis):
    average = jnp.mean(values, axis, keepdims=True)
    centred = values - average
    variance = jnp.mean(centred * centred, axis, keepdims=True)
    return centred * lax.rsqrt(variance + epsilon)


def sigmoid(x):
    return 1.0 / (1.0 + jnp.exp(-x))


def turned_rows(p):
    return (8 - p) % 8


def factor_kernel(
    msa_ref, first_ref, second_ref, pair_ref, shared_ref, right_ref,
    msa, w, pair, result, sems,
):
    other = 1 - lax.axis_index("yh")
    weights = [
        pltpu.make_async_copy(first_ref, w.at[pl.ds(0, 32)], sems.at[4]),
        pltpu.make_async_copy(second_ref, w.at[pl.ds(32, 32)], sems.at[5]),
    ]
    chunks = [
        pltpu.make_async_copy(
            msa_ref.at[pl.ds(k * 32, 32)], msa.at[pl.ds(k * 32, 32)], sems.at[k]
        )
        for k in range(4)
    ]
    pairs = pltpu.make_async_copy(pair_ref, pair, sems.at[6])
    for copy in weights + chunks + [pairs]:
        copy.start()
    for copy in weights:
        copy.wait()
    w_high, w_low = split(w[...])
    w_both = jnp.concatenate([w_high, w_low], 0)
    w_rest = jnp.concatenate([w_high, jnp.zeros_like(w_high)], 0)
    for k in range(4):
        chunks[k].wait()
        n_high, n_low = split(layer_norm(msa[pl.ds(k * 32, 32)].reshape(256, 256), -1))
        result[pl.ds(k * 256, 256), :] = mm_t(n_high, w_both) + mm_t(n_low, w_rest)
    for i in range(8):
        turned = result[pl.ds(i, 128, stride=8), :].T
        both = turned[:64] + turned[64:]
        shared_ref[pl.ds(i * 32, 32), :] = both[:32] * (1.0 / 128.0)
        right_ref[pl.ds(i, 32, stride=8), :] = both[32:]
    pairs.wait()
    for p in range(8):
        shared_ref[pl.ds(256 + p * 16, 16), :] = pair[turned_rows(p), other]


def pair_kernel(
    own_ref, met_ref, panel_ref, pair_ref, w_outer_ref, w_tri_ref, w_gate_ref,
    edges_ref, kept_ref, sent_ref, outer_ref, flat_ref,
):
    yh = lax.axis_index("yh")
    left = jnp.concatenate([own_ref[pl.ds(0, 256), :], met_ref[pl.ds(0, 256), :]], 0)
    outer_ref[...] = dot_t(panel_ref[...], left)
    lane = lax.broadcasted_iota(jnp.int32, (8, 128), 1)
    low_half = lane < 64
    even = (lane // 32) % 2 == 0
    for o in range(2):
        for bh in range(8):
            for ih in range(4):
                v = [
                    outer_ref[pl.ds((o * 32 + bh * 4 + b) * 8, 8), pl.ds(ih * 128, 128)]
                    for b in range(4)
                ]
                for p in range(2):
                    a, c = v[p], v[p + 2]
                    v[p] = jnp.where(low_half, a, pltpu.roll(c, 64, 1))
                    v[p + 2] = jnp.where(low_half, pltpu.roll(a, 64, 1), c)
                for p in (0, 2):
                    a, c = v[p], v[p + 1]
                    v[p] = jnp.where(even, a, pltpu.roll(c, 32, 1))
                    v[p + 1] = jnp.where(even, pltpu.roll(a, 96, 1), c)
                for il in range(4):
                    i = ih % 2 * 4 + il
                    row = ih // 2 * 128 + turned_rows(i) * 16 + o * 8
                    flat_ref[pl.ds(row, 8), pl.ds(bh * 128, 128)] = v[il]
    pair = jnp.concatenate(
        [pair_ref[turned_rows(p), yh] for p in range(8)] + [met_ref[pl.ds(256, 128), :]], 0
    )
    mid = pair + dot_deep(flat_ref[...], w_outer_ref[...])
    normed = layer_norm(mid, -1)
    projected = dot_t(w_tri_ref[...], normed)
    for side in range(2):
        plain, gating = projected[side * 256 :][:128], projected[side * 256 + 128 :][:128]
        edge = sigmoid(gating) * plain
        for h in range(2):
            q = side * 2 + h
            own, met = edge[h * 64 : h * 64 + 64, :128], edge[h * 64 : h * 64 + 64, 128:]
            edges_ref[pl.ds(q * 2, 64, stride=8), :] = jnp.where(yh == 0, own, met)
            edges_ref[pl.ds(q * 2 + 1, 64, stride=8), :] = jnp.where(yh == 0, met, own)
    gate = sigmoid(dot_deep(normed, w_gate_ref[...]))
    kept_ref[0], kept_ref[1] = mid[:128], gate[:128]
    sent_ref[0], sent_ref[1] = mid[128:], gate[128:]


def turn_blocks(x, masks):
    x = pltpu.roll(x, 0, 1, stride=16, stride_axis=0)
    for bit, mask in zip((1, 2, 4), masks):
        x = jnp.where(mask, pltpu.roll(x, 8 - bit, 0), x)
    return pltpu.roll(x, 0, 1, stride=16, stride_axis=0)


def triangle_kernel(left_ref, right_ref, out_ref, l_ref, r_ref):
    lane = lax.broadcasted_iota(jnp.int32, (8, 128), 1)
    masks = [(lane // 16) & bit != 0 for bit in (1, 2, 4)]
    for h in range(2):
        for z in range(8):
            for y in range(2):
                x = left_ref[pl.ds(z * 64 + h * 2 + y, 8, stride=8), :]
                l_ref[pl.ds(y * 64 + z * 8, 8), :] = turn_blocks(x, masks)
                for o in range(2):
                    x = right_ref[pl.ds(o * 256 + z * 32 + h * 2 + y, 8, stride=4), :]
                    row = y * 128 + turned_rows(z) * 16 + o * 8
                    r_ref[pl.ds(row, 8), :] = turn_blocks(x, masks)
        mixed = dot_t(l_ref[...], r_ref[...])
        for z in range(8):
            for y in range(2):
                for half in range(2):
                    block = mixed[y * 64 + z * 8 :, half * 128 :][:8, :128]
                    out_ref[pl.ds((z * 2 + y) * 32 + h * 2 + half, 8, stride=4), :] = turn_blocks(
                        block, masks
                    )


def output_kernel(mixed_ref, kept_ref, met_ref, w_ref, out_ref):
    yh = lax.axis_index("yh")
    w = w_ref[...]
    for half in range(2):
        tiles = []
        for h in range(2):
            for z in range(8):
                parts = [
                    mixed_ref[pl.ds((z * 2 + y) * 32 + h * 2 + half, 8, stride=4), :]
                    for y in range(2)
                ]
                tiles.append(parts[0] + parts[1])
        update = dot_deep(layer_norm(jnp.concatenate(tiles, 0), 0).T, w)
        mid = jnp.where(yh == half, kept_ref[0], met_ref[0])
        gate = jnp.where(yh == half, kept_ref[1], met_ref[1])
        for i in range(8):
            p = turned_rows(i) * 16
            out_ref[i, half] = mid[p : p + 16] + gate[p : p + 16] * update[i * 16 : i * 16 + 16]


def call(kernel, out_shapes, scratch, *args, limit=VMEM_LIMIT, **more):
    shapes = [jax.ShapeDtypeStruct(s, jnp.float32) for s in out_shapes]
    return pl.pallas_call(
        kernel,
        out_shape=shapes if len(shapes) > 1 else shapes[0],
        scratch_shapes=scratch,
        compiler_params=pltpu.CompilerParams(vmem_limit_bytes=limit),
        **more,
    )(*args)


def vmem(*shape):
    return pltpu.VMEM(shape, jnp.float32)


def factors(homolog, first, second, pair):
    return call(
        factor_kernel,
        [(384, 128), (256, 128)],
        [
            vmem(128, 8, 256), vmem(64, 256), vmem(8, 2, 16, 128), vmem(1024, 128),
            pltpu.SemaphoreType.DMA((7,)),
        ],
        homolog, first, second, pair,
        in_specs=[pl.BlockSpec(memory_space=pltpu.HBM)] * 4,
        limit=53 * 1024 * 1024,
    )


def pair_stage(own, met, panel, pair, w_outer, w_tri, w_gate):
    return call(
        pair_kernel,
        [(512, 128), (2, 128, 128), (2, 128, 128)],
        [vmem(512, 512), vmem(256, 1024)],
        own, met, panel, pair, w_outer, w_tri, w_gate,
    )


def triangle(left, right):
    return call(triangle_kernel, [(512, 128)], [vmem(128, 128), vmem(256, 128)], left, right)


def output_stage(mixed, kept, met, w_out):
    return call(output_kernel, [(8, 2, 16, 128)], [], mixed, kept, met, w_out)


def per_device(homolog, pair, w_first, w_second, w_outer, w_tri, w_gate, w_out):
    pair = pair.reshape(8, 2, 16, 128)
    shared, right = factors(homolog, w_first.T, w_second.T, pair)
    swap = [(0, 1), (1, 0)]
    panel = lax.ppermute(right, ALL, panel_permutation())
    met = lax.ppermute(shared, "yh", swap)
    w_outer_ba = w_outer.reshape(32, 32, 128).transpose(1, 0, 2).reshape(1024, 128)
    panel = lax.all_gather(panel, "core", axis=0, tiled=True)
    edges, kept, sent = pair_stage(shared, met, panel, pair, w_outer_ba, w_tri.T, w_gate)
    swapped = lax.all_to_all(edges.reshape(64, 8, 128), LAYER, 0, 0, tiled=True)
    sent, swapped = lax.optimization_barrier((sent, swapped))
    returned = lax.ppermute(sent, "yh", swap)
    rights = lax.all_gather(swapped[:, 4:], "core", axis=0, tiled=True)
    back = triangle(swapped.reshape(512, 128), rights.reshape(512, 128))
    back, returned = lax.optimization_barrier((back, returned))
    mixed = lax.all_to_all(back.reshape(128, 4, 128), CHIPS, 0, 0, tiled=True)
    return output_stage(mixed.reshape(512, 128), kept, returned, w_out).reshape(8, 32, 128)


def solution(mesh):
    fine = Mesh(mesh.devices.reshape(8, 2, 2, 4, 2), ALL)
    placed = (P(None, ROW, None), P(ROW, COL, None), P(), P(), P(), P(), P(), P())
    return jax.shard_map(
        per_device, mesh=fine, in_specs=placed, out_specs=P(ROW, COL, None), check_vma=False
    )
```

```python
import jax
import jax.numpy as jnp
from jax import lax
from jax.experimental import pallas as pl
from jax.experimental.pallas import tpu as pltpu
from jax.sharding import Mesh, PartitionSpec as P

epsilon = 1e-05

ALL = ("z", "yh", "core", "x", "yl")
ROW = ("z", "yh", "core")
COL = ("x", "yl")
LAYER = ("z", "x", "yl")
CHIPS = ("z", "yh", "x", "yl")
VMEM_LIMIT = 32 * 1024 * 1024


PANEL_COLUMNS = (
    (34570126, 24563107, 1675324, 1674523, 1236754, 1234675, 12467530, 1376452),
    (34560127, 45673102, 1675423, 1674253, 1237654, 2643175, 12467530, 1376542),
)


def panel_permutation():
    pairs = []
    for z in range(8):
        for yh in range(2):
            for core in range(2):
                for c in range(8):
                    column = PANEL_COLUMNS[yh][c] // 10 ** (7 - z) % 10
                    source = ((c * 2 + yh) * 2 + core) * 8 + column
                    pairs.append((source, ((z * 2 + yh) * 2 + core) * 8 + c))
    return pairs


def mm(a, b):
    return jnp.dot(a, b, preferred_element_type=jnp.float32)


def mm_t(a, b):
    return lax.dot_general(a, b, (((1,), (1,)), ((), ())), preferred_element_type=jnp.float32)


def split(x):
    high = x.astype(jnp.bfloat16)
    return high, (x - high.astype(jnp.float32)).astype(jnp.bfloat16)


def dot_deep(a, b):
    a_high, a_low = split(a)
    b_high, b_low = split(b)
    both = mm(a_high, jnp.concatenate([b_high, b_low], 1))
    return both[:, :128] + both[:, 128:] + mm(a_low, b_high)


def dot_t(a, b):
    a_high, a_low = split(a)
    b_high, b_low = split(b)
    shared = mm_t(jnp.concatenate([a_high, a_low], 1), jnp.concatenate([b_high, b_high], 1))
    return shared + mm_t(a_high, b_low)


def layer_norm(values, axis):
    average = jnp.mean(values, axis, keepdims=True)
    centred = values - average
    variance = jnp.mean(centred * centred, axis, keepdims=True)
    return centred * lax.rsqrt(variance + epsilon)


def sigmoid(x):
    return 1.0 / (1.0 + jnp.exp(-x))


def turned_rows(p):
    return (8 - p) % 8


def factor_kernel(msa_ref, first_ref, second_ref, pair_ref, shared_ref, right_ref, result):
    other = 1 - lax.axis_index("yh")
    w_high, w_low = split(jnp.concatenate([first_ref[...], second_ref[...]], 0))
    w_both = jnp.concatenate([w_high, w_low], 0)
    w_rest = jnp.concatenate([w_high, jnp.zeros_like(w_high)], 0)
    for k in range(4):
        n_high, n_low = split(layer_norm(msa_ref[pl.ds(k * 32, 32)].reshape(256, 256), -1))
        result[pl.ds(k * 256, 256), :] = mm_t(n_high, w_both) + mm_t(n_low, w_rest)
    for i in range(8):
        turned = result[pl.ds(i, 128, stride=8), :].T
        both = turned[:64] + turned[64:]
        shared_ref[pl.ds(i * 32, 32), :] = both[:32] * (1.0 / 128.0)
        right_ref[pl.ds(i, 32, stride=8), :] = both[32:]
    for p in range(8):
        shared_ref[pl.ds(256 + p * 16, 16), :] = pair_ref[turned_rows(p), other]


def pair_kernel(
    own_ref, met_ref, panel_ref, pair_ref, w_outer_ref, w_tri_ref, w_gate_ref,
    edges_ref, kept_ref, sent_ref, outer_ref, flat_ref,
):
    yh = lax.axis_index("yh")
    left = jnp.concatenate([own_ref[pl.ds(0, 256), :], met_ref[pl.ds(0, 256), :]], 0)
    outer_ref[...] = dot_t(panel_ref[...], left)
    lane = lax.broadcasted_iota(jnp.int32, (8, 128), 1)
    low_half = lane < 64
    even = (lane // 32) % 2 == 0
    for o in range(2):
        for bh in range(8):
            for ih in range(4):
                v = [
                    outer_ref[pl.ds((o * 32 + bh * 4 + b) * 8, 8), pl.ds(ih * 128, 128)]
                    for b in range(4)
                ]
                for p in range(2):
                    a, c = v[p], v[p + 2]
                    v[p] = jnp.where(low_half, a, pltpu.roll(c, 64, 1))
                    v[p + 2] = jnp.where(low_half, pltpu.roll(a, 64, 1), c)
                for p in (0, 2):
                    a, c = v[p], v[p + 1]
                    v[p] = jnp.where(even, a, pltpu.roll(c, 32, 1))
                    v[p + 1] = jnp.where(even, pltpu.roll(a, 96, 1), c)
                for il in range(4):
                    i = ih % 2 * 4 + il
                    row = ih // 2 * 128 + turned_rows(i) * 16 + o * 8
                    flat_ref[pl.ds(row, 8), pl.ds(bh * 128, 128)] = v[il]
    pair = jnp.concatenate(
        [pair_ref[turned_rows(p), yh] for p in range(8)] + [met_ref[pl.ds(256, 128), :]], 0
    )
    mid = pair + dot_deep(flat_ref[...], w_outer_ref[...])
    normed = layer_norm(mid, -1)
    projected = dot_t(w_tri_ref[...], normed)
    for side in range(2):
        plain, gating = projected[side * 256 :][:128], projected[side * 256 + 128 :][:128]
        edge = sigmoid(gating) * plain
        for h in range(2):
            q = side * 2 + h
            own, met = edge[h * 64 : h * 64 + 64, :128], edge[h * 64 : h * 64 + 64, 128:]
            edges_ref[pl.ds(q * 2, 64, stride=8), :] = jnp.where(yh == 0, own, met)
            edges_ref[pl.ds(q * 2 + 1, 64, stride=8), :] = jnp.where(yh == 0, met, own)
    gate = sigmoid(dot_deep(normed, w_gate_ref[...]))
    kept_ref[0], kept_ref[1] = mid[:128], gate[:128]
    sent_ref[0], sent_ref[1] = mid[128:], gate[128:]


def turn_blocks(x, masks):
    x = pltpu.roll(x, 0, 1, stride=16, stride_axis=0)
    for bit, mask in zip((1, 2, 4), masks):
        x = jnp.where(mask, pltpu.roll(x, 8 - bit, 0), x)
    return pltpu.roll(x, 0, 1, stride=16, stride_axis=0)


def triangle_kernel(left_ref, right_ref, out_ref, l_ref, r_ref):
    lane = lax.broadcasted_iota(jnp.int32, (8, 128), 1)
    masks = [(lane // 16) & bit != 0 for bit in (1, 2, 4)]
    for h in range(2):
        for z in range(8):
            for y in range(2):
                x = left_ref[pl.ds(z * 64 + h * 2 + y, 8, stride=8), :]
                l_ref[pl.ds(y * 64 + z * 8, 8), :] = turn_blocks(x, masks)
                for o in range(2):
                    x = right_ref[pl.ds(o * 256 + z * 32 + h * 2 + y, 8, stride=4), :]
                    row = y * 128 + turned_rows(z) * 16 + o * 8
                    r_ref[pl.ds(row, 8), :] = turn_blocks(x, masks)
        mixed = dot_t(l_ref[...], r_ref[...])
        for z in range(8):
            for y in range(2):
                for half in range(2):
                    block = mixed[y * 64 + z * 8 :, half * 128 :][:8, :128]
                    out_ref[pl.ds((z * 2 + y) * 32 + h * 2 + half, 8, stride=4), :] = turn_blocks(
                        block, masks
                    )


def output_kernel(mixed_ref, kept_ref, met_ref, w_ref, out_ref):
    yh = lax.axis_index("yh")
    w = w_ref[...]
    for half in range(2):
        tiles = []
        for h in range(2):
            for z in range(8):
                parts = [
                    mixed_ref[pl.ds((z * 2 + y) * 32 + h * 2 + half, 8, stride=4), :]
                    for y in range(2)
                ]
                tiles.append(parts[0] + parts[1])
        update = dot_deep(layer_norm(jnp.concatenate(tiles, 0), 0).T, w)
        mid = jnp.where(yh == half, kept_ref[0], met_ref[0])
        gate = jnp.where(yh == half, kept_ref[1], met_ref[1])
        for i in range(8):
            p = turned_rows(i) * 16
            out_ref[i, half] = mid[p : p + 16] + gate[p : p + 16] * update[i * 16 : i * 16 + 16]


def call(kernel, out_shapes, scratch, *args, limit=VMEM_LIMIT):
    shapes = [jax.ShapeDtypeStruct(s, jnp.float32) for s in out_shapes]
    return pl.pallas_call(
        kernel,
        out_shape=shapes if len(shapes) > 1 else shapes[0],
        scratch_shapes=scratch,
        compiler_params=pltpu.CompilerParams(vmem_limit_bytes=limit),
    )(*args)


def vmem(*shape):
    return pltpu.VMEM(shape, jnp.float32)


def factors(homolog, first, second, pair):
    return call(
        factor_kernel, [(384, 128), (256, 128)], [vmem(1024, 128)], homolog, first, second, pair,
        limit=60 * 1024 * 1024,
    )


def pair_stage(own, met, panel, pair, w_outer, w_tri, w_gate):
    return call(
        pair_kernel,
        [(512, 128), (2, 128, 128), (2, 128, 128)],
        [vmem(512, 512), vmem(256, 1024)],
        own, met, panel, pair, w_outer, w_tri, w_gate,
    )


def triangle(left, right):
    return call(triangle_kernel, [(512, 128)], [vmem(128, 128), vmem(256, 128)], left, right)


def output_stage(mixed, kept, met, w_out):
    return call(output_kernel, [(8, 2, 16, 128)], [], mixed, kept, met, w_out)


def per_device(homolog, pair, w_first, w_second, w_outer, w_tri, w_gate, w_out):
    pair = pair.reshape(8, 2, 16, 128)
    shared, right = factors(homolog, w_first.T, w_second.T, pair)
    swap = [(0, 1), (1, 0)]
    panel = lax.ppermute(right, ALL, panel_permutation())
    met = lax.ppermute(shared, "yh", swap)
    w_outer_ba = w_outer.reshape(32, 32, 128).transpose(1, 0, 2).reshape(1024, 128)
    panel = lax.all_gather(panel, "core", axis=0, tiled=True)
    edges, kept, sent = pair_stage(shared, met, panel, pair, w_outer_ba, w_tri.T, w_gate)
    swapped = lax.all_to_all(edges.reshape(64, 8, 128), LAYER, 0, 0, tiled=True)
    returned = lax.ppermute(sent, "yh", swap)
    rights = lax.all_gather(swapped[:, 4:], "core", axis=0, tiled=True)
    back = triangle(swapped.reshape(512, 128), rights.reshape(512, 128))
    mixed = lax.all_to_all(back.reshape(128, 4, 128), CHIPS, 0, 0, tiled=True)
    return output_stage(mixed.reshape(512, 128), kept, returned, w_out).reshape(8, 32, 128)


def solution(mesh):
    fine = Mesh(mesh.devices.reshape(8, 2, 2, 4, 2), ALL)
    placed = (P(None, ROW, None), P(ROW, COL, None), P(), P(), P(), P(), P(), P())
    return jax.shard_map(
        per_device, mesh=fine, in_specs=placed, out_specs=P(ROW, COL, None), check_vma=False
    )
```

```python
import jax
import jax.numpy as jnp
from jax import lax
from jax.experimental import pallas as pl
from jax.experimental.pallas import tpu as pltpu
from jax.sharding import Mesh, PartitionSpec as P

epsilon = 1e-05

ALL = ("z", "yh", "core", "x", "yl")
ROW = ("z", "yh", "core")
COL = ("x", "yl")
LAYER = ("z", "x", "yl")
CHIPS = ("z", "yh", "x", "yl")
VMEM_LIMIT = 32 * 1024 * 1024


PANEL_COLUMNS = (
    (72361054, 54671032, 53160427, 1764253, 74562031, 25647103, 76045231, 5476312),
    (61053247, 45671032, 30176425, 62347501, 34205176, 50761342, 42635701, 4276513),
)


def panel_permutation():
    pairs = []
    for z in range(8):
        for yh in range(2):
            for core in range(2):
                for c in range(8):
                    column = PANEL_COLUMNS[yh][c] // 10 ** (7 - z) % 10
                    source = ((c * 2 + yh) * 2 + core) * 8 + column
                    pairs.append((source, ((z * 2 + yh) * 2 + core) * 8 + c))
    return pairs


def mm(a, b):
    return jnp.dot(a, b, preferred_element_type=jnp.float32)


def mm_t(a, b):
    return lax.dot_general(a, b, (((1,), (1,)), ((), ())), preferred_element_type=jnp.float32)


def split(x):
    high = x.astype(jnp.bfloat16)
    return high, (x - high.astype(jnp.float32)).astype(jnp.bfloat16)


def dot_deep(a, b):
    a_high, a_low = split(a)
    b_high, b_low = split(b)
    both = mm(a_high, jnp.concatenate([b_high, b_low], 1))
    return both[:, :128] + both[:, 128:] + mm(a_low, b_high)


def dot_t(a, b):
    a_high, a_low = split(a)
    b_high, b_low = split(b)
    shared = mm_t(jnp.concatenate([a_high, a_low], 1), jnp.concatenate([b_high, b_high], 1))
    return shared + mm_t(a_high, b_low)


def layer_norm(values, axis):
    average = jnp.mean(values, axis, keepdims=True)
    centred = values - average
    variance = jnp.mean(centred * centred, axis, keepdims=True)
    return centred * lax.rsqrt(variance + epsilon)


def sigmoid(x):
    return 1.0 / (1.0 + jnp.exp(-x))


def turned_rows(p):
    return (8 - p) % 8


def factor_kernel(msa_ref, first_ref, second_ref, pair_ref, shared_ref, right_ref, result):
    other = 1 - lax.axis_index("yh")
    w_high, w_low = split(jnp.concatenate([first_ref[...], second_ref[...]], 0))
    w_both = jnp.concatenate([w_high, w_low], 0)
    w_rest = jnp.concatenate([w_high, jnp.zeros_like(w_high)], 0)
    for k in range(4):
        n_high, n_low = split(layer_norm(msa_ref[pl.ds(k * 32, 32)].reshape(256, 256), -1))
        result[pl.ds(k * 256, 256), :] = mm_t(n_high, w_both) + mm_t(n_low, w_rest)
    for i in range(8):
        turned = result[pl.ds(i, 128, stride=8), :].T
        both = turned[:64] + turned[64:]
        shared_ref[pl.ds(i * 32, 32), :] = both[:32] * (1.0 / 128.0)
        right_ref[pl.ds(i, 32, stride=8), :] = both[32:]
    for p in range(8):
        shared_ref[pl.ds(256 + p * 16, 16), :] = pair_ref[turned_rows(p), other]


def pair_kernel(
    own_ref, met_ref, panel_ref, sibling_ref, pair_ref, w_outer_ref, w_tri_ref, w_gate_ref,
    edges_ref, kept_ref, sent_ref, outer_ref, flat_ref,
):
    yh = lax.axis_index("yh")
    left = jnp.concatenate([own_ref[pl.ds(0, 256), :], met_ref[pl.ds(0, 256), :]], 0)
    first = lax.axis_index("core") == 0
    panel, sibling = panel_ref[...], sibling_ref[...]
    panels = jnp.concatenate(
        [jnp.where(first, panel, sibling), jnp.where(first, sibling, panel)], 0
    )
    outer_ref[...] = dot_t(panels, left)
    lane = lax.broadcasted_iota(jnp.int32, (8, 128), 1)
    low_half = lane < 64
    even = (lane // 32) % 2 == 0
    for o in range(2):
        for bh in range(8):
            for ih in range(4):
                v = [
                    outer_ref[pl.ds((o * 32 + bh * 4 + b) * 8, 8), pl.ds(ih * 128, 128)]
                    for b in range(4)
                ]
                for p in range(2):
                    a, c = v[p], v[p + 2]
                    v[p] = jnp.where(low_half, a, pltpu.roll(c, 64, 1))
                    v[p + 2] = jnp.where(low_half, pltpu.roll(a, 64, 1), c)
                for p in (0, 2):
                    a, c = v[p], v[p + 1]
                    v[p] = jnp.where(even, a, pltpu.roll(c, 32, 1))
                    v[p + 1] = jnp.where(even, pltpu.roll(a, 96, 1), c)
                for il in range(4):
                    i = ih % 2 * 4 + il
                    row = ih // 2 * 128 + turned_rows(i) * 16 + o * 8
                    flat_ref[pl.ds(row, 8), pl.ds(bh * 128, 128)] = v[il]
    pair = jnp.concatenate(
        [pair_ref[turned_rows(p), yh] for p in range(8)] + [met_ref[pl.ds(256, 128), :]], 0
    )
    mid = pair + dot_deep(flat_ref[...], w_outer_ref[...])
    normed = layer_norm(mid, -1)
    projected = dot_t(w_tri_ref[...], normed)
    for side in range(2):
        plain, gating = projected[side * 256 :][:128], projected[side * 256 + 128 :][:128]
        edge = sigmoid(gating) * plain
        for h in range(2):
            q = side * 2 + h
            own, met = edge[h * 64 : h * 64 + 64, :128], edge[h * 64 : h * 64 + 64, 128:]
            edges_ref[pl.ds(q * 2, 64, stride=8), :] = jnp.where(yh == 0, own, met)
            edges_ref[pl.ds(q * 2 + 1, 64, stride=8), :] = jnp.where(yh == 0, met, own)
    gate = sigmoid(dot_deep(normed, w_gate_ref[...]))
    kept_ref[0], kept_ref[1] = mid[:128], gate[:128]
    sent_ref[0], sent_ref[1] = mid[128:], gate[128:]


def turn_blocks(x, masks):
    x = pltpu.roll(x, 0, 1, stride=16, stride_axis=0)
    for bit, mask in zip((1, 2, 4), masks):
        x = jnp.where(mask, pltpu.roll(x, 8 - bit, 0), x)
    return pltpu.roll(x, 0, 1, stride=16, stride_axis=0)


def triangle_kernel(left_ref, right_ref, out_ref, l_ref, r_ref):
    core = lax.axis_index("core")
    lane = lax.broadcasted_iota(jnp.int32, (8, 128), 1)
    masks = [(lane // 16) & bit != 0 for bit in (1, 2, 4)]
    for h in range(2):
        for z in range(8):
            for y in range(2):
                x = left_ref[pl.ds(z * 64 + h * 2 + y, 8, stride=8), :]
                l_ref[pl.ds(y * 64 + z * 8, 8), :] = turn_blocks(x, masks)
                x = left_ref[pl.ds(z * 64 + (2 + h) * 2 + y, 8, stride=8), :]
                own = turn_blocks(x, masks)
                x = right_ref[pl.ds(z * 32 + h * 2 + y, 8, stride=4), :]
                other = turn_blocks(x, masks)
                row = y * 128 + turned_rows(z) * 16
                r_ref[pl.ds(row, 8), :] = jnp.where(core == 0, own, other)
                r_ref[pl.ds(row + 8, 8), :] = jnp.where(core == 0, other, own)
        mixed = dot_t(l_ref[...], r_ref[...])
        for z in range(8):
            for y in range(2):
                for half in range(2):
                    block = mixed[y * 64 + z * 8 :, half * 128 :][:8, :128]
                    out_ref[pl.ds((z * 2 + y) * 32 + h * 2 + half, 8, stride=4), :] = turn_blocks(
                        block, masks
                    )


def output_kernel(mixed_ref, kept_ref, met_ref, w_ref, out_ref):
    yh = lax.axis_index("yh")
    w = w_ref[...]
    for half in range(2):
        tiles = []
        for h in range(2):
            for z in range(8):
                parts = [
                    mixed_ref[pl.ds((z * 2 + y) * 32 + h * 2 + half, 8, stride=4), :]
                    for y in range(2)
                ]
                tiles.append(parts[0] + parts[1])
        update = dot_deep(layer_norm(jnp.concatenate(tiles, 0), 0).T, w)
        mid = jnp.where(yh == half, kept_ref[0], met_ref[0])
        gate = jnp.where(yh == half, kept_ref[1], met_ref[1])
        for i in range(8):
            p = turned_rows(i) * 16
            out_ref[i, half] = mid[p : p + 16] + gate[p : p + 16] * update[i * 16 : i * 16 + 16]


def call(kernel, out_shapes, scratch, *args, limit=VMEM_LIMIT):
    shapes = [jax.ShapeDtypeStruct(s, jnp.float32) for s in out_shapes]
    return pl.pallas_call(
        kernel,
        out_shape=shapes if len(shapes) > 1 else shapes[0],
        scratch_shapes=scratch,
        compiler_params=pltpu.CompilerParams(vmem_limit_bytes=limit),
    )(*args)


def vmem(*shape):
    return pltpu.VMEM(shape, jnp.float32)


def factors(homolog, first, second, pair):
    return call(
        factor_kernel, [(384, 128), (256, 128)], [vmem(1024, 128)], homolog, first, second, pair,
        limit=60 * 1024 * 1024,
    )


def pair_stage(own, met, panel, sibling, pair, w_outer, w_tri, w_gate):
    return call(
        pair_kernel,
        [(512, 128), (2, 128, 128), (2, 128, 128)],
        [vmem(512, 512), vmem(256, 1024)],
        own, met, panel, sibling, pair, w_outer, w_tri, w_gate,
    )


def triangle(left, right):
    return call(triangle_kernel, [(512, 128)], [vmem(128, 128), vmem(256, 128)], left, right)


def output_stage(mixed, kept, met, w_out):
    return call(output_kernel, [(8, 2, 16, 128)], [], mixed, kept, met, w_out)


def per_device(homolog, pair, w_first, w_second, w_outer, w_tri, w_gate, w_out):
    pair = pair.reshape(8, 2, 16, 128)
    shared, right = factors(homolog, w_first.T, w_second.T, pair)
    swap = [(0, 1), (1, 0)]
    panel = lax.ppermute(right, ALL, panel_permutation())
    met = lax.ppermute(shared, "yh", swap)
    w_outer_ba = w_outer.reshape(32, 32, 128).transpose(1, 0, 2).reshape(1024, 128)
    sibling = lax.ppermute(panel, "core", swap)
    edges, kept, sent = pair_stage(shared, met, panel, sibling, pair, w_outer_ba, w_tri.T, w_gate)
    swapped = lax.all_to_all(edges.reshape(64, 8, 128), LAYER, 0, 0, tiled=True)
    returned = lax.ppermute(sent, "yh", swap)
    rights = lax.ppermute(swapped[:, 4:], "core", swap)
    back = triangle(swapped.reshape(512, 128), rights.reshape(256, 128))
    mixed = lax.all_to_all(back.reshape(128, 4, 128), CHIPS, 0, 0, tiled=True)
    return output_stage(mixed.reshape(512, 128), kept, returned, w_out).reshape(8, 32, 128)


def solution(mesh):
    fine = Mesh(mesh.devices.reshape(8, 2, 2, 4, 2), ALL)
    placed = (P(None, ROW, None), P(ROW, COL, None), P(), P(), P(), P(), P(), P())
    return jax.shard_map(
        per_device, mesh=fine, in_specs=placed, out_specs=P(ROW, COL, None), check_vma=False
    )
```

```python
import jax
import jax.numpy as jnp
from jax import lax
from jax.experimental import pallas as pl
from jax.experimental.pallas import tpu as pltpu
from jax.sharding import Mesh, PartitionSpec as P

epsilon = 1e-05

ALL = ("z", "yh", "core", "x", "yl")
ROW = ("z", "yh", "core")
COL = ("x", "yl")
LAYER = ("z", "x", "yl")
CHIPS = ("z", "yh", "x", "yl")
VMEM_LIMIT = 32 * 1024 * 1024


PANEL_COLUMNS = (
    (72361054, 54671032, 53160427, 1764253, 74562031, 25647103, 76045231, 5476312),
    (61053247, 45671032, 30176425, 62347501, 34205176, 50761342, 42635701, 4276513),
)


def panel_permutation():
    pairs = []
    for z in range(8):
        for yh in range(2):
            for core in range(2):
                for c in range(8):
                    column = PANEL_COLUMNS[yh][c] // 10 ** (7 - z) % 10
                    source = ((c * 2 + yh) * 2 + core) * 8 + column
                    pairs.append((source, ((z * 2 + yh) * 2 + core) * 8 + c))
    return pairs


def mm(a, b):
    return jnp.dot(a, b, preferred_element_type=jnp.float32)


def mm_t(a, b):
    return lax.dot_general(a, b, (((1,), (1,)), ((), ())), preferred_element_type=jnp.float32)


def split(x):
    high = x.astype(jnp.bfloat16)
    return high, (x - high.astype(jnp.float32)).astype(jnp.bfloat16)


def dot_deep(a, b):
    a_high, a_low = split(a)
    b_high, b_low = split(b)
    both = mm(a_high, jnp.concatenate([b_high, b_low], 1))
    return both[:, :128] + both[:, 128:] + mm(a_low, b_high)


def dot_t(a, b):
    a_high, a_low = split(a)
    b_high, b_low = split(b)
    shared = mm_t(jnp.concatenate([a_high, a_low], 1), jnp.concatenate([b_high, b_high], 1))
    return shared + mm_t(a_high, b_low)


def layer_norm(values, axis):
    average = jnp.mean(values, axis, keepdims=True)
    centred = values - average
    variance = jnp.mean(centred * centred, axis, keepdims=True)
    return centred * lax.rsqrt(variance + epsilon)


def sigmoid(x):
    return 1.0 / (1.0 + jnp.exp(-x))


def turned_rows(p):
    return (8 - p) % 8


def factor_kernel(
    msa_ref, first_ref, second_ref, pair_ref, left_ref, right_ref, half_ref, result
):
    other = 1 - lax.axis_index("yh")
    w_high, w_low = split(jnp.concatenate([first_ref[...], second_ref[...]], 0))
    w_both = jnp.concatenate([w_high, w_low], 0)
    w_rest = jnp.concatenate([w_high, jnp.zeros_like(w_high)], 0)
    for k in range(4):
        n_high, n_low = split(layer_norm(msa_ref[pl.ds(k * 32, 32)].reshape(256, 256), -1))
        result[pl.ds(k * 256, 256), :] = mm_t(n_high, w_both) + mm_t(n_low, w_rest)
    for i in range(8):
        turned = result[pl.ds(i, 128, stride=8), :].T
        both = turned[:64] + turned[64:]
        left_ref[pl.ds(i * 32, 32), :] = both[:32] * (1.0 / 128.0)
        right_ref[pl.ds(i, 32, stride=8), :] = both[32:]
    for p in range(8):
        half_ref[pl.ds(p * 16, 16), :] = pair_ref[turned_rows(p), other]


def pair_kernel(
    own_ref, met_ref, met_pair_ref, panel_ref, sibling_ref, pair_ref, w_outer_ref, w_tri_ref, w_gate_ref,
    edges_ref, kept_ref, sent_ref, outer_ref, flat_ref,
):
    yh = lax.axis_index("yh")
    left = jnp.concatenate([own_ref[...], met_ref[...]], 0)
    first = lax.axis_index("core") == 0
    panel, sibling = panel_ref[...], sibling_ref[...]
    panels = jnp.concatenate(
        [jnp.where(first, panel, sibling), jnp.where(first, sibling, panel)], 0
    )
    outer_ref[...] = dot_t(panels, left)
    lane = lax.broadcasted_iota(jnp.int32, (8, 128), 1)
    low_half = lane < 64
    even = (lane // 32) % 2 == 0
    for o in range(2):
        for bh in range(8):
            for ih in range(4):
                v = [
                    outer_ref[pl.ds((o * 32 + bh * 4 + b) * 8, 8), pl.ds(ih * 128, 128)]
                    for b in range(4)
                ]
                for p in range(2):
                    a, c = v[p], v[p + 2]
                    v[p] = jnp.where(low_half, a, pltpu.roll(c, 64, 1))
                    v[p + 2] = jnp.where(low_half, pltpu.roll(a, 64, 1), c)
                for p in (0, 2):
                    a, c = v[p], v[p + 1]
                    v[p] = jnp.where(even, a, pltpu.roll(c, 32, 1))
                    v[p + 1] = jnp.where(even, pltpu.roll(a, 96, 1), c)
                for il in range(4):
                    i = ih % 2 * 4 + il
                    row = ih // 2 * 128 + turned_rows(i) * 16 + o * 8
                    flat_ref[pl.ds(row, 8), pl.ds(bh * 128, 128)] = v[il]
    pair = jnp.concatenate(
        [pair_ref[turned_rows(p), yh] for p in range(8)] + [met_pair_ref[...]], 0
    )
    mid = pair + dot_deep(flat_ref[...], w_outer_ref[...])
    normed = layer_norm(mid, -1)
    projected = dot_t(w_tri_ref[...], normed)
    for side in range(2):
        plain, gating = projected[side * 256 :][:128], projected[side * 256 + 128 :][:128]
        edge = sigmoid(gating) * plain
        for h in range(2):
            q = side * 2 + h
            own, met = edge[h * 64 : h * 64 + 64, :128], edge[h * 64 : h * 64 + 64, 128:]
            edges_ref[pl.ds(q * 2, 64, stride=8), :] = jnp.where(yh == 0, own, met)
            edges_ref[pl.ds(q * 2 + 1, 64, stride=8), :] = jnp.where(yh == 0, met, own)
    gate = sigmoid(dot_deep(normed, w_gate_ref[...]))
    kept_ref[0], kept_ref[1] = mid[:128], gate[:128]
    sent_ref[0], sent_ref[1] = mid[128:], gate[128:]


def turn_blocks(x, masks):
    x = pltpu.roll(x, 0, 1, stride=16, stride_axis=0)
    for bit, mask in zip((1, 2, 4), masks):
        x = jnp.where(mask, pltpu.roll(x, 8 - bit, 0), x)
    return pltpu.roll(x, 0, 1, stride=16, stride_axis=0)


def triangle_kernel(left_ref, right_ref, out_ref, l_ref, r_ref):
    core = lax.axis_index("core")
    lane = lax.broadcasted_iota(jnp.int32, (8, 128), 1)
    masks = [(lane // 16) & bit != 0 for bit in (1, 2, 4)]
    for h in range(2):
        for z in range(8):
            for y in range(2):
                x = left_ref[pl.ds(z * 64 + h * 2 + y, 8, stride=8), :]
                l_ref[pl.ds(y * 64 + z * 8, 8), :] = turn_blocks(x, masks)
                x = left_ref[pl.ds(z * 64 + (2 + h) * 2 + y, 8, stride=8), :]
                own = turn_blocks(x, masks)
                x = right_ref[pl.ds(z * 32 + h * 2 + y, 8, stride=4), :]
                other = turn_blocks(x, masks)
                row = y * 128 + turned_rows(z) * 16
                r_ref[pl.ds(row, 8), :] = jnp.where(core == 0, own, other)
                r_ref[pl.ds(row + 8, 8), :] = jnp.where(core == 0, other, own)
        mixed = dot_t(l_ref[...], r_ref[...])
        for z in range(8):
            for y in range(2):
                for half in range(2):
                    block = mixed[y * 64 + z * 8 :, half * 128 :][:8, :128]
                    out_ref[pl.ds((z * 2 + y) * 32 + h * 2 + half, 8, stride=4), :] = turn_blocks(
                        block, masks
                    )


def output_kernel(mixed_ref, kept_ref, met_ref, w_ref, out_ref):
    yh = lax.axis_index("yh")
    w = w_ref[...]
    for half in range(2):
        tiles = []
        for h in range(2):
            for z in range(8):
                parts = [
                    mixed_ref[pl.ds((z * 2 + y) * 32 + h * 2 + half, 8, stride=4), :]
                    for y in range(2)
                ]
                tiles.append(parts[0] + parts[1])
        update = dot_deep(layer_norm(jnp.concatenate(tiles, 0), 0).T, w)
        mid = jnp.where(yh == half, kept_ref[0], met_ref[0])
        gate = jnp.where(yh == half, kept_ref[1], met_ref[1])
        for i in range(8):
            p = turned_rows(i) * 16
            out_ref[i, half] = mid[p : p + 16] + gate[p : p + 16] * update[i * 16 : i * 16 + 16]


def call(kernel, out_shapes, scratch, *args, limit=VMEM_LIMIT):
    shapes = [jax.ShapeDtypeStruct(s, jnp.float32) for s in out_shapes]
    return pl.pallas_call(
        kernel,
        out_shape=shapes if len(shapes) > 1 else shapes[0],
        scratch_shapes=scratch,
        compiler_params=pltpu.CompilerParams(vmem_limit_bytes=limit),
    )(*args)


def vmem(*shape):
    return pltpu.VMEM(shape, jnp.float32)


def factors(homolog, first, second, pair):
    return call(
        factor_kernel, [(256, 128), (256, 128), (128, 128)], [vmem(1024, 128)],
        homolog, first, second, pair,
        limit=60 * 1024 * 1024,
    )


def pair_stage(own, met, met_pair, panel, sibling, pair, w_outer, w_tri, w_gate):
    return call(
        pair_kernel,
        [(512, 128), (2, 128, 128), (2, 128, 128)],
        [vmem(512, 512), vmem(256, 1024)],
        own, met, met_pair, panel, sibling, pair, w_outer, w_tri, w_gate,
    )


def triangle(left, right):
    return call(triangle_kernel, [(512, 128)], [vmem(128, 128), vmem(256, 128)], left, right)


def output_stage(mixed, kept, met, w_out):
    return call(output_kernel, [(8, 2, 16, 128)], [], mixed, kept, met, w_out)


def per_device(homolog, pair, w_first, w_second, w_outer, w_tri, w_gate, w_out):
    pair = pair.reshape(8, 2, 16, 128)
    left, right, half = factors(homolog, w_first.T, w_second.T, pair)
    swap = [(0, 1), (1, 0)]
    panel = lax.ppermute(right, ALL, panel_permutation())
    met = lax.ppermute(left, ("yh", "yl"), [(0, 3), (1, 2), (2, 1), (3, 0)])
    met_pair = lax.ppermute(half, "yh", swap)
    w_outer_ba = w_outer.reshape(32, 32, 128).transpose(1, 0, 2).reshape(1024, 128)
    sibling = lax.ppermute(panel, "core", swap)
    edges, kept, sent = pair_stage(
        left, met, met_pair, panel, sibling, pair, w_outer_ba, w_tri.T, w_gate
    )
    swapped = lax.all_to_all(edges.reshape(64, 8, 128), LAYER, 0, 0, tiled=True)
    returned = lax.ppermute(sent, "yh", swap)
    rights = lax.ppermute(swapped[:, 4:], "core", swap)
    back = triangle(swapped.reshape(512, 128), rights.reshape(256, 128))
    mixed = lax.all_to_all(back.reshape(128, 4, 128), CHIPS, 0, 0, tiled=True)
    return output_stage(mixed.reshape(512, 128), kept, returned, w_out).reshape(8, 32, 128)


def solution(mesh):
    fine = Mesh(mesh.devices.reshape(8, 2, 2, 4, 2), ALL)
    placed = (P(None, ROW, None), P(ROW, COL, None), P(), P(), P(), P(), P(), P())
    return jax.shard_map(
        per_device, mesh=fine, in_specs=placed, out_specs=P(ROW, COL, None), check_vma=False
    )
```

```python
import jax
import jax.numpy as jnp
from jax import lax
from jax.experimental import pallas as pl
from jax.experimental.pallas import tpu as pltpu
from jax.sharding import Mesh, PartitionSpec as P

epsilon = 1e-05

ALL = ("z", "yh", "core", "x", "yl")
ROW = ("z", "yh", "core")
COL = ("x", "yl")
LAYER = ("z", "x", "yl")
CHIPS = ("z", "yh", "x", "yl")
VMEM_LIMIT = 32 * 1024 * 1024


PANEL_COLUMNS = (
    (72361054, 54671032, 53160427, 1764253, 74562031, 25647103, 76045231, 5476312),
    (61053247, 45671032, 30176425, 62347501, 34205176, 50761342, 42635701, 4276513),
)


def panel_permutation():
    pairs = []
    for z in range(8):
        for yh in range(2):
            for core in range(2):
                for c in range(8):
                    column = PANEL_COLUMNS[yh][c] // 10 ** (7 - z) % 10
                    source = ((c * 2 + yh) * 2 + core) * 8 + column
                    pairs.append((source, ((z * 2 + yh) * 2 + core) * 8 + c))
    return pairs


def mm(a, b):
    return jnp.dot(a, b, preferred_element_type=jnp.float32)


def mm_t(a, b):
    return lax.dot_general(a, b, (((1,), (1,)), ((), ())), preferred_element_type=jnp.float32)


def split(x):
    high = x.astype(jnp.bfloat16)
    return high, (x - high.astype(jnp.float32)).astype(jnp.bfloat16)


def dot_deep(a, b):
    a_high, a_low = split(a)
    b_high, b_low = split(b)
    both = mm(a_high, jnp.concatenate([b_high, b_low], 1))
    return both[:, :128] + both[:, 128:] + mm(a_low, b_high)


def dot_t(a, b):
    a_high, a_low = split(a)
    b_high, b_low = split(b)
    shared = mm_t(jnp.concatenate([a_high, a_low], 1), jnp.concatenate([b_high, b_high], 1))
    return shared + mm_t(a_high, b_low)


def layer_norm(values, axis):
    average = jnp.mean(values, axis, keepdims=True)
    centred = values - average
    variance = jnp.mean(centred * centred, axis, keepdims=True)
    return centred * lax.rsqrt(variance + epsilon)


def sigmoid(x):
    return 1.0 / (1.0 + jnp.exp(-x))


def turned_rows(p):
    return (8 - p) % 8


def factor_kernel(
    msa_ref, first_ref, second_ref, pair_ref, left_ref, right_ref, half_ref, result
):
    other = 1 - lax.axis_index("yh")
    w_high, w_low = split(jnp.concatenate([first_ref[...], second_ref[...]], 0))
    w_both = jnp.concatenate([w_high, w_low], 0)
    w_rest = jnp.concatenate([w_high, jnp.zeros_like(w_high)], 0)
    for k in range(4):
        n_high, n_low = split(layer_norm(msa_ref[pl.ds(k * 32, 32)].reshape(256, 256), -1))
        result[pl.ds(k * 256, 256), :] = mm_t(n_high, w_both) + mm_t(n_low, w_rest)
    for i in range(8):
        turned = result[pl.ds(i, 128, stride=8), :].T
        both = turned[:64] + turned[64:]
        left_ref[pl.ds(i * 32, 32), :] = both[:32] * (1.0 / 128.0)
        right_ref[pl.ds(i, 32, stride=8), :] = both[32:]
    for p in range(8):
        half_ref[pl.ds(p * 16, 16), :] = pair_ref[turned_rows(p), other]


def pair_kernel(
    own_ref, met_ref, met_pair_ref, panel_ref, sibling_ref, pair_ref, w_outer_ref, w_tri_ref, w_gate_ref,
    edges_ref, kept_ref, sent_ref, outer_ref, flat_ref,
):
    yh = lax.axis_index("yh")
    left = jnp.concatenate([own_ref[...], met_ref[...]], 0)
    first = lax.axis_index("core") == 0
    panel, sibling = panel_ref[...], sibling_ref[...]
    panels = jnp.concatenate(
        [jnp.where(first, panel, sibling), jnp.where(first, sibling, panel)], 0
    )
    outer_ref[...] = dot_t(panels, left)
    lane = lax.broadcasted_iota(jnp.int32, (8, 128), 1)
    low_half = lane < 64
    even = (lane // 32) % 2 == 0
    for o in range(2):
        for bh in range(8):
            for ih in range(4):
                v = [
                    outer_ref[pl.ds((o * 32 + bh * 4 + b) * 8, 8), pl.ds(ih * 128, 128)]
                    for b in range(4)
                ]
                for p in range(2):
                    a, c = v[p], v[p + 2]
                    v[p] = jnp.where(low_half, a, pltpu.roll(c, 64, 1))
                    v[p + 2] = jnp.where(low_half, pltpu.roll(a, 64, 1), c)
                for p in (0, 2):
                    a, c = v[p], v[p + 1]
                    v[p] = jnp.where(even, a, pltpu.roll(c, 32, 1))
                    v[p + 1] = jnp.where(even, pltpu.roll(a, 96, 1), c)
                for il in range(4):
                    i = ih % 2 * 4 + il
                    row = ih // 2 * 128 + turned_rows(i) * 16 + o * 8
                    flat_ref[pl.ds(row, 8), pl.ds(bh * 128, 128)] = v[il]
    pair = jnp.concatenate(
        [pair_ref[turned_rows(p), yh] for p in range(8)] + [met_pair_ref[...]], 0
    )
    mid = pair + dot_deep(flat_ref[...], w_outer_ref[...])
    normed = layer_norm(mid, -1)
    projected = dot_t(w_tri_ref[...], normed)
    for side in range(2):
        plain, gating = projected[side * 256 :][:128], projected[side * 256 + 128 :][:128]
        edge = sigmoid(gating) * plain
        for h in range(2):
            q = side * 2 + h
            own, met = edge[h * 64 : h * 64 + 64, :128], edge[h * 64 : h * 64 + 64, 128:]
            edges_ref[pl.ds(q * 2, 64, stride=8), :] = jnp.where(yh == 0, own, met)
            edges_ref[pl.ds(q * 2 + 1, 64, stride=8), :] = jnp.where(yh == 0, met, own)
    gate = sigmoid(dot_deep(normed, w_gate_ref[...]))
    kept_ref[0], kept_ref[1] = mid[:128], gate[:128]
    sent_ref[0], sent_ref[1] = mid[128:], gate[128:]


def turn_blocks(x, masks):
    x = pltpu.roll(x, 0, 1, stride=16, stride_axis=0)
    for bit, mask in zip((1, 2, 4), masks):
        x = jnp.where(mask, pltpu.roll(x, 8 - bit, 0), x)
    return pltpu.roll(x, 0, 1, stride=16, stride_axis=0)


def triangle_kernel(left_ref, right_ref, out_ref, l_ref, r_ref):
    core = lax.axis_index("core")
    lane = lax.broadcasted_iota(jnp.int32, (8, 128), 1)
    masks = [(lane // 16) & bit != 0 for bit in (1, 2, 4)]
    for h in range(2):
        for z in range(8):
            for y in range(2):
                x = left_ref[pl.ds(z * 64 + h * 2 + y, 8, stride=8), :]
                l_ref[pl.ds(y * 64 + z * 8, 8), :] = turn_blocks(x, masks)
                x = left_ref[pl.ds(z * 64 + (2 + h) * 2 + y, 8, stride=8), :]
                own = turn_blocks(x, masks)
                x = right_ref[pl.ds(z * 32 + h * 2 + y, 8, stride=4), :]
                other = turn_blocks(x, masks)
                row = y * 128 + turned_rows(z) * 16
                r_ref[pl.ds(row, 8), :] = jnp.where(core == 0, own, other)
                r_ref[pl.ds(row + 8, 8), :] = jnp.where(core == 0, other, own)
        mixed = dot_t(l_ref[...], r_ref[...])
        for z in range(8):
            for y in range(2):
                for half in range(2):
                    block = mixed[y * 64 + z * 8 :, half * 128 :][:8, :128]
                    out_ref[pl.ds((z * 2 + y) * 32 + h * 2 + half, 8, stride=4), :] = turn_blocks(
                        block, masks
                    )


def output_kernel(mixed_ref, kept_ref, met_ref, w_ref, out_ref):
    yh = lax.axis_index("yh")
    w = w_ref[...]
    for half in range(2):
        tiles = []
        for h in range(2):
            for z in range(8):
                parts = [
                    mixed_ref[pl.ds((z * 2 + y) * 32 + h * 2 + half, 8, stride=4), :]
                    for y in range(2)
                ]
                tiles.append(parts[0] + parts[1])
        update = dot_deep(layer_norm(jnp.concatenate(tiles, 0), 0).T, w)
        mid = jnp.where(yh == half, kept_ref[0], met_ref[0])
        gate = jnp.where(yh == half, kept_ref[1], met_ref[1])
        for i in range(8):
            p = turned_rows(i) * 16
            out_ref[i, half] = mid[p : p + 16] + gate[p : p + 16] * update[i * 16 : i * 16 + 16]


def call(kernel, out_shapes, scratch, *args, limit=VMEM_LIMIT):
    shapes = [jax.ShapeDtypeStruct(s, jnp.float32) for s in out_shapes]
    return pl.pallas_call(
        kernel,
        out_shape=shapes if len(shapes) > 1 else shapes[0],
        scratch_shapes=scratch,
        compiler_params=pltpu.CompilerParams(vmem_limit_bytes=limit),
    )(*args)


def vmem(*shape):
    return pltpu.VMEM(shape, jnp.float32)


def factors(homolog, first, second, pair):
    return call(
        factor_kernel, [(256, 128), (256, 128), (128, 128)], [vmem(1024, 128)],
        homolog, first, second, pair,
        limit=60 * 1024 * 1024,
    )


def pair_stage(own, met, met_pair, panel, sibling, pair, w_outer, w_tri, w_gate):
    return call(
        pair_kernel,
        [(512, 128), (2, 128, 128), (2, 128, 128)],
        [vmem(512, 512), vmem(256, 1024)],
        own, met, met_pair, panel, sibling, pair, w_outer, w_tri, w_gate,
    )


def triangle(left, right):
    return call(triangle_kernel, [(512, 128)], [vmem(128, 128), vmem(256, 128)], left, right)


def output_stage(mixed, kept, met, w_out):
    return call(output_kernel, [(8, 2, 16, 128)], [], mixed, kept, met, w_out)


def per_device(homolog, pair, w_first, w_second, w_outer, w_tri, w_gate, w_out):
    pair = pair.reshape(8, 2, 16, 128)
    left, right, half = factors(homolog, w_first.T, w_second.T, pair)
    swap = [(0, 1), (1, 0)]
    panel = lax.ppermute(right, ALL, panel_permutation())
    met = lax.ppermute(left, ("yh", "yl"), [(0, 3), (1, 2), (2, 1), (3, 0)])
    met_pair = lax.ppermute(half, "yh", swap)
    w_outer_ba = w_outer.reshape(32, 32, 128).transpose(1, 0, 2).reshape(1024, 128)
    panel, met_pair = lax.optimization_barrier((panel, met_pair))
    sibling = lax.ppermute(panel, "core", swap)
    edges, kept, sent = pair_stage(
        left, met, met_pair, panel, sibling, pair, w_outer_ba, w_tri.T, w_gate
    )
    swapped = lax.all_to_all(edges.reshape(64, 8, 128), LAYER, 0, 0, tiled=True)
    returned = lax.ppermute(sent, "yh", swap)
    rights = lax.ppermute(swapped[:, 4:], "core", swap)
    back = triangle(swapped.reshape(512, 128), rights.reshape(256, 128))
    mixed = lax.all_to_all(back.reshape(128, 4, 128), CHIPS, 0, 0, tiled=True)
    return output_stage(mixed.reshape(512, 128), kept, returned, w_out).reshape(8, 32, 128)


def solution(mesh):
    fine = Mesh(mesh.devices.reshape(8, 2, 2, 4, 2), ALL)
    placed = (P(None, ROW, None), P(ROW, COL, None), P(), P(), P(), P(), P(), P())
    return jax.shard_map(
        per_device, mesh=fine, in_specs=placed, out_specs=P(ROW, COL, None), check_vma=False
    )
```

```python
import jax
import jax.numpy as jnp
from jax import lax
from jax.experimental import pallas as pl
from jax.experimental.pallas import tpu as pltpu
from jax.sharding import Mesh, PartitionSpec as P

epsilon = 1e-05

ALL = ("z", "yh", "core", "x", "yl")
ROW = ("z", "yh", "core")
COL = ("x", "yl")
LAYER = ("z", "x", "yl")
CHIPS = ("z", "yh", "x", "yl")
VMEM_LIMIT = 32 * 1024 * 1024


PANEL_COLUMNS = (
    (72361054, 54671032, 53160427, 1764253, 74562031, 25647103, 76045231, 5476312),
    (61053247, 45671032, 30176425, 62347501, 34205176, 50761342, 42635701, 4276513),
)


def panel_permutation():
    pairs = []
    for z in range(8):
        for yh in range(2):
            for core in range(2):
                for c in range(8):
                    column = PANEL_COLUMNS[yh][c] // 10 ** (7 - z) % 10
                    source = ((c * 2 + yh) * 2 + core) * 8 + column
                    pairs.append((source, ((z * 2 + yh) * 2 + core) * 8 + c))
    return pairs


def mm(a, b):
    return jnp.dot(a, b, preferred_element_type=jnp.float32)


def mm_t(a, b):
    return lax.dot_general(a, b, (((1,), (1,)), ((), ())), preferred_element_type=jnp.float32)


def split(x):
    high = x.astype(jnp.bfloat16)
    return high, (x - high.astype(jnp.float32)).astype(jnp.bfloat16)


def halves(x):
    return jnp.concatenate(split(x), 1)


def dot_deep(a, b):
    a_high, a_low = split(a)
    both = mm(a_high, b)
    return both[:, :128] + both[:, 128:] + mm(a_low, b[:, :128])


def dot_t(a, b):
    b_high, b_low = split(b)
    return mm_t(a, jnp.concatenate([b_high, b_high], 1)) + mm_t(a[:, :128], b_low)


def layer_norm(values, axis):
    average = jnp.mean(values, axis, keepdims=True)
    centred = values - average
    variance = jnp.mean(centred * centred, axis, keepdims=True)
    return centred * lax.rsqrt(variance + epsilon)


def sigmoid(x):
    return 1.0 / (1.0 + jnp.exp(-x))


def turned_rows(p):
    return (8 - p) % 8


def factor_kernel(
    msa_ref, first_ref, second_ref, pair_ref, left_ref, right_ref, half_ref, result
):
    other = 1 - lax.axis_index("yh")
    w_high, w_low = split(jnp.concatenate([first_ref[...], second_ref[...]], 0))
    w_both = jnp.concatenate([w_high, w_low], 0)
    w_rest = jnp.concatenate([w_high, jnp.zeros_like(w_high)], 0)
    for k in range(4):
        n_high, n_low = split(layer_norm(msa_ref[pl.ds(k * 32, 32)].reshape(256, 256), -1))
        result[pl.ds(k * 256, 256), :] = mm_t(n_high, w_both) + mm_t(n_low, w_rest)
    for i in range(8):
        turned = result[pl.ds(i, 128, stride=8), :].T
        both = turned[:64] + turned[64:]
        left_ref[pl.ds(i * 32, 32), :] = both[:32] * (1.0 / 128.0)
        right_ref[pl.ds(i, 32, stride=8), :] = both[32:]
    for p in range(8):
        half_ref[pl.ds(p * 16, 16), :] = pair_ref[turned_rows(p), other]


def weight_kernel(w_outer_ref, w_tri_ref, outer_ref, tri_ref):
    for b in range(32):
        outer_ref[pl.ds(b * 32, 32), :] = halves(w_outer_ref[pl.ds(b, 32, stride=32), :])
    tri_ref[...] = halves(w_tri_ref[...])


def gate_kernel(kept_ref, met_ref, w_ref, out_ref):
    w = halves(w_ref[...])
    for at, ref in enumerate((kept_ref, met_ref)):
        out_ref[at] = sigmoid(dot_deep(layer_norm(ref[...], -1), w))


def pair_kernel(
    own_ref, met_ref, met_pair_ref, panel_ref, sibling_ref, pair_ref, w_outer_ref, w_tri_ref,
    edges_ref, kept_ref, sent_ref, outer_ref, flat_ref,
):
    yh = lax.axis_index("yh")
    left = jnp.concatenate([own_ref[...], met_ref[...]], 0)
    first = lax.axis_index("core") == 0
    panel, sibling = panel_ref[...], sibling_ref[...]
    panels = jnp.concatenate(
        [jnp.where(first, panel, sibling), jnp.where(first, sibling, panel)], 0
    )
    outer_ref[...] = dot_t(halves(panels), left)
    lane = lax.broadcasted_iota(jnp.int32, (8, 128), 1)
    low_half = lane < 64
    even = (lane // 32) % 2 == 0
    for o in range(2):
        for bh in range(8):
            for ih in range(4):
                v = [
                    outer_ref[pl.ds((o * 32 + bh * 4 + b) * 8, 8), pl.ds(ih * 128, 128)]
                    for b in range(4)
                ]
                for p in range(2):
                    a, c = v[p], v[p + 2]
                    v[p] = jnp.where(low_half, a, pltpu.roll(c, 64, 1))
                    v[p + 2] = jnp.where(low_half, pltpu.roll(a, 64, 1), c)
                for p in (0, 2):
                    a, c = v[p], v[p + 1]
                    v[p] = jnp.where(even, a, pltpu.roll(c, 32, 1))
                    v[p + 1] = jnp.where(even, pltpu.roll(a, 96, 1), c)
                for il in range(4):
                    i = ih % 2 * 4 + il
                    row = ih // 2 * 128 + turned_rows(i) * 16 + o * 8
                    flat_ref[pl.ds(row, 8), pl.ds(bh * 128, 128)] = v[il]
    pair = jnp.concatenate(
        [pair_ref[turned_rows(p), yh] for p in range(8)] + [met_pair_ref[...]], 0
    )
    mid = pair + dot_deep(flat_ref[...], w_outer_ref[...])
    normed = layer_norm(mid, -1)
    projected = dot_t(w_tri_ref[...], normed)
    for side in range(2):
        plain, gating = projected[side * 256 :][:128], projected[side * 256 + 128 :][:128]
        edge = sigmoid(gating) * plain
        for h in range(2):
            q = side * 2 + h
            own, met = edge[h * 64 : h * 64 + 64, :128], edge[h * 64 : h * 64 + 64, 128:]
            edges_ref[pl.ds(q * 2, 64, stride=8), :] = jnp.where(yh == 0, own, met)
            edges_ref[pl.ds(q * 2 + 1, 64, stride=8), :] = jnp.where(yh == 0, met, own)
    kept_ref[...] = mid[:128]
    sent_ref[...] = mid[128:]


def turn_blocks(x, masks):
    x = pltpu.roll(x, 0, 1, stride=16, stride_axis=0)
    for bit, mask in zip((1, 2, 4), masks):
        x = jnp.where(mask, pltpu.roll(x, 8 - bit, 0), x)
    return pltpu.roll(x, 0, 1, stride=16, stride_axis=0)


def triangle_kernel(left_ref, right_ref, out_ref, l_ref, r_ref):
    core = lax.axis_index("core")
    lane = lax.broadcasted_iota(jnp.int32, (8, 128), 1)
    masks = [(lane // 16) & bit != 0 for bit in (1, 2, 4)]
    for h in range(2):
        for z in range(8):
            for y in range(2):
                x = left_ref[pl.ds(z * 64 + h * 2 + y, 8, stride=8), :]
                l_ref[pl.ds(y * 64 + z * 8, 8), :] = turn_blocks(x, masks)
                x = left_ref[pl.ds(z * 64 + (2 + h) * 2 + y, 8, stride=8), :]
                own = turn_blocks(x, masks)
                x = right_ref[pl.ds(z * 32 + h * 2 + y, 8, stride=4), :]
                other = turn_blocks(x, masks)
                row = y * 128 + turned_rows(z) * 16
                r_ref[pl.ds(row, 8), :] = jnp.where(core == 0, own, other)
                r_ref[pl.ds(row + 8, 8), :] = jnp.where(core == 0, other, own)
        mixed = dot_t(halves(l_ref[...]), r_ref[...])
        for z in range(8):
            for y in range(2):
                for half in range(2):
                    block = mixed[y * 64 + z * 8 :, half * 128 :][:8, :128]
                    out_ref[pl.ds((z * 2 + y) * 32 + h * 2 + half, 8, stride=4), :] = turn_blocks(
                        block, masks
                    )


def output_kernel(mixed_ref, kept_ref, met_ref, gates_ref, w_ref, out_ref):
    yh = lax.axis_index("yh")
    w = halves(w_ref[...])
    for half in range(2):
        tiles = []
        for h in range(2):
            for z in range(8):
                parts = [
                    mixed_ref[pl.ds((z * 2 + y) * 32 + h * 2 + half, 8, stride=4), :]
                    for y in range(2)
                ]
                tiles.append(parts[0] + parts[1])
        update = dot_deep(layer_norm(jnp.concatenate(tiles, 0), 0).T, w)
        mid = jnp.where(yh == half, kept_ref[...], met_ref[...])
        gate = jnp.where(yh == half, gates_ref[0], gates_ref[1])
        for i in range(8):
            p = turned_rows(i) * 16
            out_ref[i, half] = mid[p : p + 16] + gate[p : p + 16] * update[i * 16 : i * 16 + 16]


def call(kernel, out_shapes, scratch, *args, limit=VMEM_LIMIT, kind=jnp.float32):
    shapes = [jax.ShapeDtypeStruct(s, kind) for s in out_shapes]
    return pl.pallas_call(
        kernel,
        out_shape=shapes if len(shapes) > 1 else shapes[0],
        scratch_shapes=scratch,
        compiler_params=pltpu.CompilerParams(vmem_limit_bytes=limit),
    )(*args)


def vmem(*shape):
    return pltpu.VMEM(shape, jnp.float32)


def factors(homolog, first, second, pair):
    return call(
        factor_kernel, [(256, 128), (256, 128), (128, 128)], [vmem(1024, 128)],
        homolog, first, second, pair,
        limit=60 * 1024 * 1024,
    )


def pair_stage(*args):
    return call(
        pair_kernel,
        [(512, 128), (128, 128), (128, 128)],
        [vmem(512, 512), vmem(256, 1024)],
        *args,
    )


def triangle(left, right):
    return call(triangle_kernel, [(512, 128)], [vmem(128, 128), vmem(256, 128)], left, right)


def output_stage(mixed, kept, met, gates, w_out):
    return call(output_kernel, [(8, 2, 16, 128)], [], mixed, kept, met, gates, w_out)


def gates_of(kept, met, w_gate):
    return call(gate_kernel, [(2, 128, 128)], [], kept, met, w_gate)


def prepared(w_outer, w_tri):
    return call(weight_kernel, [(1024, 256), (512, 256)], [], w_outer, w_tri, kind=jnp.bfloat16)


def per_device(homolog, pair, w_first, w_second, w_outer, w_tri, w_gate, w_out):
    pair = pair.reshape(8, 2, 16, 128)
    left, right, half = factors(homolog, w_first.T, w_second.T, pair)
    swap = [(0, 1), (1, 0)]
    panel = lax.ppermute(right, ALL, panel_permutation())
    met = lax.ppermute(left, ("yh", "yl"), [(0, 3), (1, 2), (2, 1), (3, 0)])
    met_pair = lax.ppermute(half, "yh", swap)
    weights = prepared(w_outer, w_tri.T)
    panel, met_pair = lax.optimization_barrier((panel, met_pair))
    sibling = lax.ppermute(panel, "core", swap)
    edges, kept, sent = pair_stage(
        left, met, met_pair, panel, sibling, pair, *weights
    )
    swapped = lax.all_to_all(edges.reshape(64, 8, 128), LAYER, 0, 0, tiled=True)
    returned = lax.ppermute(sent, "yh", swap)
    rights = lax.ppermute(swapped[:, 4:], "core", swap)
    back = triangle(swapped.reshape(512, 128), rights.reshape(256, 128))
    mixed = lax.all_to_all(back.reshape(128, 4, 128), CHIPS, 0, 0, tiled=True)
    gates = gates_of(kept, returned, w_gate)
    return output_stage(mixed.reshape(512, 128), kept, returned, gates, w_out).reshape(8, 32, 128)


def solution(mesh):
    fine = Mesh(mesh.devices.reshape(8, 2, 2, 4, 2), ALL)
    placed = (P(None, ROW, None), P(ROW, COL, None), P(), P(), P(), P(), P(), P())
    return jax.shard_map(
        per_device, mesh=fine, in_specs=placed, out_specs=P(ROW, COL, None), check_vma=False
    )
```

```python
import jax
import jax.numpy as jnp
from jax import lax
from jax.experimental import pallas as pl
from jax.experimental.pallas import tpu as pltpu
from jax.sharding import Mesh, PartitionSpec as P

epsilon = 1e-05

ALL = ("z", "yh", "core", "x", "yl")
ROW = ("z", "yh", "core")
COL = ("x", "yl")
LAYER = ("x", "yl", "z")
CHIPS = ("x", "yl", "z", "yh")
VMEM_LIMIT = 32 * 1024 * 1024


PANEL_COLUMNS = (
    (72361054, 54671032, 53160427, 1764253, 74562031, 25647103, 76045231, 5476312),
    (61053247, 45671032, 30176425, 62347501, 34205176, 50761342, 42635701, 4276513),
)


def panel_permutation():
    pairs = []
    for z in range(8):
        for yh in range(2):
            for core in range(2):
                for c in range(8):
                    column = PANEL_COLUMNS[yh][c] // 10 ** (7 - z) % 10
                    source = ((c * 2 + yh) * 2 + core) * 8 + column
                    pairs.append((source, ((z * 2 + yh) * 2 + core) * 8 + c))
    return pairs


def mm(a, b):
    return jnp.dot(a, b, preferred_element_type=jnp.float32)


def mm_t(a, b):
    return lax.dot_general(a, b, (((1,), (1,)), ((), ())), preferred_element_type=jnp.float32)


def split(x):
    high = x.astype(jnp.bfloat16)
    return high, (x - high.astype(jnp.float32)).astype(jnp.bfloat16)


def halves(x):
    return jnp.concatenate(split(x), 1)


def dot_deep(a, b):
    a_high, a_low = split(a)
    both = mm(a_high, b)
    return both[:, :128] + both[:, 128:] + mm(a_low, b[:, :128])


def dot_t(a, b):
    b_high, b_low = split(b)
    return mm_t(a, jnp.concatenate([b_high, b_high], 1)) + mm_t(a[:, :128], b_low)


def layer_norm(values, axis):
    average = jnp.mean(values, axis, keepdims=True)
    centred = values - average
    variance = jnp.mean(centred * centred, axis, keepdims=True)
    return centred * lax.rsqrt(variance + epsilon)


def sigmoid(x):
    return 1.0 / (1.0 + jnp.exp(-x))


def turned_rows(p):
    return (8 - p) % 8


def factor_kernel(
    msa_ref, first_ref, second_ref, pair_ref, left_ref, right_ref, half_ref, result
):
    other = 1 - lax.axis_index("yh")
    w_high, w_low = split(jnp.concatenate([first_ref[...], second_ref[...]], 0))
    w_both = jnp.concatenate([w_high, w_low], 0)
    w_rest = jnp.concatenate([w_high, jnp.zeros_like(w_high)], 0)
    for k in range(4):
        n_high, n_low = split(layer_norm(msa_ref[pl.ds(k * 32, 32)].reshape(256, 256), -1))
        result[pl.ds(k * 256, 256), :] = mm_t(n_high, w_both) + mm_t(n_low, w_rest)
    for i in range(8):
        turned = result[pl.ds(i, 128, stride=8), :].T
        both = turned[:64] + turned[64:]
        left_ref[pl.ds(i * 32, 32), :] = both[:32] * (1.0 / 128.0)
        right_ref[pl.ds(i, 32, stride=8), :] = both[32:]
    for p in range(8):
        half_ref[pl.ds(p * 16, 16), :] = pair_ref[turned_rows(p), other]


def weight_kernel(w_outer_ref, w_tri_ref, outer_ref, tri_ref):
    for b in range(32):
        outer_ref[pl.ds(b * 32, 32), :] = halves(w_outer_ref[pl.ds(b, 32, stride=32), :])
    tri_ref[...] = halves(w_tri_ref[...])


def gate_kernel(kept_ref, met_ref, w_ref, out_ref):
    w = halves(w_ref[...])
    for at, ref in enumerate((kept_ref, met_ref)):
        out_ref[at] = sigmoid(dot_deep(layer_norm(ref[...], -1), w))


def pair_kernel(
    own_ref, met_ref, met_pair_ref, panel_ref, sibling_ref, pair_ref, w_outer_ref, w_tri_ref,
    edges_ref, kept_ref, sent_ref, outer_ref, flat_ref,
):
    yh = lax.axis_index("yh")
    left = jnp.concatenate([own_ref[...], met_ref[...]], 0)
    first = lax.axis_index("core") == 0
    panel, sibling = panel_ref[...], sibling_ref[...]
    panels = jnp.concatenate(
        [jnp.where(first, panel, sibling), jnp.where(first, sibling, panel)], 0
    )
    outer_ref[...] = dot_t(halves(panels), left)
    lane = lax.broadcasted_iota(jnp.int32, (8, 128), 1)
    low_half = lane < 64
    even = (lane // 32) % 2 == 0
    for o in range(2):
        for bh in range(8):
            for ih in range(4):
                v = [
                    outer_ref[pl.ds((o * 32 + bh * 4 + b) * 8, 8), pl.ds(ih * 128, 128)]
                    for b in range(4)
                ]
                for p in range(2):
                    a, c = v[p], v[p + 2]
                    v[p] = jnp.where(low_half, a, pltpu.roll(c, 64, 1))
                    v[p + 2] = jnp.where(low_half, pltpu.roll(a, 64, 1), c)
                for p in (0, 2):
                    a, c = v[p], v[p + 1]
                    v[p] = jnp.where(even, a, pltpu.roll(c, 32, 1))
                    v[p + 1] = jnp.where(even, pltpu.roll(a, 96, 1), c)
                for il in range(4):
                    i = ih % 2 * 4 + il
                    row = ih // 2 * 128 + turned_rows(i) * 16 + o * 8
                    flat_ref[pl.ds(row, 8), pl.ds(bh * 128, 128)] = v[il]
    pair = jnp.concatenate(
        [pair_ref[turned_rows(p), yh] for p in range(8)] + [met_pair_ref[...]], 0
    )
    mid = pair + dot_deep(flat_ref[...], w_outer_ref[...])
    normed = layer_norm(mid, -1)
    projected = dot_t(w_tri_ref[...], normed)
    for side in range(2):
        plain, gating = projected[side * 256 :][:128], projected[side * 256 + 128 :][:128]
        edge = sigmoid(gating) * plain
        for h in range(2):
            q = side * 2 + h
            own, met = edge[h * 64 : h * 64 + 64, :128], edge[h * 64 : h * 64 + 64, 128:]
            edges_ref[pl.ds(q * 2, 64, stride=8), :] = jnp.where(yh == 0, own, met)
            edges_ref[pl.ds(q * 2 + 1, 64, stride=8), :] = jnp.where(yh == 0, met, own)
    kept_ref[...] = mid[:128]
    sent_ref[...] = mid[128:]


def turn_blocks(x, masks):
    x = pltpu.roll(x, 0, 1, stride=16, stride_axis=0)
    for bit, mask in zip((1, 2, 4), masks):
        x = jnp.where(mask, pltpu.roll(x, 8 - bit, 0), x)
    return pltpu.roll(x, 0, 1, stride=16, stride_axis=0)


def triangle_kernel(left_ref, right_ref, out_ref, l_ref, r_ref):
    core = lax.axis_index("core")
    lane = lax.broadcasted_iota(jnp.int32, (8, 128), 1)
    masks = [(lane // 16) & bit != 0 for bit in (1, 2, 4)]
    for h in range(2):
        for z in range(8):
            for y in range(2):
                x = left_ref[pl.ds(z * 8 + h * 2 + y, 8, stride=64), :]
                l_ref[pl.ds(y * 64 + z * 8, 8), :] = turn_blocks(x, masks)
                x = left_ref[pl.ds(z * 8 + (2 + h) * 2 + y, 8, stride=64), :]
                own = turn_blocks(x, masks)
                x = right_ref[pl.ds(z * 4 + h * 2 + y, 8, stride=32), :]
                other = turn_blocks(x, masks)
                row = y * 128 + turned_rows(z) * 16
                r_ref[pl.ds(row, 8), :] = jnp.where(core == 0, own, other)
                r_ref[pl.ds(row + 8, 8), :] = jnp.where(core == 0, other, own)
        mixed = dot_t(halves(l_ref[...]), r_ref[...])
        for z in range(8):
            for y in range(2):
                for half in range(2):
                    block = mixed[y * 64 + z * 8 :, half * 128 :][:8, :128]
                    out_ref[pl.ds((z * 2 + y) * 4 + h * 2 + half, 8, stride=64), :] = turn_blocks(
                        block, masks
                    )


def output_kernel(mixed_ref, kept_ref, met_ref, gates_ref, w_ref, out_ref):
    yh = lax.axis_index("yh")
    w = halves(w_ref[...])
    for half in range(2):
        tiles = []
        for h in range(2):
            for c in range(8):
                parts = [
                    mixed_ref[pl.ds(c * 64 + y * 4 + h * 2 + half, 8, stride=8), :]
                    for y in range(2)
                ]
                tiles.append(parts[0] + parts[1])
        update = dot_deep(layer_norm(jnp.concatenate(tiles, 0), 0).T, w)
        mid = jnp.where(yh == half, kept_ref[...], met_ref[...])
        gate = jnp.where(yh == half, gates_ref[0], gates_ref[1])
        for i in range(8):
            p = turned_rows(i) * 16
            out_ref[i, half] = mid[p : p + 16] + gate[p : p + 16] * update[i * 16 : i * 16 + 16]


def call(kernel, out_shapes, scratch, *args, limit=VMEM_LIMIT, kind=jnp.float32):
    shapes = [jax.ShapeDtypeStruct(s, kind) for s in out_shapes]
    return pl.pallas_call(
        kernel,
        out_shape=shapes if len(shapes) > 1 else shapes[0],
        scratch_shapes=scratch,
        compiler_params=pltpu.CompilerParams(vmem_limit_bytes=limit),
    )(*args)


def vmem(*shape):
    return pltpu.VMEM(shape, jnp.float32)


def factors(homolog, first, second, pair):
    return call(
        factor_kernel, [(256, 128), (256, 128), (128, 128)], [vmem(1024, 128)],
        homolog, first, second, pair,
        limit=60 * 1024 * 1024,
    )


def pair_stage(*args):
    return call(
        pair_kernel,
        [(512, 128), (128, 128), (128, 128)],
        [vmem(512, 512), vmem(256, 1024)],
        *args,
    )


def triangle(left, right):
    return call(triangle_kernel, [(512, 128)], [vmem(128, 128), vmem(256, 128)], left, right)


def output_stage(mixed, kept, met, gates, w_out):
    return call(output_kernel, [(8, 2, 16, 128)], [], mixed, kept, met, gates, w_out)


def gates_of(kept, met, w_gate):
    return call(gate_kernel, [(2, 128, 128)], [], kept, met, w_gate)


def prepared(w_outer, w_tri):
    return call(weight_kernel, [(1024, 256), (512, 256)], [], w_outer, w_tri, kind=jnp.bfloat16)


def per_device(homolog, pair, w_first, w_second, w_outer, w_tri, w_gate, w_out):
    pair = pair.reshape(8, 2, 16, 128)
    left, right, half = factors(homolog, w_first.T, w_second.T, pair)
    swap = [(0, 1), (1, 0)]
    panel = lax.ppermute(right, ALL, panel_permutation())
    met = lax.ppermute(left, ("yh", "yl"), [(0, 3), (1, 2), (2, 1), (3, 0)])
    met_pair = lax.ppermute(half, "yh", swap)
    weights = prepared(w_outer, w_tri.T)
    panel, met_pair = lax.optimization_barrier((panel, met_pair))
    sibling = lax.ppermute(panel, "core", swap)
    edges, kept, sent = pair_stage(
        left, met, met_pair, panel, sibling, pair, *weights
    )
    swapped = lax.all_to_all(edges.reshape(64, 8, 128), LAYER, 0, 0, tiled=True)
    returned = lax.ppermute(sent, "yh", swap)
    rights = lax.ppermute(swapped[:, 4:], "core", swap)
    back = triangle(swapped.reshape(512, 128), rights.reshape(256, 128))
    mixed = lax.all_to_all(back.reshape(128, 4, 128), CHIPS, 0, 0, tiled=True)
    gates = gates_of(kept, returned, w_gate)
    return output_stage(mixed.reshape(512, 128), kept, returned, gates, w_out).reshape(8, 32, 128)


def solution(mesh):
    fine = Mesh(mesh.devices.reshape(8, 2, 2, 4, 2), ALL)
    placed = (P(None, ROW, None), P(ROW, COL, None), P(), P(), P(), P(), P(), P())
    return jax.shard_map(
        per_device, mesh=fine, in_specs=placed, out_specs=P(ROW, COL, None), check_vma=False
    )
```

```python
import jax
import jax.numpy as jnp
from jax import lax
from jax.experimental import pallas as pl
from jax.experimental.pallas import tpu as pltpu
from jax.sharding import Mesh, PartitionSpec as P

epsilon = 1e-05

ALL = ("z", "yh", "core", "x", "yl")
ROW = ("z", "yh", "core")
COL = ("x", "yl")
LAYER = ("x", "yl", "z")
CHIPS = ("x", "yl", "z", "yh")
VMEM_LIMIT = 32 * 1024 * 1024


PANEL_COLUMNS = (
    (72361054, 54671032, 53160427, 1764253, 74562031, 25647103, 76045231, 5476312),
    (61053247, 45671032, 30176425, 62347501, 34205176, 50761342, 42635701, 4276513),
)


def panel_permutation():
    pairs = []
    for z in range(8):
        for yh in range(2):
            for core in range(2):
                for c in range(8):
                    column = PANEL_COLUMNS[yh][c] // 10 ** (7 - z) % 10
                    source = ((c * 2 + yh) * 2 + core) * 8 + column
                    pairs.append((source, ((z * 2 + yh) * 2 + core) * 8 + c))
    return pairs


def mm(a, b):
    return jnp.dot(a, b, preferred_element_type=jnp.float32)


def mm_t(a, b):
    return lax.dot_general(a, b, (((1,), (1,)), ((), ())), preferred_element_type=jnp.float32)


def split(x):
    high = x.astype(jnp.bfloat16)
    return high, (x - high.astype(jnp.float32)).astype(jnp.bfloat16)


def halves(x):
    return jnp.concatenate(split(x), 1)


def dot_deep(a, b):
    a_high, a_low = split(a)
    both = mm(a_high, b)
    return both[:, :128] + both[:, 128:] + mm(a_low, b[:, :128])


def dot_t(a, b):
    b_high, b_low = split(b)
    return mm_t(a, jnp.concatenate([b_high, b_high], 1)) + mm_t(a[:, :128], b_low)


def layer_norm(values, axis):
    average = jnp.mean(values, axis, keepdims=True)
    centred = values - average
    variance = jnp.mean(centred * centred, axis, keepdims=True)
    return centred * lax.rsqrt(variance + epsilon)


def sigmoid(x):
    return 1.0 / (1.0 + jnp.exp(-x))


def turned_rows(p):
    return (8 - p) % 8


def factor_kernel(
    msa_ref, first_ref, second_ref, pair_ref, left_ref, right_ref, half_ref, result
):
    other = 1 - lax.axis_index("yh")
    w_high, w_low = split(jnp.concatenate([first_ref[...], second_ref[...]], 0))
    w_both = jnp.concatenate([w_high, w_low], 0)
    w_rest = jnp.concatenate([w_high, jnp.zeros_like(w_high)], 0)
    for k in range(4):
        n_high, n_low = split(layer_norm(msa_ref[pl.ds(k * 32, 32)].reshape(256, 256), -1))
        result[pl.ds(k * 256, 256), :] = mm_t(n_high, w_both) + mm_t(n_low, w_rest)
    for i in range(8):
        turned = result[pl.ds(i, 128, stride=8), :].T
        both = turned[:64] + turned[64:]
        left_ref[pl.ds(i * 32, 32), :] = both[:32] * (1.0 / 128.0)
        right_ref[pl.ds(i, 32, stride=8), :] = both[32:]
    for p in range(8):
        half_ref[pl.ds(p * 16, 16), :] = pair_ref[turned_rows(p), other]


def weight_kernel(w_outer_ref, w_tri_ref, outer_ref, tri_ref):
    for b in range(32):
        outer_ref[pl.ds(b * 32, 32), :] = halves(w_outer_ref[pl.ds(b, 32, stride=32), :])
    tri_ref[...] = halves(w_tri_ref[...])


def pair_kernel(
    own_ref, met_ref, met_pair_ref, panel_ref, sibling_ref, pair_ref, w_outer_ref, w_tri_ref,
    edges_ref, kept_ref, sent_ref, outer_ref, flat_ref,
):
    yh = lax.axis_index("yh")
    left = jnp.concatenate([own_ref[...], met_ref[...]], 0)
    first = lax.axis_index("core") == 0
    panel, sibling = panel_ref[...], sibling_ref[...]
    panels = jnp.concatenate(
        [jnp.where(first, panel, sibling), jnp.where(first, sibling, panel)], 0
    )
    outer_ref[...] = dot_t(halves(panels), left)
    lane = lax.broadcasted_iota(jnp.int32, (8, 128), 1)
    low_half = lane < 64
    even = (lane // 32) % 2 == 0
    for o in range(2):
        for bh in range(8):
            for ih in range(4):
                v = [
                    outer_ref[pl.ds((o * 32 + bh * 4 + b) * 8, 8), pl.ds(ih * 128, 128)]
                    for b in range(4)
                ]
                for p in range(2):
                    a, c = v[p], v[p + 2]
                    v[p] = jnp.where(low_half, a, pltpu.roll(c, 64, 1))
                    v[p + 2] = jnp.where(low_half, pltpu.roll(a, 64, 1), c)
                for p in (0, 2):
                    a, c = v[p], v[p + 1]
                    v[p] = jnp.where(even, a, pltpu.roll(c, 32, 1))
                    v[p + 1] = jnp.where(even, pltpu.roll(a, 96, 1), c)
                for il in range(4):
                    i = ih % 2 * 4 + il
                    row = ih // 2 * 128 + turned_rows(i) * 16 + o * 8
                    flat_ref[pl.ds(row, 8), pl.ds(bh * 128, 128)] = v[il]
    pair = jnp.concatenate(
        [pair_ref[turned_rows(p), yh] for p in range(8)] + [met_pair_ref[...]], 0
    )
    mid = pair + dot_deep(flat_ref[...], w_outer_ref[...])
    normed = layer_norm(mid, -1)
    projected = dot_t(w_tri_ref[...], normed)
    for side in range(2):
        plain, gating = projected[side * 256 :][:128], projected[side * 256 + 128 :][:128]
        edge = sigmoid(gating) * plain
        for h in range(2):
            q = side * 2 + h
            own, met = edge[h * 64 : h * 64 + 64, :128], edge[h * 64 : h * 64 + 64, 128:]
            edges_ref[pl.ds(q * 2, 64, stride=8), :] = jnp.where(yh == 0, own, met)
            edges_ref[pl.ds(q * 2 + 1, 64, stride=8), :] = jnp.where(yh == 0, met, own)
    kept_ref[...] = mid[:128]
    sent_ref[...] = mid[128:]


def turn_blocks(x, masks):
    x = pltpu.roll(x, 0, 1, stride=16, stride_axis=0)
    for bit, mask in zip((1, 2, 4), masks):
        x = jnp.where(mask, pltpu.roll(x, 8 - bit, 0), x)
    return pltpu.roll(x, 0, 1, stride=16, stride_axis=0)


def triangle_kernel(left_ref, right_ref, out_ref, l_ref, r_ref):
    core = lax.axis_index("core")
    lane = lax.broadcasted_iota(jnp.int32, (8, 128), 1)
    masks = [(lane // 16) & bit != 0 for bit in (1, 2, 4)]
    for h in range(2):
        for z in range(8):
            for y in range(2):
                x = left_ref[pl.ds(z * 8 + h * 2 + y, 8, stride=64), :]
                l_ref[pl.ds(y * 64 + z * 8, 8), :] = turn_blocks(x, masks)
                x = left_ref[pl.ds(z * 8 + (2 + h) * 2 + y, 8, stride=64), :]
                own = turn_blocks(x, masks)
                x = right_ref[pl.ds(z * 4 + h * 2 + y, 8, stride=32), :]
                other = turn_blocks(x, masks)
                row = y * 128 + turned_rows(z) * 16
                r_ref[pl.ds(row, 8), :] = jnp.where(core == 0, own, other)
                r_ref[pl.ds(row + 8, 8), :] = jnp.where(core == 0, other, own)
        mixed = dot_t(halves(l_ref[...]), r_ref[...])
        for z in range(8):
            for y in range(2):
                for half in range(2):
                    block = mixed[y * 64 + z * 8 :, half * 128 :][:8, :128]
                    out_ref[pl.ds((z * 2 + y) * 4 + h * 2 + half, 8, stride=64), :] = turn_blocks(
                        block, masks
                    )


def output_kernel(mixed_ref, kept_ref, met_ref, w_gate_ref, w_ref, out_ref):
    yh = lax.axis_index("yh")
    w, w_gate = halves(w_ref[...]), halves(w_gate_ref[...])
    for half in range(2):
        tiles = []
        for h in range(2):
            for c in range(8):
                parts = [
                    mixed_ref[pl.ds(c * 64 + y * 4 + h * 2 + half, 8, stride=8), :]
                    for y in range(2)
                ]
                tiles.append(parts[0] + parts[1])
        update = dot_deep(layer_norm(jnp.concatenate(tiles, 0), 0).T, w)
        mid = jnp.where(yh == half, kept_ref[...], met_ref[...])
        gate = sigmoid(dot_deep(layer_norm(mid, -1), w_gate))
        for i in range(8):
            p = turned_rows(i) * 16
            out_ref[i, half] = mid[p : p + 16] + gate[p : p + 16] * update[i * 16 : i * 16 + 16]


def call(kernel, out_shapes, scratch, *args, limit=VMEM_LIMIT, kind=jnp.float32):
    shapes = [jax.ShapeDtypeStruct(s, kind) for s in out_shapes]
    return pl.pallas_call(
        kernel,
        out_shape=shapes if len(shapes) > 1 else shapes[0],
        scratch_shapes=scratch,
        compiler_params=pltpu.CompilerParams(vmem_limit_bytes=limit),
    )(*args)


def vmem(*shape):
    return pltpu.VMEM(shape, jnp.float32)


def factors(homolog, first, second, pair):
    return call(
        factor_kernel, [(256, 128), (256, 128), (128, 128)], [vmem(1024, 128)],
        homolog, first, second, pair,
        limit=60 * 1024 * 1024,
    )


def pair_stage(*args):
    return call(
        pair_kernel,
        [(512, 128), (128, 128), (128, 128)],
        [vmem(512, 512), vmem(256, 1024)],
        *args,
    )


def triangle(left, right):
    return call(triangle_kernel, [(512, 128)], [vmem(128, 128), vmem(256, 128)], left, right)


def output_stage(*args):
    return call(output_kernel, [(8, 2, 16, 128)], [], *args)


def prepared(w_outer, w_tri):
    return call(weight_kernel, [(1024, 256), (512, 256)], [], w_outer, w_tri, kind=jnp.bfloat16)


def per_device(homolog, pair, w_first, w_second, w_outer, w_tri, w_gate, w_out):
    pair = pair.reshape(8, 2, 16, 128)
    left, right, half = factors(homolog, w_first.T, w_second.T, pair)
    swap = [(0, 1), (1, 0)]
    panel = lax.ppermute(right, ALL, panel_permutation())
    met = lax.ppermute(left, ("yh", "yl"), [(0, 3), (1, 2), (2, 1), (3, 0)])
    met_pair = lax.ppermute(half, "yh", swap)
    weights = prepared(w_outer, w_tri.T)
    panel, met_pair = lax.optimization_barrier((panel, met_pair))
    sibling = lax.ppermute(panel, "core", swap)
    edges, kept, sent = pair_stage(
        left, met, met_pair, panel, sibling, pair, *weights
    )
    swapped = lax.all_to_all(edges.reshape(64, 8, 128), LAYER, 0, 0, tiled=True)
    sent, swapped = lax.optimization_barrier((sent, swapped))
    rights = lax.ppermute(swapped[:, 4:], "core", swap)
    returned = lax.ppermute(sent, "yh", swap)
    back = triangle(swapped.reshape(512, 128), rights.reshape(256, 128))
    back, returned = lax.optimization_barrier((back, returned))
    mixed = lax.all_to_all(back.reshape(128, 4, 128), CHIPS, 0, 0, tiled=True)
    out = output_stage(mixed.reshape(512, 128), kept, returned, w_gate, w_out)
    return out.reshape(8, 32, 128)


def solution(mesh):
    fine = Mesh(mesh.devices.reshape(8, 2, 2, 4, 2), ALL)
    placed = (P(None, ROW, None), P(ROW, COL, None), P(), P(), P(), P(), P(), P())
    return jax.shard_map(
        per_device, mesh=fine, in_specs=placed, out_specs=P(ROW, COL, None), check_vma=False
    )
```

```python
import jax
import jax.numpy as jnp
from jax import lax
from jax.experimental import pallas as pl
from jax.experimental.pallas import tpu as pltpu
from jax.sharding import Mesh, PartitionSpec as P

epsilon = 1e-05

ALL = ("z", "yh", "core", "x", "yl")
ROW = ("z", "yh", "core")
COL = ("x", "yl")
LAYER = ("z", "x", "yl")
CHIPS = ("z", "yh", "x", "yl")
VMEM_LIMIT = 32 * 1024 * 1024


PANEL_COLUMNS = (
    (
        (47531062, 7463125, 12675430, 67140253, 74126350, 60453721, 3265714, 23074165),
        (13652047, 14520376, 43051627, 42673015, 30546172, 25017436, 47162053, 14732506),
    ),
    (
        (74520136, 54763120, 71653042, 76402153, 74210356, 20456137, 3574216, 12067543),
        (61732045, 13256074, 36025714, 7241635, 34765012, 21350467, 24137605, 73150246),
    ),
)


def panel_permutation():
    pairs = []
    for z in range(8):
        for yh in range(2):
            for core in range(2):
                for c in range(8):
                    column = PANEL_COLUMNS[yh][core][c] // 10 ** (7 - z) % 10
                    source = ((c * 2 + yh) * 2 + core) * 8 + column
                    pairs.append((source, ((z * 2 + yh) * 2 + core) * 8 + c))
    return pairs


def mm(a, b):
    return jnp.dot(a, b, preferred_element_type=jnp.float32)


def mm_t(a, b):
    return lax.dot_general(a, b, (((1,), (1,)), ((), ())), preferred_element_type=jnp.float32)


def split(x):
    high = x.astype(jnp.bfloat16)
    return high, (x - high.astype(jnp.float32)).astype(jnp.bfloat16)


def halves(x):
    return jnp.concatenate(split(x), 1)


def dot_deep(a, b):
    a_high, a_low = split(a)
    both = mm(a_high, b)
    return both[:, :128] + both[:, 128:] + mm(a_low, b[:, :128])


def dot_t(a, b):
    b_high, b_low = split(b)
    return mm_t(a, jnp.concatenate([b_high, b_high], 1)) + mm_t(a[:, :128], b_low)


def layer_norm(values, axis):
    average = jnp.mean(values, axis, keepdims=True)
    centred = values - average
    variance = jnp.mean(centred * centred, axis, keepdims=True)
    return centred * lax.rsqrt(variance + epsilon)


def sigmoid(x):
    return 1.0 / (1.0 + jnp.exp(-x))


def turned_rows(p):
    return (8 - p) % 8


def factor_kernel(
    msa_ref, first_ref, second_ref, pair_ref, left_ref, right_ref, half_ref, result
):
    other = 1 - lax.axis_index("yh")
    w_high, w_low = split(jnp.concatenate([first_ref[...], second_ref[...]], 0))
    w_both = jnp.concatenate([w_high, w_low], 0)
    w_rest = jnp.concatenate([w_high, jnp.zeros_like(w_high)], 0)
    for k in range(4):
        n_high, n_low = split(layer_norm(msa_ref[pl.ds(k * 32, 32)].reshape(256, 256), -1))
        result[pl.ds(k * 256, 256), :] = mm_t(n_high, w_both) + mm_t(n_low, w_rest)
    for i in range(8):
        turned = result[pl.ds(i, 128, stride=8), :].T
        both = turned[:64] + turned[64:]
        left_ref[pl.ds(i * 32, 32), :] = both[:32] * (1.0 / 128.0)
        right_ref[pl.ds(i, 32, stride=8), :] = both[32:]
    for p in range(8):
        half_ref[pl.ds(p * 16, 16), :] = pair_ref[turned_rows(p), other]


def weight_kernel(w_outer_ref, w_tri_ref, outer_ref, tri_ref):
    for b in range(32):
        outer_ref[pl.ds(b * 32, 32), :] = halves(w_outer_ref[pl.ds(b, 32, stride=32), :])
    tri_ref[...] = halves(w_tri_ref[...])


def gate_kernel(kept_ref, met_ref, w_ref, out_ref):
    w = halves(w_ref[...])
    for at, ref in enumerate((kept_ref, met_ref)):
        out_ref[at] = sigmoid(dot_deep(layer_norm(ref[...], -1), w))


def pair_kernel(
    own_ref, met_ref, met_pair_ref, panel_ref, sibling_ref, pair_ref, w_outer_ref, w_tri_ref,
    edges_ref, kept_ref, sent_ref, outer_ref, flat_ref,
):
    yh = lax.axis_index("yh")
    left = jnp.concatenate([own_ref[...], met_ref[...]], 0)
    first = lax.axis_index("core") == 0
    panel, sibling = panel_ref[...], sibling_ref[...]
    panels = jnp.concatenate(
        [jnp.where(first, panel, sibling), jnp.where(first, sibling, panel)], 0
    )
    outer_ref[...] = dot_t(halves(panels), left)
    lane = lax.broadcasted_iota(jnp.int32, (8, 128), 1)
    low_half = lane < 64
    even = (lane // 32) % 2 == 0
    for o in range(2):
        for bh in range(8):
            for ih in range(4):
                v = [
                    outer_ref[pl.ds((o * 32 + bh * 4 + b) * 8, 8), pl.ds(ih * 128, 128)]
                    for b in range(4)
                ]
                for p in range(2):
                    a, c = v[p], v[p + 2]
                    v[p] = jnp.where(low_half, a, pltpu.roll(c, 64, 1))
                    v[p + 2] = jnp.where(low_half, pltpu.roll(a, 64, 1), c)
                for p in (0, 2):
                    a, c = v[p], v[p + 1]
                    v[p] = jnp.where(even, a, pltpu.roll(c, 32, 1))
                    v[p + 1] = jnp.where(even, pltpu.roll(a, 96, 1), c)
                for il in range(4):
                    i = ih % 2 * 4 + il
                    row = ih // 2 * 128 + turned_rows(i) * 16 + o * 8
                    flat_ref[pl.ds(row, 8), pl.ds(bh * 128, 128)] = v[il]
    pair = jnp.concatenate(
        [pair_ref[turned_rows(p), yh] for p in range(8)] + [met_pair_ref[...]], 0
    )
    mid = pair + dot_deep(flat_ref[...], w_outer_ref[...])
    normed = layer_norm(mid, -1)
    projected = dot_t(w_tri_ref[...], normed)
    for side in range(2):
        plain, gating = projected[side * 256 :][:128], projected[side * 256 + 128 :][:128]
        edge = sigmoid(gating) * plain
        for h in range(2):
            q = side * 2 + h
            own, met = edge[h * 64 : h * 64 + 64, :128], edge[h * 64 : h * 64 + 64, 128:]
            edges_ref[pl.ds(q * 2, 64, stride=8), :] = jnp.where(yh == 0, own, met)
            edges_ref[pl.ds(q * 2 + 1, 64, stride=8), :] = jnp.where(yh == 0, met, own)
    kept_ref[...] = mid[:128]
    sent_ref[...] = mid[128:]


def turn_blocks(x, masks):
    x = pltpu.roll(x, 0, 1, stride=16, stride_axis=0)
    for bit, mask in zip((1, 2, 4), masks):
        x = jnp.where(mask, pltpu.roll(x, 8 - bit, 0), x)
    return pltpu.roll(x, 0, 1, stride=16, stride_axis=0)


def triangle_kernel(left_ref, right_ref, out_ref, l_ref, r_ref):
    core = lax.axis_index("core")
    lane = lax.broadcasted_iota(jnp.int32, (8, 128), 1)
    masks = [(lane // 16) & bit != 0 for bit in (1, 2, 4)]
    for h in range(2):
        for z in range(8):
            for y in range(2):
                x = left_ref[pl.ds(z * 64 + h * 2 + y, 8, stride=8), :]
                l_ref[pl.ds(y * 64 + z * 8, 8), :] = turn_blocks(x, masks)
                x = left_ref[pl.ds(z * 64 + (2 + h) * 2 + y, 8, stride=8), :]
                own = turn_blocks(x, masks)
                x = right_ref[pl.ds(z * 32 + h * 2 + y, 8, stride=4), :]
                other = turn_blocks(x, masks)
                row = y * 128 + turned_rows(z) * 16
                r_ref[pl.ds(row, 8), :] = jnp.where(core == 0, own, other)
                r_ref[pl.ds(row + 8, 8), :] = jnp.where(core == 0, other, own)
        mixed = dot_t(halves(l_ref[...]), r_ref[...])
        for z in range(8):
            for y in range(2):
                for half in range(2):
                    block = mixed[y * 64 + z * 8 :, half * 128 :][:8, :128]
                    out_ref[pl.ds((z * 2 + y) * 32 + h * 2 + half, 8, stride=4), :] = turn_blocks(
                        block, masks
                    )


def output_kernel(mixed_ref, kept_ref, met_ref, gates_ref, w_ref, out_ref):
    yh = lax.axis_index("yh")
    w = halves(w_ref[...])
    for half in range(2):
        tiles = []
        for h in range(2):
            for z in range(8):
                parts = [
                    mixed_ref[pl.ds((z * 2 + y) * 32 + h * 2 + half, 8, stride=4), :]
                    for y in range(2)
                ]
                tiles.append(parts[0] + parts[1])
        update = dot_deep(layer_norm(jnp.concatenate(tiles, 0), 0).T, w)
        mid = jnp.where(yh == half, kept_ref[...], met_ref[...])
        gate = jnp.where(yh == half, gates_ref[0], gates_ref[1])
        for i in range(8):
            p = turned_rows(i) * 16
            out_ref[i, half] = mid[p : p + 16] + gate[p : p + 16] * update[i * 16 : i * 16 + 16]


def call(kernel, out_shapes, scratch, *args, limit=VMEM_LIMIT, kind=jnp.float32):
    shapes = [jax.ShapeDtypeStruct(s, kind) for s in out_shapes]
    return pl.pallas_call(
        kernel,
        out_shape=shapes if len(shapes) > 1 else shapes[0],
        scratch_shapes=scratch,
        compiler_params=pltpu.CompilerParams(vmem_limit_bytes=limit),
    )(*args)


def vmem(*shape):
    return pltpu.VMEM(shape, jnp.float32)


def factors(homolog, first, second, pair):
    return call(
        factor_kernel, [(256, 128), (256, 128), (128, 128)], [vmem(1024, 128)],
        homolog, first, second, pair,
        limit=60 * 1024 * 1024,
    )


def pair_stage(*args):
    return call(
        pair_kernel,
        [(512, 128), (128, 128), (128, 128)],
        [vmem(512, 512), vmem(256, 1024)],
        *args,
    )


def triangle(left, right):
    return call(triangle_kernel, [(512, 128)], [vmem(128, 128), vmem(256, 128)], left, right)


def output_stage(mixed, kept, met, gates, w_out):
    return call(output_kernel, [(8, 2, 16, 128)], [], mixed, kept, met, gates, w_out)


def gates_of(kept, met, w_gate):
    return call(gate_kernel, [(2, 128, 128)], [], kept, met, w_gate)


def prepared(w_outer, w_tri):
    return call(weight_kernel, [(1024, 256), (512, 256)], [], w_outer, w_tri, kind=jnp.bfloat16)


def per_device(homolog, pair, w_first, w_second, w_outer, w_tri, w_gate, w_out):
    pair = pair.reshape(8, 2, 16, 128)
    left, right, half = factors(homolog, w_first.T, w_second.T, pair)
    swap = [(0, 1), (1, 0)]
    panel = lax.ppermute(right, ALL, panel_permutation())
    met = lax.ppermute(left, ("yh", "yl"), [(0, 3), (1, 2), (2, 1), (3, 0)])
    met_pair = lax.ppermute(half, "yh", swap)
    weights = prepared(w_outer, w_tri.T)
    panel, met_pair = lax.optimization_barrier((panel, met_pair))
    sibling = lax.ppermute(panel, "core", swap)
    edges, kept, sent = pair_stage(
        left, met, met_pair, panel, sibling, pair, *weights
    )
    swapped = lax.all_to_all(edges.reshape(64, 8, 128), LAYER, 0, 0, tiled=True)
    returned = lax.ppermute(sent, "yh", swap)
    rights = lax.ppermute(swapped[:, 4:], "core", swap)
    back = triangle(swapped.reshape(512, 128), rights.reshape(256, 128))
    mixed = lax.all_to_all(back.reshape(128, 4, 128), CHIPS, 0, 0, tiled=True)
    gates = gates_of(kept, returned, w_gate)
    return output_stage(mixed.reshape(512, 128), kept, returned, gates, w_out).reshape(8, 32, 128)


def solution(mesh):
    fine = Mesh(mesh.devices.reshape(8, 2, 2, 4, 2), ALL)
    placed = (P(None, ROW, None), P(ROW, COL, None), P(), P(), P(), P(), P(), P())
    return jax.shard_map(
        per_device, mesh=fine, in_specs=placed, out_specs=P(ROW, COL, None), check_vma=False
    )
```

```python
import jax
import jax.numpy as jnp
from jax import lax
from jax.experimental import pallas as pl
from jax.experimental.pallas import tpu as pltpu
from jax.sharding import Mesh, PartitionSpec as P

epsilon = 1e-05

ALL = ("z", "yh", "core", "x", "yl")
ROW = ("z", "yh", "core")
COL = ("x", "yl")
LAYER = ("z", "x", "yl")
CHIPS = ("z", "yh", "x", "yl")
VMEM_LIMIT = 32 * 1024 * 1024


PANEL_COLUMNS = (
    (
        (47531062, 7463125, 12675430, 67140253, 74126350, 60453721, 3265714, 23074165),
        (13652047, 14520376, 43051627, 42673015, 30546172, 25017436, 47162053, 14732506),
    ),
    (
        (74520136, 54763120, 71653042, 76402153, 74210356, 20456137, 3574216, 12067543),
        (61732045, 13256074, 36025714, 7241635, 34765012, 21350467, 24137605, 73150246),
    ),
)


def panel_permutation():
    pairs = []
    for z in range(8):
        for yh in range(2):
            for core in range(2):
                for c in range(8):
                    column = PANEL_COLUMNS[yh][core][c] // 10 ** (7 - z) % 10
                    source = ((c * 2 + yh) * 2 + core) * 8 + column
                    pairs.append((source, ((z * 2 + yh) * 2 + core) * 8 + c))
    return pairs


def mm(a, b):
    return jnp.dot(a, b, preferred_element_type=jnp.float32)


def mm_t(a, b):
    return lax.dot_general(a, b, (((1,), (1,)), ((), ())), preferred_element_type=jnp.float32)


def split(x):
    high = x.astype(jnp.bfloat16)
    return high, (x - high.astype(jnp.float32)).astype(jnp.bfloat16)


def halves(x):
    return jnp.concatenate(split(x), 1)


def dot_deep(a, b):
    a_high, a_low = split(a)
    both = mm(a_high, b)
    return both[:, :128] + both[:, 128:] + mm(a_low, b[:, :128])


def dot_t(a, b):
    b_high, b_low = split(b)
    return mm_t(a, jnp.concatenate([b_high, b_high], 1)) + mm_t(a[:, :128], b_low)


def layer_norm(values, axis):
    average = jnp.mean(values, axis, keepdims=True)
    centred = values - average
    variance = jnp.mean(centred * centred, axis, keepdims=True)
    return centred * lax.rsqrt(variance + epsilon)


def sigmoid(x):
    return 1.0 / (1.0 + jnp.exp(-x))


def turned_rows(p):
    return (8 - p) % 8


def factor_kernel(
    msa_ref, first_ref, second_ref, pair_ref, left_ref, right_ref, half_ref, result
):
    other = 1 - lax.axis_index("yh")
    w_high, w_low = split(jnp.concatenate([first_ref[...], second_ref[...]], 0))
    w_both = jnp.concatenate([w_high, w_low], 0)
    w_rest = jnp.concatenate([w_high, jnp.zeros_like(w_high)], 0)
    for k in range(4):
        n_high, n_low = split(layer_norm(msa_ref[pl.ds(k * 32, 32)].reshape(256, 256), -1))
        result[pl.ds(k * 256, 256), :] = mm_t(n_high, w_both) + mm_t(n_low, w_rest)
    for i in range(8):
        turned = result[pl.ds(i, 128, stride=8), :].T
        both = turned[:64] + turned[64:]
        left_ref[pl.ds(i * 32, 32), :] = both[:32] * (1.0 / 128.0)
        right_ref[pl.ds(i, 32, stride=8), :] = both[32:]
    for p in range(8):
        half_ref[pl.ds(p * 16, 16), :] = pair_ref[turned_rows(p), other]


def weight_kernel(w_outer_ref, w_tri_ref, outer_ref, tri_ref):
    for b in range(32):
        outer_ref[pl.ds(b * 32, 32), :] = halves(w_outer_ref[pl.ds(b, 32, stride=32), :])
    tri_ref[...] = halves(w_tri_ref[...])


def gate_kernel(kept_ref, met_ref, w_ref, out_ref):
    w = halves(w_ref[...])
    for at, ref in enumerate((kept_ref, met_ref)):
        out_ref[at] = sigmoid(dot_deep(layer_norm(ref[...], -1), w))


def project_block(left, panel, w_outer, outer_ref, flat_ref):
    outer_ref[...] = dot_t(halves(panel), left)
    lane = lax.broadcasted_iota(jnp.int32, (8, 128), 1)
    low_half = lane < 64
    even = (lane // 32) % 2 == 0
    for bh in range(8):
        for ih in range(4):
            v = [
                outer_ref[pl.ds((bh * 4 + b) * 8, 8), pl.ds(ih * 128, 128)] for b in range(4)
            ]
            for p in range(2):
                a, c = v[p], v[p + 2]
                v[p] = jnp.where(low_half, a, pltpu.roll(c, 64, 1))
                v[p + 2] = jnp.where(low_half, pltpu.roll(a, 64, 1), c)
            for p in (0, 2):
                a, c = v[p], v[p + 1]
                v[p] = jnp.where(even, a, pltpu.roll(c, 32, 1))
                v[p + 1] = jnp.where(even, pltpu.roll(a, 96, 1), c)
            for il in range(4):
                row = ih // 2 * 64 + turned_rows(ih % 2 * 4 + il) * 8
                flat_ref[pl.ds(row, 8), pl.ds(bh * 128, 128)] = v[il]
    return dot_deep(flat_ref[...], w_outer)


def block_kernel(own_ref, met_ref, panel_ref, w_outer_ref, update_ref, outer_ref, flat_ref):
    left = jnp.concatenate([own_ref[...], met_ref[...]], 0)
    update_ref[...] = project_block(left, panel_ref[...], w_outer_ref[...], outer_ref, flat_ref)


def pair_kernel(
    own_ref, met_ref, met_pair_ref, sibling_ref, update_ref, pair_ref, w_outer_ref, w_tri_ref,
    edges_ref, kept_ref, sent_ref, outer_ref, flat_ref,
):
    yh = lax.axis_index("yh")
    first = lax.axis_index("core") == 0
    left = jnp.concatenate([own_ref[...], met_ref[...]], 0)
    other = project_block(left, sibling_ref[...], w_outer_ref[...], outer_ref, flat_ref)
    mine = update_ref[...]
    blocks = jnp.where(first, mine, other), jnp.where(first, other, mine)
    update = [block[t * 8 : t * 8 + 8] for t in range(16) for block in blocks]
    pair = jnp.concatenate(
        [pair_ref[turned_rows(p), yh] for p in range(8)] + [met_pair_ref[...]], 0
    )
    mid = pair + jnp.concatenate(update, 0)
    normed = layer_norm(mid, -1)
    projected = dot_t(w_tri_ref[...], normed)
    for side in range(2):
        plain, gating = projected[side * 256 :][:128], projected[side * 256 + 128 :][:128]
        edge = sigmoid(gating) * plain
        for h in range(2):
            q = side * 2 + h
            own, met = edge[h * 64 : h * 64 + 64, :128], edge[h * 64 : h * 64 + 64, 128:]
            edges_ref[pl.ds(q * 2, 64, stride=8), :] = jnp.where(yh == 0, own, met)
            edges_ref[pl.ds(q * 2 + 1, 64, stride=8), :] = jnp.where(yh == 0, met, own)
    kept_ref[...] = mid[:128]
    sent_ref[...] = mid[128:]


def turn_blocks(x, masks):
    x = pltpu.roll(x, 0, 1, stride=16, stride_axis=0)
    for bit, mask in zip((1, 2, 4), masks):
        x = jnp.where(mask, pltpu.roll(x, 8 - bit, 0), x)
    return pltpu.roll(x, 0, 1, stride=16, stride_axis=0)


def block_masks():
    lane = lax.broadcasted_iota(jnp.int32, (8, 128), 1)
    return [(lane // 16) & bit != 0 for bit in (1, 2, 4)]


def own_kernel(edges_ref, l_ref, r_ref):
    masks = block_masks()
    for h in range(2):
        for z in range(8):
            for y in range(2):
                x = edges_ref[pl.ds(z * 64 + h * 2 + y, 8, stride=8), :]
                l_ref[h, pl.ds(y * 64 + z * 8, 8), :] = turn_blocks(x, masks)
                x = edges_ref[pl.ds(z * 64 + (2 + h) * 2 + y, 8, stride=8), :]
                r_ref[h, pl.ds(y * 64 + turned_rows(z) * 8, 8), :] = turn_blocks(x, masks)


def triangle_kernel(l_ref, own_ref, right_ref, out_ref, r_ref):
    masks = block_masks()
    first = lax.axis_index("core") == 0
    for h in range(2):
        for z in range(8):
            for y in range(2):
                x = right_ref[pl.ds(z * 32 + h * 2 + y, 8, stride=4), :]
                other = turn_blocks(x, masks)
                at = y * 64 + turned_rows(z) * 8
                own = own_ref[h, pl.ds(at, 8), :]
                r_ref[pl.ds(at * 2, 8), :] = jnp.where(first, own, other)
                r_ref[pl.ds(at * 2 + 8, 8), :] = jnp.where(first, other, own)
        mixed = dot_t(halves(l_ref[h]), r_ref[...])
        for z in range(8):
            for y in range(2):
                for half in range(2):
                    block = mixed[y * 64 + z * 8 :, half * 128 :][:8, :128]
                    out_ref[pl.ds((z * 2 + y) * 32 + h * 2 + half, 8, stride=4), :] = turn_blocks(
                        block, masks
                    )


def output_kernel(mixed_ref, kept_ref, met_ref, gates_ref, w_ref, out_ref):
    yh = lax.axis_index("yh")
    w = halves(w_ref[...])
    for half in range(2):
        tiles = []
        for h in range(2):
            for z in range(8):
                parts = [
                    mixed_ref[pl.ds((z * 2 + y) * 32 + h * 2 + half, 8, stride=4), :]
                    for y in range(2)
                ]
                tiles.append(parts[0] + parts[1])
        update = dot_deep(layer_norm(jnp.concatenate(tiles, 0), 0).T, w)
        mid = jnp.where(yh == half, kept_ref[...], met_ref[...])
        gate = jnp.where(yh == half, gates_ref[0], gates_ref[1])
        for i in range(8):
            p = turned_rows(i) * 16
            out_ref[i, half] = mid[p : p + 16] + gate[p : p + 16] * update[i * 16 : i * 16 + 16]


def call(kernel, out_shapes, scratch, *args, limit=VMEM_LIMIT, kind=jnp.float32):
    shapes = [jax.ShapeDtypeStruct(s, kind) for s in out_shapes]
    return pl.pallas_call(
        kernel,
        out_shape=shapes if len(shapes) > 1 else shapes[0],
        scratch_shapes=scratch,
        compiler_params=pltpu.CompilerParams(vmem_limit_bytes=limit),
    )(*args)


def vmem(*shape):
    return pltpu.VMEM(shape, jnp.float32)


def factors(homolog, first, second, pair):
    return call(
        factor_kernel, [(256, 128), (256, 128), (128, 128)], [vmem(1024, 128)],
        homolog, first, second, pair,
        limit=60 * 1024 * 1024,
    )


def block_update(*args):
    return call(block_kernel, [(128, 128)], [vmem(256, 512), vmem(128, 1024)], *args)


def pair_stage(*args):
    return call(
        pair_kernel,
        [(512, 128), (128, 128), (128, 128)],
        [vmem(256, 512), vmem(128, 1024)],
        *args,
    )


def own_edges(edges):
    return call(own_kernel, [(2, 128, 128), (2, 128, 128)], [], edges)


def triangle(*args):
    return call(triangle_kernel, [(512, 128)], [vmem(256, 128)], *args)


def output_stage(mixed, kept, met, gates, w_out):
    return call(output_kernel, [(8, 2, 16, 128)], [], mixed, kept, met, gates, w_out)


def gates_of(kept, met, w_gate):
    return call(gate_kernel, [(2, 128, 128)], [], kept, met, w_gate)


def prepared(w_outer, w_tri):
    return call(weight_kernel, [(1024, 256), (512, 256)], [], w_outer, w_tri, kind=jnp.bfloat16)


def per_device(homolog, pair, w_first, w_second, w_outer, w_tri, w_gate, w_out):
    pair = pair.reshape(8, 2, 16, 128)
    left, right, half = factors(homolog, w_first.T, w_second.T, pair)
    swap = [(0, 1), (1, 0)]
    panel = lax.ppermute(right, ALL, panel_permutation())
    met = lax.ppermute(left, ("yh", "yl"), [(0, 3), (1, 2), (2, 1), (3, 0)])
    met_pair = lax.ppermute(half, "yh", swap)
    weights = prepared(w_outer, w_tri.T)
    panel, met_pair = lax.optimization_barrier((panel, met_pair))
    sibling = lax.ppermute(panel, "core", swap)
    update = block_update(left, met, panel, weights[0])
    edges, kept, sent = pair_stage(left, met, met_pair, sibling, update, pair, *weights)
    swapped = lax.all_to_all(edges.reshape(64, 8, 128), LAYER, 0, 0, tiled=True)
    returned = lax.ppermute(sent, "yh", swap)
    rights = lax.ppermute(swapped[:, 4:], "core", swap)
    back = triangle(*own_edges(swapped.reshape(512, 128)), rights.reshape(256, 128))
    mixed = lax.all_to_all(back.reshape(128, 4, 128), CHIPS, 0, 0, tiled=True)
    gates = gates_of(kept, returned, w_gate)
    return output_stage(mixed.reshape(512, 128), kept, returned, gates, w_out).reshape(8, 32, 128)


def solution(mesh):
    fine = Mesh(mesh.devices.reshape(8, 2, 2, 4, 2), ALL)
    placed = (P(None, ROW, None), P(ROW, COL, None), P(), P(), P(), P(), P(), P())
    return jax.shard_map(
        per_device, mesh=fine, in_specs=placed, out_specs=P(ROW, COL, None), check_vma=False
    )
```

```python
import jax
import jax.numpy as jnp
from jax import lax
from jax.experimental import pallas as pl
from jax.experimental.pallas import tpu as pltpu
from jax.sharding import Mesh, PartitionSpec as P

epsilon = 1e-05

ALL = ("z", "yh", "core", "x", "yl")
ROW = ("z", "yh", "core")
COL = ("x", "yl")
LAYER = ("z", "x", "yl")
CHIPS = ("z", "yh", "x", "yl")
VMEM_LIMIT = 32 * 1024 * 1024


PANEL_COLUMNS = (
    (
        (47531062, 7463125, 12675430, 67140253, 74126350, 60453721, 3265714, 23074165),
        (13652047, 14520376, 43051627, 42673015, 30546172, 25017436, 47162053, 14732506),
    ),
    (
        (74520136, 54763120, 71653042, 76402153, 74210356, 20456137, 3574216, 12067543),
        (61732045, 13256074, 36025714, 7241635, 34765012, 21350467, 24137605, 73150246),
    ),
)


def panel_permutation():
    pairs = []
    for z in range(8):
        for yh in range(2):
            for core in range(2):
                for c in range(8):
                    column = PANEL_COLUMNS[yh][core][c] // 10 ** (7 - z) % 10
                    source = ((c * 2 + yh) * 2 + core) * 8 + column
                    pairs.append((source, ((z * 2 + yh) * 2 + core) * 8 + c))
    return pairs


def mm(a, b):
    return jnp.dot(a, b, preferred_element_type=jnp.float32)


def mm_t(a, b):
    return lax.dot_general(a, b, (((1,), (1,)), ((), ())), preferred_element_type=jnp.float32)


def split(x):
    high = x.astype(jnp.bfloat16)
    return high, (x - high.astype(jnp.float32)).astype(jnp.bfloat16)


def halves(x):
    return jnp.concatenate(split(x), 1)


def dot_deep(a, b):
    a_high, a_low = split(a)
    both = mm(a_high, b)
    return both[:, :128] + both[:, 128:] + mm(a_low, b[:, :128])


def dot_t(a, b):
    b_high, b_low = split(b)
    return mm_t(a, jnp.concatenate([b_high, b_high], 1)) + mm_t(a[:, :128], b_low)


def layer_norm(values, axis):
    average = jnp.mean(values, axis, keepdims=True)
    centred = values - average
    variance = jnp.mean(centred * centred, axis, keepdims=True)
    return centred * lax.rsqrt(variance + epsilon)


def sigmoid(x):
    return 1.0 / (1.0 + jnp.exp(-x))


def turned_rows(p):
    return (8 - p) % 8


def factor_kernel(
    msa_ref, first_ref, second_ref, pair_ref, left_ref, right_ref, half_ref, result
):
    other = 1 - lax.axis_index("yh")
    w_high, w_low = split(jnp.concatenate([first_ref[...], second_ref[...]], 0))
    w_both = jnp.concatenate([w_high, w_low], 0)
    w_rest = jnp.concatenate([w_high, jnp.zeros_like(w_high)], 0)
    for k in range(4):
        n_high, n_low = split(layer_norm(msa_ref[pl.ds(k * 32, 32)].reshape(256, 256), -1))
        result[pl.ds(k * 256, 256), :] = mm_t(n_high, w_both) + mm_t(n_low, w_rest)
    for i in range(8):
        turned = result[pl.ds(i, 128, stride=8), :].T
        both = turned[:64] + turned[64:]
        left_ref[pl.ds(i * 32, 32), :] = both[:32] * (1.0 / 128.0)
        right_ref[pl.ds(i, 32, stride=8), :] = both[32:]
    for p in range(8):
        half_ref[pl.ds(p * 16, 16), :] = pair_ref[turned_rows(p), other]


def weight_kernel(w_outer_ref, w_tri_ref, left_ref, outer_ref, tri_ref, kept_ref):
    kept_ref[...] = left_ref[...]
    for b in range(32):
        outer_ref[pl.ds(b * 32, 32), :] = halves(w_outer_ref[pl.ds(b, 32, stride=32), :])
    tri_ref[...] = halves(w_tri_ref[...])


def gate_kernel(kept_ref, met_ref, w_ref, out_ref):
    w = halves(w_ref[...])
    for at, ref in enumerate((kept_ref, met_ref)):
        out_ref[at] = sigmoid(dot_deep(layer_norm(ref[...], -1), w))


def project_block(left, panel, w_outer, outer_ref, flat_ref):
    outer_ref[...] = dot_t(halves(panel), left)
    lane = lax.broadcasted_iota(jnp.int32, (8, 128), 1)
    low_half = lane < 64
    even = (lane // 32) % 2 == 0
    for bh in range(8):
        for ih in range(4):
            v = [
                outer_ref[pl.ds((bh * 4 + b) * 8, 8), pl.ds(ih * 128, 128)] for b in range(4)
            ]
            for p in range(2):
                a, c = v[p], v[p + 2]
                v[p] = jnp.where(low_half, a, pltpu.roll(c, 64, 1))
                v[p + 2] = jnp.where(low_half, pltpu.roll(a, 64, 1), c)
            for p in (0, 2):
                a, c = v[p], v[p + 1]
                v[p] = jnp.where(even, a, pltpu.roll(c, 32, 1))
                v[p + 1] = jnp.where(even, pltpu.roll(a, 96, 1), c)
            for il in range(4):
                row = ih // 2 * 64 + turned_rows(ih % 2 * 4 + il) * 8
                flat_ref[pl.ds(row, 8), pl.ds(bh * 128, 128)] = v[il]
    return dot_deep(flat_ref[...], w_outer)


def block_kernel(own_ref, met_ref, panel_ref, w_outer_ref, update_ref, outer_ref, flat_ref):
    left = jnp.concatenate([own_ref[...], met_ref[...]], 0)
    update_ref[...] = project_block(left, panel_ref[...], w_outer_ref[...], outer_ref, flat_ref)


def pair_kernel(
    own_ref, met_ref, met_pair_ref, sibling_ref, update_ref, pair_ref, w_outer_ref, w_tri_ref,
    edges_ref, kept_ref, sent_ref, outer_ref, flat_ref,
):
    yh = lax.axis_index("yh")
    first = lax.axis_index("core") == 0
    left = jnp.concatenate([own_ref[...], met_ref[...]], 0)
    other = project_block(left, sibling_ref[...], w_outer_ref[...], outer_ref, flat_ref)
    mine = update_ref[...]
    blocks = jnp.where(first, mine, other), jnp.where(first, other, mine)
    update = [block[t * 8 : t * 8 + 8] for t in range(16) for block in blocks]
    pair = jnp.concatenate(
        [pair_ref[turned_rows(p), yh] for p in range(8)] + [met_pair_ref[...]], 0
    )
    mid = pair + jnp.concatenate(update, 0)
    normed = layer_norm(mid, -1)
    projected = dot_t(w_tri_ref[...], normed)
    for side in range(2):
        plain, gating = projected[side * 256 :][:128], projected[side * 256 + 128 :][:128]
        edge = sigmoid(gating) * plain
        for h in range(2):
            q = side * 2 + h
            own, met = edge[h * 64 : h * 64 + 64, :128], edge[h * 64 : h * 64 + 64, 128:]
            edges_ref[pl.ds(q * 2, 64, stride=8), :] = jnp.where(yh == 0, own, met)
            edges_ref[pl.ds(q * 2 + 1, 64, stride=8), :] = jnp.where(yh == 0, met, own)
    kept_ref[...] = mid[:128]
    sent_ref[...] = mid[128:]


def turn_blocks(x, masks):
    x = pltpu.roll(x, 0, 1, stride=16, stride_axis=0)
    for bit, mask in zip((1, 2, 4), masks):
        x = jnp.where(mask, pltpu.roll(x, 8 - bit, 0), x)
    return pltpu.roll(x, 0, 1, stride=16, stride_axis=0)


def block_masks():
    lane = lax.broadcasted_iota(jnp.int32, (8, 128), 1)
    return [(lane // 16) & bit != 0 for bit in (1, 2, 4)]


def own_kernel(edges_ref, l_ref, r_ref):
    masks = block_masks()
    for h in range(2):
        for z in range(8):
            for y in range(2):
                x = edges_ref[pl.ds(z * 64 + h * 2 + y, 8, stride=8), :]
                l_ref[h, pl.ds(y * 64 + z * 8, 8), :] = turn_blocks(x, masks)
                x = edges_ref[pl.ds(z * 64 + (2 + h) * 2 + y, 8, stride=8), :]
                r_ref[h, pl.ds(y * 64 + turned_rows(z) * 8, 8), :] = turn_blocks(x, masks)


def triangle_kernel(l_ref, own_ref, right_ref, out_ref, r_ref):
    masks = block_masks()
    first = lax.axis_index("core") == 0
    for h in range(2):
        for z in range(8):
            for y in range(2):
                x = right_ref[pl.ds(z * 32 + h * 2 + y, 8, stride=4), :]
                other = turn_blocks(x, masks)
                at = y * 64 + turned_rows(z) * 8
                own = own_ref[h, pl.ds(at, 8), :]
                r_ref[pl.ds(at * 2, 8), :] = jnp.where(first, own, other)
                r_ref[pl.ds(at * 2 + 8, 8), :] = jnp.where(first, other, own)
        mixed = dot_t(halves(l_ref[h]), r_ref[...])
        for z in range(8):
            for y in range(2):
                for half in range(2):
                    block = mixed[y * 64 + z * 8 :, half * 128 :][:8, :128]
                    out_ref[pl.ds((z * 2 + y) * 32 + h * 2 + half, 8, stride=4), :] = turn_blocks(
                        block, masks
                    )


def output_kernel(mixed_ref, kept_ref, met_ref, gates_ref, w_ref, out_ref):
    yh = lax.axis_index("yh")
    w = halves(w_ref[...])
    for half in range(2):
        tiles = []
        for h in range(2):
            for z in range(8):
                parts = [
                    mixed_ref[pl.ds((z * 2 + y) * 32 + h * 2 + half, 8, stride=4), :]
                    for y in range(2)
                ]
                tiles.append(parts[0] + parts[1])
        update = dot_deep(layer_norm(jnp.concatenate(tiles, 0), 0).T, w)
        mid = jnp.where(yh == half, kept_ref[...], met_ref[...])
        gate = jnp.where(yh == half, gates_ref[0], gates_ref[1])
        for i in range(8):
            p = turned_rows(i) * 16
            out_ref[i, half] = mid[p : p + 16] + gate[p : p + 16] * update[i * 16 : i * 16 + 16]


def call(kernel, out_shapes, scratch, *args, limit=VMEM_LIMIT, short=0):
    kinds = [jnp.bfloat16] * short + [jnp.float32] * (len(out_shapes) - short)
    shapes = [jax.ShapeDtypeStruct(s, kind) for s, kind in zip(out_shapes, kinds)]
    return pl.pallas_call(
        kernel,
        out_shape=shapes if len(shapes) > 1 else shapes[0],
        scratch_shapes=scratch,
        compiler_params=pltpu.CompilerParams(vmem_limit_bytes=limit),
    )(*args)


def vmem(*shape):
    return pltpu.VMEM(shape, jnp.float32)


def factors(homolog, first, second, pair):
    return call(
        factor_kernel, [(256, 128), (256, 128), (128, 128)], [vmem(1024, 128)],
        homolog, first, second, pair,
        limit=60 * 1024 * 1024,
    )


def block_update(*args):
    return call(block_kernel, [(128, 128)], [vmem(256, 512), vmem(128, 1024)], *args)


def pair_stage(*args):
    return call(
        pair_kernel,
        [(512, 128), (128, 128), (128, 128)],
        [vmem(256, 512), vmem(128, 1024)],
        *args,
    )


def own_edges(edges):
    return call(own_kernel, [(2, 128, 128), (2, 128, 128)], [], edges)


def triangle(*args):
    return call(triangle_kernel, [(512, 128)], [vmem(256, 128)], *args)


def output_stage(mixed, kept, met, gates, w_out):
    return call(output_kernel, [(8, 2, 16, 128)], [], mixed, kept, met, gates, w_out)


def gates_of(kept, met, w_gate):
    return call(gate_kernel, [(2, 128, 128)], [], kept, met, w_gate)


def prepared(*args):
    return call(weight_kernel, [(1024, 256), (512, 256), (256, 128)], [], *args, short=2)


def per_device(homolog, pair, w_first, w_second, w_outer, w_tri, w_gate, w_out):
    pair = pair.reshape(8, 2, 16, 128)
    left, right, half = factors(homolog, w_first.T, w_second.T, pair)
    swap = [(0, 1), (1, 0)]
    panel = lax.ppermute(right, ALL, panel_permutation())
    met = lax.ppermute(left, ("yh", "yl"), [(0, 3), (1, 2), (2, 1), (3, 0)])
    met_pair = lax.ppermute(half, "yh", swap)
    ready = prepared(w_outer, w_tri.T, left)
    panel, met_pair, (*weights, left) = lax.optimization_barrier((panel, met_pair, ready))
    sibling = lax.ppermute(panel, "core", swap)
    update = block_update(left, met, panel, weights[0])
    edges, kept, sent = pair_stage(left, met, met_pair, sibling, update, pair, *weights)
    swapped = lax.all_to_all(edges.reshape(64, 8, 128), LAYER, 0, 0, tiled=True)
    returned = lax.ppermute(sent, "yh", swap)
    rights = lax.ppermute(swapped[:, 4:], "core", swap)
    back = triangle(*own_edges(swapped.reshape(512, 128)), rights.reshape(256, 128))
    mixed = lax.all_to_all(back.reshape(128, 4, 128), CHIPS, 0, 0, tiled=True)
    gates = gates_of(kept, returned, w_gate)
    return output_stage(mixed.reshape(512, 128), kept, returned, gates, w_out).reshape(8, 32, 128)


def solution(mesh):
    fine = Mesh(mesh.devices.reshape(8, 2, 2, 4, 2), ALL)
    placed = (P(None, ROW, None), P(ROW, COL, None), P(), P(), P(), P(), P(), P())
    return jax.shard_map(
        per_device, mesh=fine, in_specs=placed, out_specs=P(ROW, COL, None), check_vma=False
    )
```

```python
import jax
import jax.numpy as jnp
from jax import lax
from jax.experimental import pallas as pl
from jax.experimental.pallas import tpu as pltpu
from jax.sharding import Mesh, PartitionSpec as P

epsilon = 1e-05

ALL = ("z", "yh", "core", "x", "yl")
ROW = ("z", "yh", "core")
COL = ("x", "yl")
LAYER = ("z", "x", "yl")
CHIPS = ("z", "yh", "x", "yl")
VMEM_LIMIT = 32 * 1024 * 1024


PANEL_COLUMNS = (
    (
        (47531062, 7463125, 12675430, 67140253, 74126350, 60453721, 3265714, 23074165),
        (13652047, 14520376, 43051627, 42673015, 30546172, 25017436, 47162053, 14732506),
    ),
    (
        (74520136, 54763120, 71653042, 76402153, 74210356, 20456137, 3574216, 12067543),
        (61732045, 13256074, 36025714, 7241635, 34765012, 21350467, 24137605, 73150246),
    ),
)


def panel_permutation():
    pairs = []
    for z in range(8):
        for yh in range(2):
            for core in range(2):
                for c in range(8):
                    column = PANEL_COLUMNS[yh][core][c] // 10 ** (7 - z) % 10
                    source = ((c * 2 + yh) * 2 + core) * 8 + column
                    pairs.append((source, ((z * 2 + yh) * 2 + core) * 8 + c))
    return pairs


def mm(a, b):
    return jnp.dot(a, b, preferred_element_type=jnp.float32)


def mm_t(a, b):
    return lax.dot_general(a, b, (((1,), (1,)), ((), ())), preferred_element_type=jnp.float32)


def split(x):
    high = x.astype(jnp.bfloat16)
    return high, (x - high.astype(jnp.float32)).astype(jnp.bfloat16)


def halves(x):
    return jnp.concatenate(split(x), 1)


def dot_deep(a, b):
    a_high, a_low = split(a)
    both = mm(a_high, b)
    return both[:, :128] + both[:, 128:] + mm(a_low, b[:, :128])


def dot_t(a, b):
    b_high, b_low = split(b)
    return mm_t(a, jnp.concatenate([b_high, b_high], 1)) + mm_t(a[:, :128], b_low)


def layer_norm(values, axis):
    average = jnp.mean(values, axis, keepdims=True)
    centred = values - average
    variance = jnp.mean(centred * centred, axis, keepdims=True)
    return centred * lax.rsqrt(variance + epsilon)


def sigmoid(x):
    return 1.0 / (1.0 + jnp.exp(-x))


def turned_rows(p):
    return (8 - p) % 8


def factor_kernel(
    msa_ref, first_ref, second_ref, pair_ref, left_ref, right_ref, half_ref, result
):
    other = 1 - lax.axis_index("yh")
    w_high, w_low = split(jnp.concatenate([first_ref[...], second_ref[...]], 0))
    w_both = jnp.concatenate([w_high, w_low], 0)
    w_rest = jnp.concatenate([w_high, jnp.zeros_like(w_high)], 0)
    for k in range(4):
        n_high, n_low = split(layer_norm(msa_ref[pl.ds(k * 32, 32)].reshape(256, 256), -1))
        result[pl.ds(k * 256, 256), :] = mm_t(n_high, w_both) + mm_t(n_low, w_rest)
    for i in range(8):
        turned = result[pl.ds(i, 128, stride=8), :].T
        both = turned[:64] + turned[64:]
        left_ref[pl.ds(i * 32, 32), :] = both[:32] * (1.0 / 128.0)
        right_ref[pl.ds(i, 32, stride=8), :] = both[32:]
    for p in range(8):
        half_ref[pl.ds(p * 16, 16), :] = pair_ref[turned_rows(p), other]


def weight_kernel(w_outer_ref, w_tri_ref, left_ref, outer_ref, tri_ref, kept_ref):
    kept_ref[...] = left_ref[...]
    for b in range(32):
        outer_ref[pl.ds(b * 32, 32), :] = halves(w_outer_ref[pl.ds(b, 32, stride=32), :])
    tri_ref[...] = halves(w_tri_ref[...])


def gate_kernel(kept_ref, met_ref, w_ref, out_ref):
    w = halves(w_ref[...])
    for at, ref in enumerate((kept_ref, met_ref)):
        out_ref[at] = sigmoid(dot_deep(layer_norm(ref[...], -1), w))


def project_block(left, panel, w_outer, outer_ref, flat_ref):
    outer_ref[...] = dot_t(halves(panel), left)
    lane = lax.broadcasted_iota(jnp.int32, (8, 128), 1)
    low_half = lane < 64
    even = (lane // 32) % 2 == 0
    for bh in range(8):
        for ih in range(4):
            v = [
                outer_ref[pl.ds((bh * 4 + b) * 8, 8), pl.ds(ih * 128, 128)] for b in range(4)
            ]
            for p in range(2):
                a, c = v[p], v[p + 2]
                v[p] = jnp.where(low_half, a, pltpu.roll(c, 64, 1))
                v[p + 2] = jnp.where(low_half, pltpu.roll(a, 64, 1), c)
            for p in (0, 2):
                a, c = v[p], v[p + 1]
                v[p] = jnp.where(even, a, pltpu.roll(c, 32, 1))
                v[p + 1] = jnp.where(even, pltpu.roll(a, 96, 1), c)
            for il in range(4):
                row = ih // 2 * 64 + turned_rows(ih % 2 * 4 + il) * 8
                flat_ref[pl.ds(row, 8), pl.ds(bh * 128, 128)] = v[il]
    return dot_deep(flat_ref[...], w_outer)


def block_kernel(own_ref, met_ref, panel_ref, w_outer_ref, update_ref, outer_ref, flat_ref):
    left = jnp.concatenate([own_ref[...], met_ref[...]], 0)
    update_ref[...] = project_block(left, panel_ref[...], w_outer_ref[...], outer_ref, flat_ref)


def pair_kernel(
    own_ref, met_ref, met_pair_ref, sibling_ref, update_ref, pair_ref, w_outer_ref, w_tri_ref,
    edges_ref, kept_ref, sent_ref, outer_ref, flat_ref,
):
    yh = lax.axis_index("yh")
    first = lax.axis_index("core") == 0
    left = jnp.concatenate([own_ref[...], met_ref[...]], 0)
    other = project_block(left, sibling_ref[...], w_outer_ref[...], outer_ref, flat_ref)
    mine = update_ref[...]
    blocks = jnp.where(first, mine, other), jnp.where(first, other, mine)
    update = [block[t * 8 : t * 8 + 8] for t in range(16) for block in blocks]
    pair = jnp.concatenate(
        [pair_ref[turned_rows(p), yh] for p in range(8)] + [met_pair_ref[...]], 0
    )
    mid = pair + jnp.concatenate(update, 0)
    normed = layer_norm(mid, -1)
    projected = dot_t(w_tri_ref[...], normed)
    for side in range(2):
        plain, gating = projected[side * 256 :][:128], projected[side * 256 + 128 :][:128]
        edge = sigmoid(gating) * plain
        for h in range(2):
            q = side * 2 + h
            own, met = edge[h * 64 : h * 64 + 64, :128], edge[h * 64 : h * 64 + 64, 128:]
            edges_ref[pl.ds(q * 2, 64, stride=8), :] = jnp.where(yh == 0, own, met)
            edges_ref[pl.ds(q * 2 + 1, 64, stride=8), :] = jnp.where(yh == 0, met, own)
    kept_ref[...] = mid[:128]
    sent_ref[...] = mid[128:]


def turn_blocks(x, masks):
    x = pltpu.roll(x, 0, 1, stride=16, stride_axis=0)
    for bit, mask in zip((1, 2, 4), masks):
        x = jnp.where(mask, pltpu.roll(x, 8 - bit, 0), x)
    return pltpu.roll(x, 0, 1, stride=16, stride_axis=0)


def block_masks():
    lane = lax.broadcasted_iota(jnp.int32, (8, 128), 1)
    return [(lane // 16) & bit != 0 for bit in (1, 2, 4)]


def own_kernel(edges_ref, l_ref, r_ref):
    masks = block_masks()
    for h in range(2):
        for z in range(8):
            for y in range(2):
                x = edges_ref[pl.ds(z * 64 + h * 2 + y, 8, stride=8), :]
                l_ref[h, pl.ds(y * 64 + z * 8, 8), :] = turn_blocks(x, masks)
                x = edges_ref[pl.ds(z * 64 + (2 + h) * 2 + y, 8, stride=8), :]
                r_ref[h, pl.ds(y * 64 + turned_rows(z) * 8, 8), :] = turn_blocks(x, masks)


def triangle_kernel(l_ref, own_ref, right_ref, out_ref, r_ref):
    masks = block_masks()
    first = lax.axis_index("core") == 0
    for h in range(2):
        for z in range(8):
            for y in range(2):
                x = right_ref[pl.ds(z * 32 + h * 2 + y, 8, stride=4), :]
                other = turn_blocks(x, masks)
                at = y * 64 + turned_rows(z) * 8
                own = own_ref[h, pl.ds(at, 8), :]
                r_ref[pl.ds(at * 2, 8), :] = jnp.where(first, own, other)
                r_ref[pl.ds(at * 2 + 8, 8), :] = jnp.where(first, other, own)
        mixed = dot_t(halves(l_ref[h]), r_ref[...])
        for z in range(8):
            for y in range(2):
                for half in range(2):
                    block = mixed[y * 64 + z * 8 :, half * 128 :][:8, :128]
                    out_ref[pl.ds((z * 2 + y) * 32 + h * 2 + half, 8, stride=4), :] = turn_blocks(
                        block, masks
                    )


def output_kernel(mixed_ref, kept_ref, met_ref, gates_ref, w_ref, out_ref, held, sems):
    yh = lax.axis_index("yh")
    w = halves(w_ref[...])
    copies = []
    for half in range(2):
        tiles = []
        for h in range(2):
            for z in range(8):
                parts = [
                    mixed_ref[pl.ds((z * 2 + y) * 32 + h * 2 + half, 8, stride=4), :]
                    for y in range(2)
                ]
                tiles.append(parts[0] + parts[1])
        update = dot_deep(layer_norm(jnp.concatenate(tiles, 0), 0).T, w)
        mid = jnp.where(yh == half, kept_ref[...], met_ref[...])
        gate = jnp.where(yh == half, gates_ref[0], gates_ref[1])
        for i in range(8):
            p = turned_rows(i) * 16
            held[half, i] = mid[p : p + 16] + gate[p : p + 16] * update[i * 16 : i * 16 + 16]
        copies.append(pltpu.make_async_copy(held.at[half], out_ref.at[:, half], sems.at[half]))
        copies[half].start()
    for copy in copies:
        copy.wait()


def call(kernel, out_shapes, scratch, *args, limit=VMEM_LIMIT, short=0, **more):
    kinds = [jnp.bfloat16] * short + [jnp.float32] * (len(out_shapes) - short)
    shapes = [jax.ShapeDtypeStruct(s, kind) for s, kind in zip(out_shapes, kinds)]
    return pl.pallas_call(
        kernel,
        out_shape=shapes if len(shapes) > 1 else shapes[0],
        scratch_shapes=scratch,
        compiler_params=pltpu.CompilerParams(vmem_limit_bytes=limit),
        **more,
    )(*args)


def vmem(*shape):
    return pltpu.VMEM(shape, jnp.float32)


def factors(homolog, first, second, pair):
    return call(
        factor_kernel, [(256, 128), (256, 128), (128, 128)], [vmem(1024, 128)],
        homolog, first, second, pair,
        limit=60 * 1024 * 1024,
    )


def block_update(*args):
    return call(block_kernel, [(128, 128)], [vmem(256, 512), vmem(128, 1024)], *args)


def pair_stage(*args):
    return call(
        pair_kernel,
        [(512, 128), (128, 128), (128, 128)],
        [vmem(256, 512), vmem(128, 1024)],
        *args,
    )


def own_edges(edges):
    return call(own_kernel, [(2, 128, 128), (2, 128, 128)], [], edges)


def triangle(*args):
    return call(triangle_kernel, [(512, 128)], [vmem(256, 128)], *args)


def output_stage(*args):
    return call(
        output_kernel,
        [(8, 2, 16, 128)],
        [vmem(2, 8, 16, 128), pltpu.SemaphoreType.DMA((2,))],
        *args,
        out_specs=pl.BlockSpec(memory_space=pl.ANY),
    )


def gates_of(kept, met, w_gate):
    return call(gate_kernel, [(2, 128, 128)], [], kept, met, w_gate)


def prepared(*args):
    return call(weight_kernel, [(1024, 256), (512, 256), (256, 128)], [], *args, short=2)


def per_device(homolog, pair, w_first, w_second, w_outer, w_tri, w_gate, w_out):
    pair = pair.reshape(8, 2, 16, 128)
    left, right, half = factors(homolog, w_first.T, w_second.T, pair)
    swap = [(0, 1), (1, 0)]
    panel = lax.ppermute(right, ALL, panel_permutation())
    met = lax.ppermute(left, ("yh", "yl"), [(0, 3), (1, 2), (2, 1), (3, 0)])
    met_pair = lax.ppermute(half, "yh", swap)
    ready = prepared(w_outer, w_tri.T, left)
    panel, met_pair, (*weights, left) = lax.optimization_barrier((panel, met_pair, ready))
    sibling = lax.ppermute(panel, "core", swap)
    update = block_update(left, met, panel, weights[0])
    edges, kept, sent = pair_stage(left, met, met_pair, sibling, update, pair, *weights)
    swapped = lax.all_to_all(edges.reshape(64, 8, 128), LAYER, 0, 0, tiled=True)
    returned = lax.ppermute(sent, "yh", swap)
    rights = lax.ppermute(swapped[:, 4:], "core", swap)
    back = triangle(*own_edges(swapped.reshape(512, 128)), rights.reshape(256, 128))
    mixed = lax.all_to_all(back.reshape(128, 4, 128), CHIPS, 0, 0, tiled=True)
    gates = gates_of(kept, returned, w_gate)
    return output_stage(mixed.reshape(512, 128), kept, returned, gates, w_out).reshape(8, 32, 128)


def solution(mesh):
    fine = Mesh(mesh.devices.reshape(8, 2, 2, 4, 2), ALL)
    placed = (P(None, ROW, None), P(ROW, COL, None), P(), P(), P(), P(), P(), P())
    return jax.shard_map(
        per_device, mesh=fine, in_specs=placed, out_specs=P(ROW, COL, None), check_vma=False
    )
```

```python
import jax
import jax.numpy as jnp
from jax import lax
from jax.experimental import pallas as pl
from jax.experimental.pallas import tpu as pltpu
from jax.sharding import Mesh, PartitionSpec as P

epsilon = 1e-05

ALL = ("z", "yh", "core", "x", "yl")
ROW = ("z", "yh", "core")
COL = ("x", "yl")
LAYER = ("z", "x", "yl")
CHIPS = ("z", "yh", "x", "yl")
VMEM_LIMIT = 32 * 1024 * 1024


PANEL_COLUMNS = (
    (
        (47531062, 7463125, 12675430, 67140253, 74126350, 60453721, 3265714, 23074165),
        (13652047, 14520376, 43051627, 42673015, 30546172, 25017436, 47162053, 14732506),
    ),
    (
        (74520136, 54763120, 71653042, 76402153, 74210356, 20456137, 3574216, 12067543),
        (61732045, 13256074, 36025714, 7241635, 34765012, 21350467, 24137605, 73150246),
    ),
)


def panel_permutation():
    pairs = []
    for z in range(8):
        for yh in range(2):
            for core in range(2):
                for c in range(8):
                    column = PANEL_COLUMNS[yh][core][c] // 10 ** (7 - z) % 10
                    source = ((c * 2 + yh) * 2 + core) * 8 + column
                    pairs.append((source, ((z * 2 + yh) * 2 + core) * 8 + c))
    return pairs


def mm(a, b):
    return jnp.dot(a, b, preferred_element_type=jnp.float32)


def mm_t(a, b):
    return lax.dot_general(a, b, (((1,), (1,)), ((), ())), preferred_element_type=jnp.float32)


def split(x):
    high = x.astype(jnp.bfloat16)
    return high, (x - high.astype(jnp.float32)).astype(jnp.bfloat16)


def halves(x):
    return jnp.concatenate(split(x), 1)


def dot_deep(a, b):
    a_high, a_low = split(a)
    both = mm(a_high, b)
    return both[:, :128] + both[:, 128:] + mm(a_low, b[:, :128])


def dot_t(a, b):
    b_high, b_low = split(b)
    return mm_t(a, jnp.concatenate([b_high, b_high], 1)) + mm_t(a[:, :128], b_low)


def layer_norm(values, axis):
    average = jnp.mean(values, axis, keepdims=True)
    centred = values - average
    variance = jnp.mean(centred * centred, axis, keepdims=True)
    return centred * lax.rsqrt(variance + epsilon)


def sigmoid(x):
    return 1.0 / (1.0 + jnp.exp(-x))


def turned_rows(p):
    return (8 - p) % 8


def factor_kernel(
    msa_ref, first_ref, second_ref, pair_ref, left_ref, right_ref, half_ref, result
):
    other = 1 - lax.axis_index("yh")
    w_high, w_low = split(jnp.concatenate([first_ref[...], second_ref[...]], 0))
    w_both = jnp.concatenate([w_high, w_low], 0)
    w_rest = jnp.concatenate([w_high, jnp.zeros_like(w_high)], 0)
    for k in range(4):
        n_high, n_low = split(layer_norm(msa_ref[pl.ds(k * 32, 32)].reshape(256, 256), -1))
        result[pl.ds(k * 256, 256), :] = mm_t(n_high, w_both) + mm_t(n_low, w_rest)
    for i in range(8):
        turned = result[pl.ds(i, 128, stride=8), :].T
        both = turned[:64] + turned[64:]
        left_ref[pl.ds(i * 32, 32), :] = both[:32] * (1.0 / 128.0)
        right_ref[pl.ds(i, 32, stride=8), :] = both[32:]
    for p in range(8):
        half_ref[pl.ds(p * 16, 16), :] = pair_ref[turned_rows(p), other]


def weight_kernel(
    w_outer_ref, w_tri_ref, left_ref, pair_ref, outer_ref, tri_ref, kept_ref, kept_pair_ref
):
    kept_ref[...] = left_ref[...]
    kept_pair_ref[...] = pair_ref[...]
    for b in range(32):
        outer_ref[pl.ds(b * 32, 32), :] = halves(w_outer_ref[pl.ds(b, 32, stride=32), :])
    tri_ref[...] = halves(w_tri_ref[...])


def gate_kernel(kept_ref, met_ref, w_ref, out_ref):
    w = halves(w_ref[...])
    for at, ref in enumerate((kept_ref, met_ref)):
        out_ref[at] = sigmoid(dot_deep(layer_norm(ref[...], -1), w))


def project_block(left, panel, w_outer, outer_ref, flat_ref):
    outer_ref[...] = dot_t(halves(panel), left)
    lane = lax.broadcasted_iota(jnp.int32, (8, 128), 1)
    low_half = lane < 64
    even = (lane // 32) % 2 == 0
    for bh in range(8):
        for ih in range(4):
            v = [
                outer_ref[pl.ds((bh * 4 + b) * 8, 8), pl.ds(ih * 128, 128)] for b in range(4)
            ]
            for p in range(2):
                a, c = v[p], v[p + 2]
                v[p] = jnp.where(low_half, a, pltpu.roll(c, 64, 1))
                v[p + 2] = jnp.where(low_half, pltpu.roll(a, 64, 1), c)
            for p in (0, 2):
                a, c = v[p], v[p + 1]
                v[p] = jnp.where(even, a, pltpu.roll(c, 32, 1))
                v[p + 1] = jnp.where(even, pltpu.roll(a, 96, 1), c)
            for il in range(4):
                row = ih // 2 * 64 + turned_rows(ih % 2 * 4 + il) * 8
                flat_ref[pl.ds(row, 8), pl.ds(bh * 128, 128)] = v[il]
    return dot_deep(flat_ref[...], w_outer)


def block_kernel(own_ref, met_ref, panel_ref, w_outer_ref, update_ref, outer_ref, flat_ref):
    left = jnp.concatenate([own_ref[...], met_ref[...]], 0)
    update_ref[...] = project_block(left, panel_ref[...], w_outer_ref[...], outer_ref, flat_ref)


def pair_kernel(
    own_ref, met_ref, met_pair_ref, sibling_ref, update_ref, pair_ref, w_outer_ref, w_tri_ref,
    edges_ref, kept_ref, sent_ref, outer_ref, flat_ref,
):
    yh = lax.axis_index("yh")
    first = lax.axis_index("core") == 0
    left = jnp.concatenate([own_ref[...], met_ref[...]], 0)
    other = project_block(left, sibling_ref[...], w_outer_ref[...], outer_ref, flat_ref)
    mine = update_ref[...]
    blocks = jnp.where(first, mine, other), jnp.where(first, other, mine)
    update = [block[t * 8 : t * 8 + 8] for t in range(16) for block in blocks]
    pair = jnp.concatenate(
        [pair_ref[turned_rows(p), yh] for p in range(8)] + [met_pair_ref[...]], 0
    )
    mid = pair + jnp.concatenate(update, 0)
    normed = layer_norm(mid, -1)
    projected = dot_t(w_tri_ref[...], normed)
    for side in range(2):
        plain, gating = projected[side * 256 :][:128], projected[side * 256 + 128 :][:128]
        edge = sigmoid(gating) * plain
        for h in range(2):
            q = side * 2 + h
            own, met = edge[h * 64 : h * 64 + 64, :128], edge[h * 64 : h * 64 + 64, 128:]
            edges_ref[pl.ds(q * 2, 64, stride=8), :] = jnp.where(yh == 0, own, met)
            edges_ref[pl.ds(q * 2 + 1, 64, stride=8), :] = jnp.where(yh == 0, met, own)
    kept_ref[...] = mid[:128]
    sent_ref[...] = mid[128:]


def turn_blocks(x, masks):
    x = pltpu.roll(x, 0, 1, stride=16, stride_axis=0)
    for bit, mask in zip((1, 2, 4), masks):
        x = jnp.where(mask, pltpu.roll(x, 8 - bit, 0), x)
    return pltpu.roll(x, 0, 1, stride=16, stride_axis=0)


def block_masks():
    lane = lax.broadcasted_iota(jnp.int32, (8, 128), 1)
    return [(lane // 16) & bit != 0 for bit in (1, 2, 4)]


def own_kernel(edges_ref, l_ref, r_ref):
    masks = block_masks()
    for h in range(2):
        for z in range(8):
            for y in range(2):
                x = edges_ref[pl.ds(z * 64 + h * 2 + y, 8, stride=8), :]
                l_ref[h, pl.ds(y * 64 + z * 8, 8), :] = turn_blocks(x, masks)
                x = edges_ref[pl.ds(z * 64 + (2 + h) * 2 + y, 8, stride=8), :]
                r_ref[h, pl.ds(y * 64 + turned_rows(z) * 8, 8), :] = turn_blocks(x, masks)


def triangle_kernel(l_ref, own_ref, right_ref, out_ref, r_ref):
    masks = block_masks()
    first = lax.axis_index("core") == 0
    for h in range(2):
        for z in range(8):
            for y in range(2):
                x = right_ref[pl.ds(z * 32 + h * 2 + y, 8, stride=4), :]
                other = turn_blocks(x, masks)
                at = y * 64 + turned_rows(z) * 8
                own = own_ref[h, pl.ds(at, 8), :]
                r_ref[pl.ds(at * 2, 8), :] = jnp.where(first, own, other)
                r_ref[pl.ds(at * 2 + 8, 8), :] = jnp.where(first, other, own)
        mixed = dot_t(halves(l_ref[h]), r_ref[...])
        for z in range(8):
            for y in range(2):
                for half in range(2):
                    block = mixed[y * 64 + z * 8 :, half * 128 :][:8, :128]
                    out_ref[pl.ds((z * 2 + y) * 32 + h * 2 + half, 8, stride=4), :] = turn_blocks(
                        block, masks
                    )


def output_kernel(mixed_ref, kept_ref, met_ref, gates_ref, w_ref, out_ref):
    yh = lax.axis_index("yh")
    w = halves(w_ref[...])
    for half in range(2):
        tiles = []
        for h in range(2):
            for z in range(8):
                parts = [
                    mixed_ref[pl.ds((z * 2 + y) * 32 + h * 2 + half, 8, stride=4), :]
                    for y in range(2)
                ]
                tiles.append(parts[0] + parts[1])
        update = dot_deep(layer_norm(jnp.concatenate(tiles, 0), 0).T, w)
        mid = jnp.where(yh == half, kept_ref[...], met_ref[...])
        gate = jnp.where(yh == half, gates_ref[0], gates_ref[1])
        for i in range(8):
            p = turned_rows(i) * 16
            out_ref[i, half] = mid[p : p + 16] + gate[p : p + 16] * update[i * 16 : i * 16 + 16]


def call(kernel, out_shapes, scratch, *args, limit=VMEM_LIMIT, short=0):
    kinds = [jnp.bfloat16] * short + [jnp.float32] * (len(out_shapes) - short)
    shapes = [jax.ShapeDtypeStruct(s, kind) for s, kind in zip(out_shapes, kinds)]
    return pl.pallas_call(
        kernel,
        out_shape=shapes if len(shapes) > 1 else shapes[0],
        scratch_shapes=scratch,
        compiler_params=pltpu.CompilerParams(vmem_limit_bytes=limit),
    )(*args)


def vmem(*shape):
    return pltpu.VMEM(shape, jnp.float32)


def factors(homolog, first, second, pair):
    return call(
        factor_kernel, [(256, 128), (256, 128), (128, 128)], [vmem(1024, 128)],
        homolog, first, second, pair,
        limit=60 * 1024 * 1024,
    )


def block_update(*args):
    return call(block_kernel, [(128, 128)], [vmem(256, 512), vmem(128, 1024)], *args)


def pair_stage(*args):
    return call(
        pair_kernel,
        [(512, 128), (128, 128), (128, 128)],
        [vmem(256, 512), vmem(128, 1024)],
        *args,
    )


def own_edges(edges):
    return call(own_kernel, [(2, 128, 128), (2, 128, 128)], [], edges)


def triangle(*args):
    return call(triangle_kernel, [(512, 128)], [vmem(256, 128)], *args)


def output_stage(mixed, kept, met, gates, w_out):
    return call(output_kernel, [(8, 2, 16, 128)], [], mixed, kept, met, gates, w_out)


def gates_of(kept, met, w_gate):
    return call(gate_kernel, [(2, 128, 128)], [], kept, met, w_gate)


def prepared(*args):
    shapes = [(1024, 256), (512, 256), (256, 128), (8, 2, 16, 128)]
    return call(weight_kernel, shapes, [], *args, short=2)


def per_device(homolog, pair, w_first, w_second, w_outer, w_tri, w_gate, w_out):
    pair = pair.reshape(8, 2, 16, 128)
    left, right, half = factors(homolog, w_first.T, w_second.T, pair)
    swap = [(0, 1), (1, 0)]
    panel = lax.ppermute(right, ALL, panel_permutation())
    met = lax.ppermute(left, ("yh", "yl"), [(0, 3), (1, 2), (2, 1), (3, 0)])
    met_pair = lax.ppermute(half, "yh", swap)
    ready = prepared(w_outer, w_tri.T, left, pair)
    panel, met_pair, ready = lax.optimization_barrier((panel, met_pair, ready))
    *weights, left, pair = ready
    sibling = lax.ppermute(panel, "core", swap)
    update = block_update(left, met, panel, weights[0])
    edges, kept, sent = pair_stage(left, met, met_pair, sibling, update, pair, *weights)
    swapped = lax.all_to_all(edges.reshape(64, 8, 128), LAYER, 0, 0, tiled=True)
    returned = lax.ppermute(sent, "yh", swap)
    rights = lax.ppermute(swapped[:, 4:], "core", swap)
    back = triangle(*own_edges(swapped.reshape(512, 128)), rights.reshape(256, 128))
    mixed = lax.all_to_all(back.reshape(128, 4, 128), CHIPS, 0, 0, tiled=True)
    gates = gates_of(kept, returned, w_gate)
    return output_stage(mixed.reshape(512, 128), kept, returned, gates, w_out).reshape(8, 32, 128)


def solution(mesh):
    fine = Mesh(mesh.devices.reshape(8, 2, 2, 4, 2), ALL)
    placed = (P(None, ROW, None), P(ROW, COL, None), P(), P(), P(), P(), P(), P())
    return jax.shard_map(
        per_device, mesh=fine, in_specs=placed, out_specs=P(ROW, COL, None), check_vma=False
    )
```
